32 devices in a mesh: groups: 2 (over y), frame: 4 (over z), strip: 2 (over x), slab: 2 (over core).
Axes of the slice: x: 2, y: 2, z: 4, core: 2. Of those that a mesh axis runs over, the one named last changes fastest.
Arguments:
- frames_in: bfloat16 [16, 8, 128, 192], P(('groups', 'frame'), 'strip', 'slab'), parts along dimension 0, may hold values from -6 to 6
- weight_first: bfloat16 [3, 3, 3, 192, 192], replicated, may hold values from -0.078125 to 0.078125
- scale_first: float32 [192], replicated, may hold values from 0.25 to 1.75
- weight_second: bfloat16 [3, 3, 3, 192, 192], replicated, may hold values from -0.078125 to 0.078125
- scale_second: float32 [192], replicated, may hold values from 0.25 to 1.75
Outputs:
- latents_out: bfloat16 [16, 8, 128, 192], P(('groups', 'frame'), 'strip', 'slab'), parts along dimension 0
The draws below stay inside these ranges and needn't reach their ends.
There are 2 independent parts, one for each index of `groups`. The reference program is written for one: setup_inputs(seed, part) draws one part's arguments, and reference() takes and returns one part's arrays. A program takes and returns all parts, laid end to end along the dimension named above; an argument that names none is the same for every part. Nothing has to cross between parts.
All inputs are finite; a program needn't handle non-finite values.
Results may differ from the reference program's by a relative error of at most 0.0051.
Values may be sent and summed in bfloat16 or wider, within the bound.
No kernel may reach another device: no remote copies, remote signals or barrier semaphores. Data moves between devices by JAX's collectives and lax.ppermute only.
A program may use at most 64 MiB of HBM per device.

```python
import jax
import jax.numpy as jnp
from jax import lax

C = 192
NF = 8
NH = 8
NW = 128


def block_scale(rng, shape, cuts, smallest, largest):
    level, own = 1.0, jax.random.fold_in(rng, 6)
    for position, shards_of in cuts:
        heights = jnp.exp(jax.random.uniform(jax.random.fold_in(own, position), (shards_of,), jnp.float32, smallest / len(cuts), largest / len(cuts)))
        level = level * jnp.repeat(heights, shape[position] // shards_of).reshape([-1 if axis == position else 1 for axis in range(len(shape))])
    return level


def noise(rng, dims, scale, most, cuts=(), held_as=jnp.bfloat16):
    drawn = jax.random.normal(rng, dims, jnp.float32) * scale
    if len(cuts) > 0:
        drawn = block_scale(rng, dims, cuts, -0.22, 0.18) * drawn
    return jnp.clip(drawn, min=-most, max=most).astype(held_as)


def setup_inputs(seed: int = 0, part: int = 0) -> dict:
    splits = jax.random.split(jax.random.key(seed), 6)
    part_keys = jax.random.split(jax.random.fold_in(splits[5], part), 6)
    frames_in = noise(part_keys[0], (NF, NH, NW, C), 1.0, 6.0, ((0, 4), (1, 2), (2, 2)))
    weight_first = noise(splits[1], (3, 3, 3, C, C), (27 * C) ** -0.5, 0.078125)
    scale_first = jnp.clip(1.0 + 0.15 * jax.random.normal(splits[2], (C,), jnp.float32), 0.25, 1.75)
    weight_second = noise(splits[3], (3, 3, 3, C, C), (27 * C) ** -0.5, 0.078125)
    scale_second = jnp.clip(1.0 + 0.15 * jax.random.normal(splits[4], (C,), jnp.float32), 0.25, 1.75)
    return {"frames_in": frames_in, "weight_first": weight_first, "scale_first": scale_first, "weight_second": weight_second, "scale_second": scale_second}


def tap_rows(block, rows, cols):
    pieces = [block[offset_y:offset_y + rows, offset_x:offset_x + cols] for offset_y in range(3) for offset_x in range(3)]
    return jnp.concatenate(pieces, axis=-1).reshape(rows * cols, -1)

def finish(convolved, scales):
    mean_square = lax.optimization_barrier(jnp.mean(convolved * convolved, axis=-1, keepdims=True))
    normed = convolved * lax.rsqrt(mean_square + 1e-06) * scales
    return jax.nn.silu(normed).astype(jnp.bfloat16)

def conv_layer(features, weight, scales):
    channels = features.shape[-1]
    padded = jnp.pad(features, ((2, 0), (1, 1), (1, 1), (0, 0)))
    flat_weight = weight.reshape(3, 9 * channels, channels)

    def single_frame(frame_index):
        window = lax.dynamic_slice_in_dim(padded, frame_index, 3, 0)
        accumulated = jnp.zeros((NH * NW, channels), jnp.float32)
        for offset_t in range(3):
            accumulated = accumulated + jnp.dot(tap_rows(window[offset_t], NH, NW), flat_weight[offset_t], preferred_element_type=jnp.float32)
        return accumulated
    convolved = lax.map(single_frame, jnp.arange(NF, dtype=jnp.int32))
    return finish(convolved, scales).reshape(features.shape)

def reference(frames_in, weight_first, scale_first, weight_second, scale_second):
    hidden = conv_layer(frames_in, weight_first, scale_first)
    return conv_layer(hidden, weight_second, scale_second)
```

```python
import functools

import jax
import jax.numpy as jnp
from jax import lax
from jax.experimental import pallas as pl
from jax.experimental.pallas import tpu as pltpu
from jax.sharding import PartitionSpec as P

LANES = 128
TILE = 16
EPS = 1e-06


def exchange(first, last, axis, offset=0):
    count = lax.axis_size(axis)
    steps = lax.axis_size("frame")

    def move(x, pairs):
        if offset == 0:
            return lax.ppermute(x, axis, pairs)
        both = [(f * count + i, (f + offset) * count + j) for f in range(steps - offset) for i, j in pairs]
        return lax.ppermute(x, ("frame", axis), both)

    if count == 2:
        facing = jnp.where(lax.axis_index(axis) == 0, last, first)
        return (move(facing, [(0, 1), (1, 0)]),)
    return (
        move(last, [(i, i + 1) for i in range(count - 1)]),
        move(first, [(i + 1, i) for i in range(count - 1)]),
    )


def fill(lo, pairs, stacked, frame, row, cols, cells):
    n_rows = cells.shape[0]
    at = pl.ds(row, n_rows)
    low, high = cells[:, :, :LANES], cells[:, :, LANES:]
    rest = high.shape[-1]
    lo[frame, at, cols, :] = low
    pairs[frame, pl.ds(row + 1, n_rows), cols, :rest] = high
    pairs[frame, at, cols, rest:] = high
    if frame < stacked.shape[0]:
        stacked[frame, at, cols, :rest] = high
    if frame > 0:
        stacked[frame - 1, at, cols, rest:] = high


def columns(taps, lo, pairs, stacked, row, rows):
    def flat(block):
        return block.reshape(-1, LANES)

    pieces = [flat(lo[f, pl.ds(row + b, rows)]) for f, _ in taps for b in range(3)]
    pieces += [flat(pairs[f, pl.ds(row + 1, rows)]) for f, _ in taps]
    for k in range(0, len(taps), 2):
        f = taps[k][0]
        if k + 1 < len(taps):
            pieces.append(flat(stacked[f, pl.ds(row + 2, rows)]))
        else:
            pieces.append(flat(pairs[f, pl.ds(row + 3, rows)]))
    return jnp.concatenate(pieces, axis=-1)


def planes(taps, weight, c):
    pieces = [weight[a, b, c, :LANES, :] for _, a in taps for b in range(3)]
    for _, a in taps:
        pieces += [weight[a, 0, c, LANES:, :], weight[a, 1, c, LANES:, :]]
    for _, a in taps:
        pieces.append(weight[a, 2, c, LANES:, :])
    if len(taps) % 2:
        pieces.append(jnp.zeros_like(weight[0, 0, 0, LANES:, :]))
    return jnp.concatenate(pieces, axis=0)


def convolve(taps, weight, lefts):
    return [
        jnp.dot(lefts, planes(taps, weight, c), preferred_element_type=jnp.float32)
        for c in range(3)
    ]


def join(products, start, width):
    before, middle, after = [p[start : start + width] for p in products]
    return pltpu.roll(before, 1, 0) + middle + pltpu.roll(after, width - 1, 0)


def activate(y, gains):
    mean_square = jnp.sum(y * y, axis=-1, keepdims=True) * (1.0 / y.shape[-1])
    v = y * lax.rsqrt(mean_square + EPS) * gains
    return v / (1.0 + jnp.exp(-v))


def keep_halo(cells, slabs, side):
    at = lax.broadcasted_iota(jnp.int32, cells.shape, cells.ndim - 2)
    if side is None:
        side = 1 - lax.axis_index("slab")
    begin, end = jnp.where(side == 1, 0, TILE - 2), jnp.where(side == 1, 2, TILE)
    wanted = (at >= begin) & (at < end)
    return jnp.where(wanted, cells.astype(jnp.float32), 0.0).astype(cells.dtype)


def first_kernel(strips, slabs, n_rows_h, *refs):
    n_strip = 1 if strips == 2 else 2
    n_slab = 1 if slabs == 2 else 2
    refs = list(refs)

    def take(n):
        got = refs[:n]
        del refs[:n]
        return got

    (own, prev) = take(2)
    own_rows, prev_rows = take(n_strip), take(n_strip)
    own_cols, prev_cols = take(n_slab), take(n_slab)
    w1, gains, w2 = take(3)
    h_lo, h_pairs, h_stacked, partial = take(4)
    lo, pairs, stacked = take(3)

    frames, rows, cols, channels = own.shape
    width = cols + TILE
    strip, slab = lax.axis_index("strip"), lax.axis_index("slab")

    for buffer in (lo, pairs, stacked):
        buffer[...] = jnp.zeros_like(buffer)

    def tiles(received, f, k):
        if slabs == 2:
            return keep_halo(received[0][f, k], slabs, None)
        return keep_halo(received[0][f, k], slabs, 0) + keep_halo(received[1][f, k], slabs, 1)

    every = slice(0, cols)
    edge = slice(cols, width)
    for source, source_rows, source_cols, base, skip in (
        (prev, prev_rows, prev_cols, 0, frames - 2),
        (own, own_rows, own_cols, 2, 0),
    ):
        for f in range(skip, frames):
            at = base + f - skip
            fill(lo, pairs, stacked, at, 2, every, source[f])
            fill(lo, pairs, stacked, at, 2, edge, tiles(source_cols, f, slice(None)))
            if strips == 2:
                places = [(source_rows[0], jnp.where(strip == 0, rows + 2, 0))]
            else:
                places = [(source_rows[0], 0), (source_rows[1], rows + 2)]
            for received, row in places:
                fill(lo, pairs, stacked, at, row, every, received[f, :, :cols])
                if slabs == 2:
                    corner = keep_halo(received[f, :, cols:], slabs, None)
                else:
                    corner = received[f, :, cols:]
                fill(lo, pairs, stacked, at, row, edge, corner)

    origin = jnp.where(strip == 0, 1, 0) if strips == 2 else 0
    lefts = jnp.concatenate(
        [
            columns([(t, 0), (t + 1, 1), (t + 2, 2)], lo, pairs, stacked, origin, n_rows_h)
            for t in range(frames)
        ],
        axis=0,
    )
    products = convolve([(0, 0), (1, 1), (2, 2)], w1, lefts)

    for buffer in (h_lo, h_pairs, h_stacked):
        buffer[...] = jnp.zeros_like(buffer)
    gain = gains[...]
    position = lax.broadcasted_iota(jnp.int32, (width, 1), 0)
    right, left = jnp.where(slab < slabs - 1, cols + 1, cols), jnp.where(slab > 0, width - 1, width)
    inside = (position < right) | (position >= left)
    for t in range(frames):
        for r in range(n_rows_h):
            h = activate(join(products, (t * n_rows_h + r) * width, width), gain)
            h = jnp.where(inside, h, 0.0)
            if strips != 2 and r == 0:
                h = h * jnp.where(strip > 0, 1.0, 0.0)
            if strips != 2 and r == n_rows_h - 1:
                h = h * jnp.where(strip < strips - 1, 1.0, 0.0)
            h = h.astype(jnp.bfloat16)
            fill(h_lo, h_pairs, h_stacked, t, origin + r, slice(0, width), h[None])

    last = frames - 1
    for t, taps in enumerate(([(last - 1, 0), (last, 1)], [(last, 0)])):
        lefts = columns(taps, h_lo, h_pairs, h_stacked, 0, rows)
        products = convolve(taps, w2, lefts)
        for r in range(rows):
            y = join(products, r * width, width)[:cols].astype(jnp.bfloat16)
            rest = channels - LANES
            partial[t, r] = y[:, :LANES]
            half = r % 2
            partial[t, rows + r // 2, :, half * rest : (half + 1) * rest] = y[:, LANES:]


def second_kernel(frames, rows, cols, h_lo, h_pairs, h_stacked, w2, out):
    width = cols + TILE
    for t in range(frames):
        taps = [(f, f - t + 2) for f in range(max(0, t - 2), t + 1)]
        products = convolve(taps, w2, columns(taps, h_lo, h_pairs, h_stacked, 0, rows))
        for r in range(rows):
            out[t, r] = join(products, r * width, width)[:cols]


def third_kernel(partial, own, gains, out):
    frames, rows, cols, channels = out.shape
    rest = channels - LANES
    gain = gains[...]
    for t in range(frames):
        for r in range(rows):
            y = own[t, r]
            if t < 2:
                half = r % 2
                high = partial[t, rows + r // 2, :, half * rest : (half + 1) * rest]
                sent = jnp.concatenate([partial[t, r], high], axis=-1)
                y = y + sent.astype(jnp.float32)
            out[t, r] = activate(y, gain).astype(jnp.bfloat16)


def in_vmem(n):
    return [pl.BlockSpec(memory_space=pltpu.VMEM)] * n


def forward(x):
    steps = lax.axis_size("frame")
    return lax.ppermute(x, "frame", [(i, i + 1) for i in range(steps - 1)])


def shards(frames_in, weight_first, scale_first, weight_second, scale_second):
    frames, rows, cols, channels = frames_in.shape
    strips, slabs = lax.axis_size("strip"), lax.axis_size("slab")
    width = cols + TILE
    n_rows_h = rows + 1 if strips == 2 else rows + 2
    gain_first, gain_second = scale_first[None], scale_second[None]
    weight_first = pltpu.with_memory_space_constraint(weight_first, pltpu.VMEM)
    weight_second = pltpu.with_memory_space_constraint(weight_second, pltpu.VMEM)

    def edge_cols(x):
        return exchange(x[:, :, :TILE], x[:, :, cols - TILE :], "slab")

    prev = forward(frames_in)
    own_cols = edge_cols(frames_in)

    def wide(rows_of, at):
        if slabs == 2:
            tile = own_cols[0][:, at]
        else:
            spot = lax.broadcasted_iota(jnp.int32, (1, 1, TILE, 1), 2)
            tile = jnp.where(spot < 2, own_cols[1][:, at], jnp.where(spot >= TILE - 2, own_cols[0][:, at], 0))
        return jnp.concatenate([rows_of[:, at], tile], axis=2)

    top, bottom = wide(frames_in, slice(0, 2)), wide(frames_in, slice(rows - 2, rows))
    own_rows = exchange(top, bottom, "strip")
    prev_rows = exchange(top, bottom, "strip", 1)
    prev_cols = edge_cols(prev)

    h_shapes = [
        jax.ShapeDtypeStruct((frames, rows + 2, width, LANES), jnp.bfloat16),
        jax.ShapeDtypeStruct((frames, rows + 3, width, LANES), jnp.bfloat16),
        jax.ShapeDtypeStruct((frames - 1, rows + 2, width, LANES), jnp.bfloat16),
    ]
    ins = [frames_in, prev, *own_rows, *prev_rows, *own_cols, *prev_cols, weight_first, gain_first, weight_second]
    h_lo, h_pairs, h_stacked, partial = pl.pallas_call(
        functools.partial(first_kernel, strips, slabs, n_rows_h),
        out_shape=h_shapes + [jax.ShapeDtypeStruct((2, rows + rows // 2, cols, LANES), jnp.bfloat16)],
        in_specs=in_vmem(len(ins)),
        out_specs=in_vmem(4),
        scratch_shapes=[
            pltpu.VMEM((frames + 2, rows + 4, width, LANES), jnp.bfloat16),
            pltpu.VMEM((frames + 2, rows + 5, width, LANES), jnp.bfloat16),
            pltpu.VMEM((frames + 1, rows + 4, width, LANES), jnp.bfloat16),
        ],
        compiler_params=pltpu.CompilerParams(vmem_limit_bytes=32 * 1024 * 1024),
        name="first_layer",
    )(*ins)
    sent = forward(partial)
    taps = frames * rows * cols * 27 * channels * channels
    own = pl.pallas_call(
        functools.partial(second_kernel, frames, rows, cols),
        out_shape=jax.ShapeDtypeStruct((frames, rows, cols, channels), jnp.float32),
        in_specs=in_vmem(4),
        out_specs=in_vmem(1)[0],
        compiler_params=pltpu.CompilerParams(vmem_limit_bytes=32 * 1024 * 1024),
        cost_estimate=pl.CostEstimate(flops=taps, bytes_accessed=4 * 1024 * 1024, transcendentals=0),
        name="second_layer",
    )(h_lo, h_pairs, h_stacked, weight_second)
    return pl.pallas_call(
        third_kernel,
        out_shape=jax.ShapeDtypeStruct((frames, rows, cols, channels), jnp.bfloat16),
        in_specs=in_vmem(3),
        out_specs=in_vmem(1)[0],
        compiler_params=pltpu.CompilerParams(vmem_limit_bytes=32 * 1024 * 1024),
        name="finish",
    )(sent, own, gain_second)


def solution(mesh):
    return jax.shard_map(
        shards,
        mesh=mesh,
        in_specs=(P(("groups", "frame"), "strip", "slab", None), P(), P(), P(), P()),
        out_specs=P(("groups", "frame"), "strip", "slab", None),
        check_vma=False,
    )
```

```python
import functools

import jax
import jax.numpy as jnp
from jax import lax
from jax.experimental import pallas as pl
from jax.experimental.pallas import tpu as pltpu
from jax.sharding import PartitionSpec as P

LANES = 128
TILE = 16
EPS = 1e-06


HALO = 2


def swap(x, axis, offset=0):
    return shift(x, axis, [(0, 1), (1, 0)], offset)


def shift(x, axis, pairs, offset=0):
    if offset == 0:
        return lax.ppermute(x, axis, pairs)
    count, steps = lax.axis_size(axis), lax.axis_size("frame")
    both = [(f * count + i, (f + offset) * count + j) for f in range(steps - offset) for i, j in pairs]
    return lax.ppermute(x, ("frame", axis), both)


def forward(x):
    steps = lax.axis_size("frame")
    return lax.ppermute(x, "frame", [(i, i + 1) for i in range(steps - 1)])


class Packed:
    def __init__(self, frames, rows, cols):
        self.frames, self.rows, self.cols = frames, rows, cols
        self.high = frames * rows * cols
        self.beside = self.high + frames * (rows // 2) * cols
        self.tiles = -(-frames * rows * HALO // TILE)
        self.shape = (self.beside + 2 * self.tiles * TILE, LANES)

    def low_at(self, f, r):
        return slice((f * self.rows + r) * self.cols, (f * self.rows + r + 1) * self.cols)

    def high_at(self, f, r):
        start = self.high + (f * (self.rows // 2) + r // 2) * self.cols
        return slice(start, start + self.cols)

    def spot(self, f, r):
        cell = (f * self.rows + r) * HALO
        return cell // TILE, cell % TILE

    def beside_at(self, tile, high):
        start = self.beside + (2 * tile + high) * TILE
        return slice(start, start + TILE)

    def write(self, out, cells, tile_of):
        slab = lax.axis_index("slab")
        at = lax.broadcasted_iota(jnp.int32, (TILE, 1), 0)
        sums = [None] * self.tiles
        for f in range(self.frames):
            for r in range(self.rows):
                row = cells(f, r)
                out[self.low_at(f, r), :] = row[:, :LANES]
                rest = row.shape[-1] - LANES
                half = slice((r % 2) * rest, (r % 2 + 1) * rest)
                out[self.high_at(f, r), half] = row[:, LANES:]
                tile, place = self.spot(f, r)
                moved = pltpu.roll(tile_of(f, r).astype(jnp.float32), lax.rem(place + HALO * slab, TILE), 0)
                moved = jnp.where((at >= place) & (at < place + HALO), moved, 0.0)
                sums[tile] = moved if sums[tile] is None else sums[tile] + moved
        for tile, cells_beside in enumerate(sums):
            cells_beside = cells_beside.astype(jnp.bfloat16)
            out[self.beside_at(tile, 0), :] = cells_beside[:, :LANES]
            out[self.beside_at(tile, 1), :rest] = cells_beside[:, LANES:]

    def read(self, ref, f, r, rest):
        half = slice((r % 2) * rest, (r % 2 + 1) * rest)
        return ref[self.low_at(f, r), :], ref[self.high_at(f, r), half]

    def read_beside(self, ref, f, r, rest):
        slab = lax.axis_index("slab")
        tile, place = self.spot(f, r)
        parts = []
        for high, lanes in ((0, LANES), (1, rest)):
            cells = ref[self.beside_at(tile, high), :].astype(jnp.float32)
            cells = pltpu.roll(cells, lax.rem(2 * TILE - place - HALO * slab, TILE), 0)
            parts.append(only_beside(cells).astype(jnp.bfloat16)[:, :lanes])
        return parts


def only_beside(tile):
    slab = lax.axis_index("slab")
    at = lax.broadcasted_iota(jnp.int32, tile.shape, 0)
    begin = slab * (TILE - HALO)
    return jnp.where((at >= begin) & (at < begin + HALO), tile, 0.0)


def fill(lo, pairs, stacked, frame, row, cols, low, high):
    rest = high.shape[-1]
    lo[frame, row, cols, :] = low
    pairs[frame, row + 1, cols, :rest] = high
    pairs[frame, row, cols, rest:] = high
    if frame < stacked.shape[0]:
        stacked[frame, row, cols, :rest] = high
    if frame > 0:
        stacked[frame - 1, row, cols, rest:] = high


def columns(taps, lo, pairs, stacked, row, rows):
    def flat(block):
        return block.reshape(-1, LANES)

    pieces = [flat(lo[f, pl.ds(row + b, rows)]) for f, _ in taps for b in range(3)]
    pieces += [flat(pairs[f, pl.ds(row + 1, rows)]) for f, _ in taps]
    for k in range(0, len(taps), 2):
        f = taps[k][0]
        if k + 1 < len(taps):
            pieces.append(flat(stacked[f, pl.ds(row + 2, rows)]))
        else:
            pieces.append(flat(pairs[f, pl.ds(row + 3, rows)]))
    return jnp.concatenate(pieces, axis=-1)


def planes(taps, weight, c):
    pieces = [weight[a, b, c, :LANES, :] for _, a in taps for b in range(3)]
    for _, a in taps:
        pieces += [weight[a, 0, c, LANES:, :], weight[a, 1, c, LANES:, :]]
    for _, a in taps:
        pieces.append(weight[a, 2, c, LANES:, :])
    if len(taps) % 2:
        pieces.append(jnp.zeros_like(weight[0, 0, 0, LANES:, :]))
    return jnp.concatenate(pieces, axis=0)


def convolve(taps, weight, lefts):
    return [
        jnp.dot(lefts, planes(taps, weight, c), preferred_element_type=jnp.float32)
        for c in range(3)
    ]


def join(products, start, width):
    before, middle, after = [p[start : start + width] for p in products]
    return pltpu.roll(before, 1, 0) + middle + pltpu.roll(after, width - 1, 0)


def activate(y, gains):
    mean_square = jnp.sum(y * y, axis=-1, keepdims=True) * (1.0 / y.shape[-1])
    v = y * lax.rsqrt(mean_square + EPS) * gains
    return v / (1.0 + jnp.exp(-v))


def fetch_planes(source, target, arrived):
    copies = [pltpu.make_async_copy(source.at[a], target.at[a], arrived.at[a]) for a in range(3)]
    for copy in copies[::-1]:
        copy.start()
    waited = set()

    def wait(a):
        if a not in waited:
            copies[a].wait()
            waited.add(a)

    return wait


def clear(buffers):
    for buffer in buffers:
        buffer[...] = jnp.zeros_like(buffer)


def facing(strips, rows):
    if strips == 2:
        return [jnp.where(lax.axis_index("strip") == 0, rows - HALO, 0)]
    return [rows - HALO, 0]


def beyond(strips, rows):
    if strips == 2:
        return [jnp.where(lax.axis_index("strip") == 0, rows + HALO, 0)]
    return [0, rows + HALO]


def first_row(strips):
    return 1 - lax.axis_index("strip") if strips == 2 else 0


def beside_of(neighbour, f, r, cols):
    start = pl.multiple_of(lax.axis_index("slab") * (cols - TILE), TILE)
    return neighbour[f, r, pl.ds(start, TILE), :]


def pack_kernel(strips, own, neighbour, block, *edges):
    frames, rows, cols, _ = own.shape
    whole = Packed(HALO, rows, cols)
    skip = frames - HALO
    whole.write(block, lambda f, r: own[f + skip, r], lambda f, r: beside_of(neighbour, f + skip, r, cols))
    for start, edge in zip(facing(strips, rows), edges):
        Packed(frames, HALO, cols).write(
            edge, lambda f, r: own[f, start + r], lambda f, r: beside_of(neighbour, f, start + r, cols)
        )


def own_kernel(strips, n_rows_h, *refs):
    own, neighbour, *edges, weight_far, out, weight, lo, pairs, stacked, arrived = refs
    frames, rows, cols, channels = own.shape
    fetch = fetch_planes(weight_far, weight, arrived)
    width, rest = cols + TILE, channels - LANES
    every, beside = slice(0, cols), slice(cols, width)
    clear((lo, pairs, stacked))
    strip_block = Packed(frames, HALO, cols)
    for f in range(frames):
        for r in range(rows):
            cells = own[f, r]
            fill(lo, pairs, stacked, f, r + HALO, every, cells[:, :LANES], cells[:, LANES:])
            tile = only_beside(beside_of(neighbour, f, r, cols).astype(jnp.float32)).astype(jnp.bfloat16)
            fill(lo, pairs, stacked, f, r + HALO, beside, tile[:, :LANES], tile[:, LANES:])
        for edge, row in zip(edges, beyond(strips, rows)):
            for r in range(HALO):
                fill(lo, pairs, stacked, f, row + r, every, *strip_block.read(edge, f, r, rest))
                fill(lo, pairs, stacked, f, row + r, beside, *strip_block.read_beside(edge, f, r, rest))
    for t in range(frames):
        taps = [(f, f - t + 2) for f in range(max(0, t - 2), t + 1)]
        for _, a in taps:
            fetch(a)
        products = convolve(taps, weight, columns(taps, lo, pairs, stacked, first_row(strips), n_rows_h))
        for r in range(n_rows_h):
            out[t, r] = join(products, r * width, width)
    for a in range(3):
        fetch(a)


def first_kernel(strips, n_rows_h, rows, cols, *refs):
    block, *edges, own, w1, gains, w2_far, h_lo, h_pairs, h_stacked, partial, w2, lo, pairs, stacked, arrived = refs
    fetch = fetch_planes(w2_far, w2, arrived)
    frames, channels = own.shape[0], own.shape[-1]
    width, rest = cols + TILE, channels - LANES
    every, beside = slice(0, cols), slice(cols, width)
    strip, slab = lax.axis_index("strip"), lax.axis_index("slab")
    clear((lo, pairs, stacked, h_lo, h_pairs, h_stacked))
    whole, strip_block = Packed(HALO, rows, cols), Packed(frames, HALO, cols)
    for f in range(HALO):
        for r in range(rows):
            fill(lo, pairs, stacked, f, r + HALO, every, *whole.read(block, f, r, rest))
            fill(lo, pairs, stacked, f, r + HALO, beside, *whole.read_beside(block, f, r, rest))
        for edge, row in zip(edges, beyond(strips, rows)):
            for r in range(HALO):
                sent = frames - HALO + f
                fill(lo, pairs, stacked, f, row + r, every, *strip_block.read(edge, sent, r, rest))
                fill(lo, pairs, stacked, f, row + r, beside, *strip_block.read_beside(edge, sent, r, rest))

    origin = first_row(strips)
    gain = gains[...]
    position = lax.broadcasted_iota(jnp.int32, (width, 1), 0)
    right = cols + (slab == 0).astype(jnp.int32)
    left = width - (slab == 1).astype(jnp.int32)
    inside = (position < right) | (position >= left)
    for t in range(frames):
        taps = [(f, f - t) for f in range(t, HALO)]
        products = convolve(taps, w1, columns(taps, lo, pairs, stacked, origin, n_rows_h)) if taps else None
        for r in range(n_rows_h):
            y = own[t, r]
            if taps:
                y = y + join(products, r * width, width)
            h = jnp.where(inside, activate(y, gain), 0.0)
            if strips != 2 and r == 0:
                h = h * jnp.where(strip > 0, 1.0, 0.0)
            if strips != 2 and r == n_rows_h - 1:
                h = h * jnp.where(strip < strips - 1, 1.0, 0.0)
            h = h.astype(jnp.bfloat16)
            fill(h_lo, h_pairs, h_stacked, t, origin + r, slice(0, width), h[:, :LANES], h[:, LANES:])

    for a in range(3):
        fetch(a)
    last = frames - 1
    for t, taps in enumerate(([(last - 1, 0), (last, 1)], [(last, 0)])):
        products = convolve(taps, w2, columns(taps, h_lo, h_pairs, h_stacked, 0, rows))
        for r in range(rows):
            y = join(products, r * width, width)[:cols].astype(jnp.bfloat16)
            partial[t, r] = y[:, :LANES]
            half = r % 2
            partial[t, rows + r // 2, :, half * rest : (half + 1) * rest] = y[:, LANES:]


def second_kernel(frames, rows, cols, h_lo, h_pairs, h_stacked, w2, out):
    width = cols + TILE
    for t in range(frames):
        taps = [(f, f - t + 2) for f in range(max(0, t - 2), t + 1)]
        products = convolve(taps, w2, columns(taps, h_lo, h_pairs, h_stacked, 0, rows))
        for r in range(rows):
            out[t, r] = join(products, r * width, width)[:cols]


def third_kernel(partial, own, gains, out):
    frames, rows, cols, channels = out.shape
    rest = channels - LANES
    gain = gains[...]
    for t in range(frames):
        for r in range(rows):
            y = own[t, r]
            if t < 2:
                half = r % 2
                high = partial[t, rows + r // 2, :, half * rest : (half + 1) * rest]
                sent = jnp.concatenate([partial[t, r], high], axis=-1)
                y = y + sent.astype(jnp.float32)
            out[t, r] = activate(y, gain).astype(jnp.bfloat16)


def in_vmem(n):
    return [pl.BlockSpec(memory_space=pltpu.VMEM)] * n


def call(kernel, name, ins, outs, scratch=(), flops=0, far=()):
    in_specs, ins = in_vmem(len(ins)), list(ins)
    for place in far:
        ins[place] = pltpu.with_memory_space_constraint(ins[place], pltpu.HBM)
        in_specs[place] = pl.BlockSpec(memory_space=pltpu.HBM)
    return pl.pallas_call(
        kernel,
        out_shape=outs,
        in_specs=in_specs,
        out_specs=in_vmem(len(outs)) if isinstance(outs, list) else in_vmem(1)[0],
        scratch_shapes=[pltpu.VMEM(shape, jnp.bfloat16) for shape in scratch]
        + [pltpu.SemaphoreType.DMA((3,))] * len(far),
        compiler_params=pltpu.CompilerParams(vmem_limit_bytes=24 * 1024 * 1024),
        cost_estimate=pl.CostEstimate(flops=flops, bytes_accessed=4 * 1024 * 1024, transcendentals=0),
        name=name,
    )(*ins)


def block_scratch(frames, rows, width):
    return [(frames, rows, width, LANES), (frames, rows + 1, width, LANES), (frames - 1, rows, width, LANES)]


def shards(frames_in, weight_first, scale_first, weight_second, scale_second):
    frames, rows, cols, channels = frames_in.shape
    strips = lax.axis_size("strip")
    width = cols + TILE
    n_rows_h = rows + 1 if strips == 2 else rows + 2
    flops = frames * rows * cols * 27 * channels * channels
    bf16 = functools.partial(jax.ShapeDtypeStruct, dtype=jnp.bfloat16)
    f32 = functools.partial(jax.ShapeDtypeStruct, dtype=jnp.float32)

    neighbour = swap(frames_in, "slab")
    edge_shape = bf16(Packed(frames, HALO, cols).shape)
    block, *edges = call(
        functools.partial(pack_kernel, strips),
        "pack",
        [frames_in, neighbour],
        [bf16(Packed(HALO, rows, cols).shape)] + [edge_shape] * (1 if strips == 2 else 2),
    )
    ups = [(i, i + 1) for i in range(strips - 1)]
    downs = [(i + 1, i) for i in range(strips - 1)]
    ways = [[(0, 1), (1, 0)]] if strips == 2 else [ups, downs]
    before = forward(block)
    own_edges = [shift(edge, "strip", way) for edge, way in zip(edges, ways)]
    before_edges = [shift(edge, "strip", way, 1) for edge, way in zip(edges, ways)]

    weight_shape = bf16(weight_first.shape)
    own, weight_first = call(
        functools.partial(own_kernel, strips, n_rows_h),
        "first_layer_own",
        [frames_in, neighbour, *own_edges, weight_first],
        [f32((frames, n_rows_h, width, channels)), weight_shape],
        block_scratch(frames, rows + 2 * HALO, width),
        flops,
        far=[-1],
    )
    h_shapes = [bf16(shape) for shape in block_scratch(frames, rows + 2, width)]
    h_lo, h_pairs, h_stacked, partial, weight_second = call(
        functools.partial(first_kernel, strips, n_rows_h, rows, cols),
        "first_layer",
        [before, *before_edges, own, weight_first, scale_first[None], weight_second],
        h_shapes + [bf16((HALO, rows + rows // 2, cols, LANES)), weight_shape],
        block_scratch(HALO, rows + 2 * HALO, width),
        flops,
        far=[-1],
    )
    sent = forward(partial)
    own = call(
        functools.partial(second_kernel, frames, rows, cols),
        "second_layer",
        [h_lo, h_pairs, h_stacked, weight_second],
        f32((frames, rows, cols, channels)),
        flops=flops,
    )
    return call(third_kernel, "finish", [sent, own, scale_second[None]], bf16((frames, rows, cols, channels)))


def solution(mesh):
    return jax.shard_map(
        shards,
        mesh=mesh,
        in_specs=(P(("groups", "frame"), "strip", "slab", None), P(), P(), P(), P()),
        out_specs=P(("groups", "frame"), "strip", "slab", None),
        check_vma=False,
    )
```

```python
import functools

import jax
import jax.numpy as jnp
from jax import lax
from jax.experimental import pallas as pl
from jax.experimental.pallas import tpu as pltpu
from jax.sharding import PartitionSpec as P

LANES = 128
TILE = 16
EPS = 1e-06


HALO = 2


def swap(x, axis):
    return lax.ppermute(x, axis, [(0, 1), (1, 0)])


def forward(x, way=None):
    steps, count = lax.axis_size("frame"), lax.axis_size("strip")
    way = [(i, i) for i in range(count)] if way is None else way
    received = []
    for parity in range(2):
        there = [(f * count + i, (f + 1) * count + j) for f in range(parity, steps - 1, 2) for i, j in way]
        received.append(lax.ppermute(x, ("frame", "strip"), there + [(j, i) for i, j in there]))
    return received


def by_parity(build, first, second):
    odd = lax.rem(lax.axis_index("frame"), 2) == 1
    pl.when(odd)(lambda: build(first))
    pl.when(jnp.logical_not(odd))(lambda: build(second))


class Packed:
    def __init__(self, frames, rows, cols):
        self.frames, self.rows, self.cols = frames, rows, cols
        self.high = frames * rows * cols
        self.beside = self.high + frames * (rows // 2) * cols
        self.tiles = -(-frames * rows * HALO // TILE)
        self.shape = (self.beside + 2 * self.tiles * TILE, LANES)

    def low_at(self, f, r):
        return slice((f * self.rows + r) * self.cols, (f * self.rows + r + 1) * self.cols)

    def high_at(self, f, r):
        start = self.high + (f * (self.rows // 2) + r // 2) * self.cols
        return slice(start, start + self.cols)

    def spot(self, f, r):
        cell = (f * self.rows + r) * HALO
        return cell // TILE, cell % TILE

    def beside_at(self, tile, high):
        start = self.beside + (2 * tile + high) * TILE
        return slice(start, start + TILE)

    def write(self, out, cells, tile_of):
        slab = lax.axis_index("slab")
        at = lax.broadcasted_iota(jnp.int32, (TILE, 1), 0)
        sums = [None] * self.tiles
        for f in range(self.frames):
            for r in range(self.rows):
                row = cells(f, r)
                out[self.low_at(f, r), :] = row[:, :LANES]
                rest = row.shape[-1] - LANES
                half = slice((r % 2) * rest, (r % 2 + 1) * rest)
                out[self.high_at(f, r), half] = row[:, LANES:]
                tile, place = self.spot(f, r)
                moved = pltpu.roll(tile_of(f, r).astype(jnp.float32), lax.rem(place + HALO * slab, TILE), 0)
                moved = jnp.where((at >= place) & (at < place + HALO), moved, 0.0)
                sums[tile] = moved if sums[tile] is None else sums[tile] + moved
        for tile, cells_beside in enumerate(sums):
            cells_beside = cells_beside.astype(jnp.bfloat16)
            out[self.beside_at(tile, 0), :] = cells_beside[:, :LANES]
            out[self.beside_at(tile, 1), :rest] = cells_beside[:, LANES:]

    def read(self, ref, f, r, rest):
        half = slice((r % 2) * rest, (r % 2 + 1) * rest)
        return ref[self.low_at(f, r), :], ref[self.high_at(f, r), half]

    def read_beside(self, ref, f, r, rest):
        slab = lax.axis_index("slab")
        tile, place = self.spot(f, r)
        parts = []
        for high, lanes in ((0, LANES), (1, rest)):
            cells = ref[self.beside_at(tile, high), :].astype(jnp.float32)
            cells = pltpu.roll(cells, lax.rem(2 * TILE - place - HALO * slab, TILE), 0)
            parts.append(only_beside(cells).astype(jnp.bfloat16)[:, :lanes])
        return parts


def only_beside(tile):
    slab = lax.axis_index("slab")
    at = lax.broadcasted_iota(jnp.int32, tile.shape, 0)
    begin = slab * (TILE - HALO)
    return jnp.where((at >= begin) & (at < begin + HALO), tile, 0.0)


def fill(lo, pairs, stacked, frame, row, cols, low, high):
    rest = high.shape[-1]
    lo[frame, row, cols, :] = low
    pairs[frame, row + 1, cols, :rest] = high
    pairs[frame, row, cols, rest:] = high
    if frame < stacked.shape[0]:
        stacked[frame, row, cols, :rest] = high
    if frame > 0:
        stacked[frame - 1, row, cols, rest:] = high


def columns(taps, lo, pairs, stacked, row, rows):
    def flat(block):
        return block.reshape(-1, LANES)

    pieces = [flat(lo[f, pl.ds(row + b, rows)]) for f, _ in taps for b in range(3)]
    pieces += [flat(pairs[f, pl.ds(row + 1, rows)]) for f, _ in taps]
    for k in range(0, len(taps), 2):
        f = taps[k][0]
        if k + 1 < len(taps):
            pieces.append(flat(stacked[f, pl.ds(row + 2, rows)]))
        else:
            pieces.append(flat(pairs[f, pl.ds(row + 3, rows)]))
    return jnp.concatenate(pieces, axis=-1)


def planes(taps, weight, c):
    pieces = [weight[a][b, c, :LANES, :] for _, a in taps for b in range(3)]
    for _, a in taps:
        pieces += [weight[a][0, c, LANES:, :], weight[a][1, c, LANES:, :]]
    for _, a in taps:
        pieces.append(weight[a][2, c, LANES:, :])
    if len(taps) % 2:
        pieces.append(jnp.zeros_like(weight[a][0, c, LANES:, :]))
    return jnp.concatenate(pieces, axis=0)


def convolve(taps, weight, lefts):
    return [
        jnp.dot(lefts, planes(taps, weight, c), preferred_element_type=jnp.float32)
        for c in range(3)
    ]


def join(products, start, width):
    before, middle, after = [p[start : start + width] for p in products]
    return pltpu.roll(before, 1, 0) + middle + pltpu.roll(after, width - 1, 0)


def activate(y, gains):
    mean_square = jnp.sum(y * y, axis=-1, keepdims=True) * (1.0 / y.shape[-1])
    v = y * lax.rsqrt(mean_square + EPS) * gains
    return v / (1.0 + jnp.exp(-v))


def clear(buffers):
    for buffer in buffers:
        buffer[...] = jnp.zeros_like(buffer)


def facing(strips, rows):
    if strips == 2:
        return [jnp.where(lax.axis_index("strip") == 0, rows - HALO, 0)]
    return [rows - HALO, 0]


def beyond(strips, rows):
    if strips == 2:
        return [jnp.where(lax.axis_index("strip") == 0, rows + HALO, 0)]
    return [0, rows + HALO]


def first_row(strips):
    return 1 - lax.axis_index("strip") if strips == 2 else 0


def beside_of(neighbour, f, r, cols):
    start = pl.multiple_of(lax.axis_index("slab") * (cols - TILE), TILE)
    return neighbour[f, r, pl.ds(start, TILE), :]


def stage_kernel(own_far, weight_far, own, middle, last, arrived):
    copies = [
        pltpu.make_async_copy(own_far, own, arrived.at[0]),
        pltpu.make_async_copy(weight_far.at[2], last, arrived.at[1]),
        pltpu.make_async_copy(weight_far.at[1], middle, arrived.at[2]),
    ]
    for copy in copies:
        copy.start()
    for copy in copies:
        copy.wait()


def pack_kernel(strips, own, neighbour, block, *edges):
    frames, rows, cols, _ = own.shape
    whole = Packed(HALO, rows, cols)
    skip = frames - HALO
    whole.write(block, lambda f, r: own[f + skip, r], lambda f, r: beside_of(neighbour, f + skip, r, cols))
    for start, edge in zip(facing(strips, rows), edges):
        Packed(frames, HALO, cols).write(
            edge, lambda f, r: own[f, start + r], lambda f, r: beside_of(neighbour, f, start + r, cols)
        )


def own_kernel(strips, n_rows_h, *refs):
    own, neighbour, *edges, middle, last, weight_far, out, plane, lo, pairs, stacked, arrived = refs
    frames, rows, cols, channels = own.shape
    copy = pltpu.make_async_copy(weight_far.at[0], plane, arrived.at[0])
    copy.start()
    if frames > 2:
        copy.wait()
    width, rest = cols + TILE, channels - LANES
    every, beside = slice(0, cols), slice(cols, width)
    clear((lo, pairs, stacked))
    strip_block = Packed(frames, HALO, cols)
    for f in range(frames):
        for r in range(rows):
            cells = own[f, r]
            fill(lo, pairs, stacked, f, r + HALO, every, cells[:, :LANES], cells[:, LANES:])
            tile = only_beside(beside_of(neighbour, f, r, cols).astype(jnp.float32)).astype(jnp.bfloat16)
            fill(lo, pairs, stacked, f, r + HALO, beside, tile[:, :LANES], tile[:, LANES:])
        for edge, row in zip(edges, beyond(strips, rows)):
            for r in range(HALO):
                fill(lo, pairs, stacked, f, row + r, every, *strip_block.read(edge, f, r, rest))
                fill(lo, pairs, stacked, f, row + r, beside, *strip_block.read_beside(edge, f, r, rest))
    for t in range(frames):
        taps = [(f, f - t + 2) for f in range(max(0, t - 2), t + 1)]
        products = convolve(taps, [plane, middle, last], columns(taps, lo, pairs, stacked, first_row(strips), n_rows_h))
        for r in range(n_rows_h):
            out[t, r] = join(products, r * width, width)
    if frames <= 2:
        copy.wait()


def first_kernel(strips, n_rows_h, rows, cols, *refs):
    *refs, lo, pairs, stacked, arrived = refs
    *refs, h_lo, h_pairs, h_stacked, partial, w2_first, w2_middle, w2_last = refs
    *received, own, plane, middle, gains, w2_far = refs
    w2 = [w2_first, w2_middle, w2_last]
    copies = [pltpu.make_async_copy(w2_far.at[a], w2[a], arrived.at[a]) for a in range(3)]
    for copy in copies:
        copy.start()
    frames, channels = own.shape[0], own.shape[-1]
    width, rest = cols + TILE, channels - LANES
    every, beside = slice(0, cols), slice(cols, width)
    strip, slab = lax.axis_index("strip"), lax.axis_index("slab")
    clear((lo, pairs, stacked, h_lo, h_pairs, h_stacked))
    whole, strip_block = Packed(HALO, rows, cols), Packed(frames, HALO, cols)

    def build(pieces):
        block, *edges = pieces
        for f in range(HALO):
            for r in range(rows):
                fill(lo, pairs, stacked, f, r + HALO, every, *whole.read(block, f, r, rest))
                fill(lo, pairs, stacked, f, r + HALO, beside, *whole.read_beside(block, f, r, rest))
            for edge, row in zip(edges, beyond(strips, rows)):
                for r in range(HALO):
                    sent = frames - HALO + f
                    fill(lo, pairs, stacked, f, row + r, every, *strip_block.read(edge, sent, r, rest))
                    fill(lo, pairs, stacked, f, row + r, beside, *strip_block.read_beside(edge, sent, r, rest))

    by_parity(build, received[0::2], received[1::2])

    origin = first_row(strips)
    gain = gains[...]
    position = lax.broadcasted_iota(jnp.int32, (width, 1), 0)
    right = cols + (slab == 0).astype(jnp.int32)
    left = width - (slab == 1).astype(jnp.int32)
    inside = (position < right) | (position >= left)
    for t in range(frames):
        taps = [(f, f - t) for f in range(t, HALO)]
        products = convolve(taps, [plane, middle], columns(taps, lo, pairs, stacked, origin, n_rows_h)) if taps else None
        for r in range(n_rows_h):
            y = own[t, r]
            if taps:
                y = y + join(products, r * width, width)
            h = jnp.where(inside, activate(y, gain), 0.0)
            if strips != 2 and r == 0:
                h = h * jnp.where(strip > 0, 1.0, 0.0)
            if strips != 2 and r == n_rows_h - 1:
                h = h * jnp.where(strip < strips - 1, 1.0, 0.0)
            h = h.astype(jnp.bfloat16)
            fill(h_lo, h_pairs, h_stacked, t, origin + r, slice(0, width), h[:, :LANES], h[:, LANES:])

    for copy in copies:
        copy.wait()
    last = frames - 1
    for t, taps in enumerate(([(last - 1, 0), (last, 1)], [(last, 0)])):
        products = convolve(taps, w2, columns(taps, h_lo, h_pairs, h_stacked, 0, rows))
        for r in range(rows):
            y = join(products, r * width, width)[:cols].astype(jnp.bfloat16)
            partial[t, r] = y[:, :LANES]
            half = r % 2
            partial[t, rows + r // 2, :, half * rest : (half + 1) * rest] = y[:, LANES:]


def second_kernel(frames, rows, cols, h_lo, h_pairs, h_stacked, *refs):
    *w2, out = refs
    width = cols + TILE
    for t in range(frames):
        taps = [(f, f - t + 2) for f in range(max(0, t - 2), t + 1)]
        products = convolve(taps, w2, columns(taps, h_lo, h_pairs, h_stacked, 0, rows))
        for r in range(rows):
            out[t, r] = join(products, r * width, width)[:cols]


def finish_kernel(first, second, own, gains, out_far, out, left):
    frames, rows, cols, channels = out.shape
    rest = channels - LANES
    gain = gains[...]

    def build(partial):
        for t in range(frames):
            for r in range(rows):
                y = own[t, r]
                if t < HALO:
                    half = r % 2
                    high = partial[t, rows + r // 2, :, half * rest : (half + 1) * rest]
                    sent = jnp.concatenate([partial[t, r], high], axis=-1)
                    y = y + sent.astype(jnp.float32)
                out[t, r] = activate(y, gain).astype(jnp.bfloat16)
            copies[t].start()

    copies = [pltpu.make_async_copy(out.at[t], out_far.at[t], left.at[t]) for t in range(frames)]
    by_parity(build, first, second)
    for copy in copies:
        copy.wait()


def call(kernel, name, ins, outs, scratch=(), semaphores=0, flops=0, far=(), far_out=False):
    near, away = pl.BlockSpec(memory_space=pltpu.VMEM), pl.BlockSpec(memory_space=pltpu.HBM)
    in_specs, ins = [near] * len(ins), list(ins)
    for place in far:
        ins[place] = pltpu.with_memory_space_constraint(ins[place], pltpu.HBM)
        in_specs[place] = away
    one = not isinstance(outs, list)
    return pl.pallas_call(
        kernel,
        out_shape=outs,
        in_specs=in_specs,
        out_specs=(away if far_out else near) if one else [near] * len(outs),
        scratch_shapes=[pltpu.VMEM(shape, jnp.bfloat16) for shape in scratch]
        + [pltpu.SemaphoreType.DMA((semaphores,))] * (semaphores > 0),
        compiler_params=pltpu.CompilerParams(vmem_limit_bytes=24 * 1024 * 1024),
        cost_estimate=pl.CostEstimate(flops=flops, bytes_accessed=4 * 1024 * 1024, transcendentals=0),
        name=name,
    )(*ins)


def block_scratch(frames, rows, width):
    return [(frames, rows, width, LANES), (frames, rows + 1, width, LANES), (frames - 1, rows, width, LANES)]


def shards(frames_in, weight_first, scale_first, weight_second, scale_second):
    frames, rows, cols, channels = frames_in.shape
    strips = lax.axis_size("strip")
    width = cols + TILE
    n_rows_h = rows + 1 if strips == 2 else rows + 2
    flops = frames * rows * cols * 27 * channels * channels
    bf16 = functools.partial(jax.ShapeDtypeStruct, dtype=jnp.bfloat16)
    f32 = functools.partial(jax.ShapeDtypeStruct, dtype=jnp.float32)

    plane_shape = bf16(weight_first.shape[1:])
    neighbour = swap(frames_in, "slab")
    own_in, middle, last = call(
        stage_kernel,
        "stage",
        [frames_in, weight_first],
        [bf16(frames_in.shape), plane_shape, plane_shape],
        semaphores=3,
        far=[0, 1],
    )
    edge_shape = bf16(Packed(frames, HALO, cols).shape)
    block, *edges = call(
        functools.partial(pack_kernel, strips),
        "pack",
        [own_in, neighbour],
        [bf16(Packed(HALO, rows, cols).shape)] + [edge_shape] * (1 if strips == 2 else 2),
    )
    ups = [(i, i + 1) for i in range(strips - 1)]
    downs = [(i + 1, i) for i in range(strips - 1)]
    ways = [[(0, 1), (1, 0)]] if strips == 2 else [ups, downs]
    before = forward(block)
    own_edges = [lax.ppermute(edge, "strip", way) for edge, way in zip(edges, ways)]
    for edge, way in zip(edges, ways):
        before += forward(edge, way)

    own, plane = call(
        functools.partial(own_kernel, strips, n_rows_h),
        "first_layer_own",
        [own_in, neighbour, *own_edges, middle, last, weight_first],
        [f32((frames, n_rows_h, width, channels)), plane_shape],
        block_scratch(frames, rows + 2 * HALO, width),
        semaphores=1,
        flops=flops,
        far=[-1],
    )
    h_shapes = [bf16(shape) for shape in block_scratch(frames, rows + 2, width)]
    h_lo, h_pairs, h_stacked, partial, *w2 = call(
        functools.partial(first_kernel, strips, n_rows_h, rows, cols),
        "first_layer",
        [*before, own, plane, middle, scale_first[None], weight_second],
        h_shapes + [bf16((HALO, rows + rows // 2, cols, LANES))] + [plane_shape] * 3,
        block_scratch(HALO, rows + 2 * HALO, width),
        semaphores=3,
        flops=flops,
        far=[-1],
    )
    sent = forward(partial)
    own = call(
        functools.partial(second_kernel, frames, rows, cols),
        "second_layer",
        [h_lo, h_pairs, h_stacked, *w2],
        f32((frames, rows, cols, channels)),
        flops=flops,
    )
    out = bf16(frames_in.shape)
    return call(
        finish_kernel,
        "finish",
        [*sent, own, scale_second[None]],
        out,
        [out.shape],
        semaphores=frames,
        far_out=True,
    )


def solution(mesh):
    return jax.shard_map(
        shards,
        mesh=mesh,
        in_specs=(P(("groups", "frame"), "strip", "slab", None), P(), P(), P(), P()),
        out_specs=P(("groups", "frame"), "strip", "slab", None),
        check_vma=False,
    )
```

```python
import functools

import jax
import jax.numpy as jnp
from jax import lax
from jax.experimental import pallas as pl
from jax.experimental.pallas import tpu as pltpu
from jax.sharding import PartitionSpec as P

LANES = 128
TILE = 16
EPS = 1e-06


HALO = 2


def swap(x, axis):
    return lax.ppermute(x, axis, [(0, 1), (1, 0)])


def forward(x, way=None):
    steps, count = lax.axis_size("frame"), lax.axis_size("strip")
    way = [(i, i) for i in range(count)] if way is None else way
    pairs = [(f * count + i, (f + 1) * count + j) for f in range(steps - 1) for i, j in way]
    return lax.ppermute(x, ("frame", "strip"), pairs)


def if_earlier(build):
    pl.when(lax.axis_index("frame") > 0)(build)


class Packed:
    def __init__(self, frames, rows, cols):
        self.frames, self.rows, self.cols = frames, rows, cols
        self.high = frames * rows * cols
        self.beside = self.high + frames * (rows // 2) * cols
        self.tiles = -(-frames * rows * HALO // TILE)
        self.shape = (self.beside + 2 * self.tiles * TILE, LANES)

    def low_at(self, f, r):
        return slice((f * self.rows + r) * self.cols, (f * self.rows + r + 1) * self.cols)

    def high_at(self, f, r):
        start = self.high + (f * (self.rows // 2) + r // 2) * self.cols
        return slice(start, start + self.cols)

    def spot(self, f, r):
        cell = (f * self.rows + r) * HALO
        return cell // TILE, cell % TILE

    def beside_at(self, tile, high):
        start = self.beside + (2 * tile + high) * TILE
        return slice(start, start + TILE)

    def write(self, out, cells, tile_of):
        slab = lax.axis_index("slab")
        at = lax.broadcasted_iota(jnp.int32, (TILE, 1), 0)
        sums = [None] * self.tiles
        for f in range(self.frames):
            for r in range(self.rows):
                row = cells(f, r)
                out[self.low_at(f, r), :] = row[:, :LANES]
                rest = row.shape[-1] - LANES
                half = slice((r % 2) * rest, (r % 2 + 1) * rest)
                out[self.high_at(f, r), half] = row[:, LANES:]
                tile, place = self.spot(f, r)
                moved = pltpu.roll(tile_of(f, r).astype(jnp.float32), lax.rem(place + HALO * slab, TILE), 0)
                moved = jnp.where((at >= place) & (at < place + HALO), moved, 0.0)
                sums[tile] = moved if sums[tile] is None else sums[tile] + moved
        for tile, cells_beside in enumerate(sums):
            cells_beside = cells_beside.astype(jnp.bfloat16)
            out[self.beside_at(tile, 0), :] = cells_beside[:, :LANES]
            out[self.beside_at(tile, 1), :rest] = cells_beside[:, LANES:]

    def read(self, ref, f, r, rest):
        half = slice((r % 2) * rest, (r % 2 + 1) * rest)
        return ref[self.low_at(f, r), :], ref[self.high_at(f, r), half]

    def read_beside(self, ref, f, r, rest):
        slab = lax.axis_index("slab")
        tile, place = self.spot(f, r)
        parts = []
        for high, lanes in ((0, LANES), (1, rest)):
            cells = ref[self.beside_at(tile, high), :].astype(jnp.float32)
            cells = pltpu.roll(cells, lax.rem(2 * TILE - place - HALO * slab, TILE), 0)
            parts.append(only_beside(cells).astype(jnp.bfloat16)[:, :lanes])
        return parts


def only_beside(tile):
    slab = lax.axis_index("slab")
    at = lax.broadcasted_iota(jnp.int32, tile.shape, 0)
    begin = slab * (TILE - HALO)
    return jnp.where((at >= begin) & (at < begin + HALO), tile, 0.0)


def fill(lo, pairs, stacked, frame, row, cols, low, high):
    rest = high.shape[-1]
    lo[frame, row, cols, :] = low
    pairs[frame, row + 1, cols, :rest] = high
    pairs[frame, row, cols, rest:] = high
    if frame < stacked.shape[0]:
        stacked[frame, row, cols, :rest] = high
    if frame > 0:
        stacked[frame - 1, row, cols, rest:] = high


def columns(taps, lo, pairs, stacked, row, rows):
    def flat(block):
        return block.reshape(-1, LANES)

    pieces = [flat(lo[f, pl.ds(row + b, rows)]) for f, _ in taps for b in range(3)]
    pieces += [flat(pairs[f, pl.ds(row + 1, rows)]) for f, _ in taps]
    for k in range(0, len(taps), 2):
        f = taps[k][0]
        if k + 1 < len(taps):
            pieces.append(flat(stacked[f, pl.ds(row + 2, rows)]))
        else:
            pieces.append(flat(pairs[f, pl.ds(row + 3, rows)]))
    return jnp.concatenate(pieces, axis=-1)


def planes(taps, weight, c):
    pieces = [weight[a][b, c, :LANES, :] for _, a in taps for b in range(3)]
    for _, a in taps:
        pieces += [weight[a][0, c, LANES:, :], weight[a][1, c, LANES:, :]]
    for _, a in taps:
        pieces.append(weight[a][2, c, LANES:, :])
    if len(taps) % 2:
        pieces.append(jnp.zeros_like(weight[a][0, c, LANES:, :]))
    return jnp.concatenate(pieces, axis=0)


def convolve(taps, weight, lefts):
    return [
        jnp.dot(lefts, planes(taps, weight, c), preferred_element_type=jnp.float32)
        for c in range(3)
    ]


def join(products, start, width):
    before, middle, after = [p[start : start + width] for p in products]
    return pltpu.roll(before, 1, 0) + middle + pltpu.roll(after, width - 1, 0)


def activate(y, gains):
    mean_square = jnp.sum(y * y, axis=-1, keepdims=True) * (1.0 / y.shape[-1])
    v = y * lax.rsqrt(mean_square + EPS) * gains
    return v / (1.0 + jnp.exp(-v))


def clear(buffers):
    for buffer in buffers:
        buffer[...] = jnp.zeros_like(buffer)


def facing(strips, rows):
    if strips == 2:
        return [jnp.where(lax.axis_index("strip") == 0, rows - HALO, 0)]
    return [rows - HALO, 0]


def beyond(strips, rows):
    if strips == 2:
        return [jnp.where(lax.axis_index("strip") == 0, rows + HALO, 0)]
    return [0, rows + HALO]


def first_row(strips):
    return 1 - lax.axis_index("strip") if strips == 2 else 0


def beside_of(neighbour, f, r, cols):
    start = pl.multiple_of(lax.axis_index("slab") * (cols - TILE), TILE)
    return neighbour[f, r, pl.ds(start, TILE), :]


def stage_kernel(own_far, weight_far, own, middle, last, arrived):
    copies = [
        pltpu.make_async_copy(own_far, own, arrived.at[0]),
        pltpu.make_async_copy(weight_far.at[2], last, arrived.at[1]),
        pltpu.make_async_copy(weight_far.at[1], middle, arrived.at[2]),
    ]
    for copy in copies:
        copy.start()
    for copy in copies:
        copy.wait()


def pack_kernel(strips, own, neighbour, block, *edges):
    frames, rows, cols, _ = own.shape
    whole = Packed(HALO, rows, cols)
    skip = frames - HALO
    whole.write(block, lambda f, r: own[f + skip, r], lambda f, r: beside_of(neighbour, f + skip, r, cols))
    for start, edge in zip(facing(strips, rows), edges):
        Packed(frames, HALO, cols).write(
            edge, lambda f, r: own[f, start + r], lambda f, r: beside_of(neighbour, f, start + r, cols)
        )


def own_kernel(strips, n_rows_h, *refs):
    own, neighbour, *edges, middle, last, weight_far, out, plane, lo, pairs, stacked, arrived = refs
    frames, rows, cols, channels = own.shape
    copy = pltpu.make_async_copy(weight_far.at[0], plane, arrived.at[0])
    copy.start()
    if frames > 2:
        copy.wait()
    width, rest = cols + TILE, channels - LANES
    every, beside = slice(0, cols), slice(cols, width)
    clear((lo, pairs, stacked))
    strip_block = Packed(frames, HALO, cols)
    for f in range(frames):
        for r in range(rows):
            cells = own[f, r]
            fill(lo, pairs, stacked, f, r + HALO, every, cells[:, :LANES], cells[:, LANES:])
            tile = only_beside(beside_of(neighbour, f, r, cols).astype(jnp.float32)).astype(jnp.bfloat16)
            fill(lo, pairs, stacked, f, r + HALO, beside, tile[:, :LANES], tile[:, LANES:])
        for edge, row in zip(edges, beyond(strips, rows)):
            for r in range(HALO):
                fill(lo, pairs, stacked, f, row + r, every, *strip_block.read(edge, f, r, rest))
                fill(lo, pairs, stacked, f, row + r, beside, *strip_block.read_beside(edge, f, r, rest))
    for t in range(frames):
        taps = [(f, f - t + 2) for f in range(max(0, t - 2), t + 1)]
        products = convolve(taps, [plane, middle, last], columns(taps, lo, pairs, stacked, first_row(strips), n_rows_h))
        for r in range(n_rows_h):
            out[t, r] = join(products, r * width, width)
    if frames <= 2:
        copy.wait()


def first_kernel(strips, n_rows_h, rows, cols, *refs):
    *refs, lo, pairs, stacked, arrived = refs
    *refs, h_lo, h_pairs, h_stacked, partial, w2_first, w2_middle, w2_last = refs
    block, *edges, own, plane, middle, gains, w2_far = refs
    w2 = [w2_first, w2_middle, w2_last]
    copies = [pltpu.make_async_copy(w2_far.at[a], w2[a], arrived.at[a]) for a in range(3)]
    for copy in copies:
        copy.start()
    frames, channels = own.shape[0], own.shape[-1]
    width, rest = cols + TILE, channels - LANES
    every, beside = slice(0, cols), slice(cols, width)
    strip, slab = lax.axis_index("strip"), lax.axis_index("slab")
    clear((lo, pairs, stacked, h_lo, h_pairs, h_stacked))
    whole, strip_block = Packed(HALO, rows, cols), Packed(frames, HALO, cols)

    @if_earlier
    def build():
        for f in range(HALO):
            for r in range(rows):
                fill(lo, pairs, stacked, f, r + HALO, every, *whole.read(block, f, r, rest))
                fill(lo, pairs, stacked, f, r + HALO, beside, *whole.read_beside(block, f, r, rest))
            for edge, row in zip(edges, beyond(strips, rows)):
                for r in range(HALO):
                    sent = frames - HALO + f
                    fill(lo, pairs, stacked, f, row + r, every, *strip_block.read(edge, sent, r, rest))
                    fill(lo, pairs, stacked, f, row + r, beside, *strip_block.read_beside(edge, sent, r, rest))


    origin = first_row(strips)
    gain = gains[...]
    position = lax.broadcasted_iota(jnp.int32, (width, 1), 0)
    right = cols + (slab == 0).astype(jnp.int32)
    left = width - (slab == 1).astype(jnp.int32)
    inside = (position < right) | (position >= left)
    for t in range(frames):
        taps = [(f, f - t) for f in range(t, HALO)]
        products = convolve(taps, [plane, middle], columns(taps, lo, pairs, stacked, origin, n_rows_h)) if taps else None
        for r in range(n_rows_h):
            y = own[t, r]
            if taps:
                y = y + join(products, r * width, width)
            h = jnp.where(inside, activate(y, gain), 0.0)
            if strips != 2 and r == 0:
                h = h * jnp.where(strip > 0, 1.0, 0.0)
            if strips != 2 and r == n_rows_h - 1:
                h = h * jnp.where(strip < strips - 1, 1.0, 0.0)
            h = h.astype(jnp.bfloat16)
            fill(h_lo, h_pairs, h_stacked, t, origin + r, slice(0, width), h[:, :LANES], h[:, LANES:])

    for copy in copies:
        copy.wait()
    last = frames - 1
    for t, taps in enumerate(([(last - 1, 0), (last, 1)], [(last, 0)])):
        products = convolve(taps, w2, columns(taps, h_lo, h_pairs, h_stacked, 0, rows))
        for r in range(rows):
            y = join(products, r * width, width)[:cols].astype(jnp.bfloat16)
            partial[t, r] = y[:, :LANES]
            half = r % 2
            partial[t, rows + r // 2, :, half * rest : (half + 1) * rest] = y[:, LANES:]


def second_kernel(frames, rows, cols, h_lo, h_pairs, h_stacked, *refs):
    *w2, out = refs
    width = cols + TILE
    for t in range(frames):
        taps = [(f, f - t + 2) for f in range(max(0, t - 2), t + 1)]
        products = convolve(taps, w2, columns(taps, h_lo, h_pairs, h_stacked, 0, rows))
        for r in range(rows):
            out[t, r] = join(products, r * width, width)[:cols]


def finish_kernel(partial, own, gains, out_far, out, left):
    frames, rows, cols, channels = out.shape
    rest = channels - LANES
    gain = gains[...]

    copies = [pltpu.make_async_copy(out.at[t], out_far.at[t], left.at[t]) for t in range(frames)]
    for t in range(frames):
        for r in range(rows):
            y = own[t, r]
            if t < HALO:
                half = r % 2
                high = partial[t, rows + r // 2, :, half * rest : (half + 1) * rest]
                sent = jnp.concatenate([partial[t, r], high], axis=-1)
                y = y + sent.astype(jnp.float32)
            out[t, r] = activate(y, gain).astype(jnp.bfloat16)
        copies[t].start()
    for copy in copies:
        copy.wait()


def call(kernel, name, ins, outs, scratch=(), semaphores=0, flops=0, far=(), far_out=False):
    near, away = pl.BlockSpec(memory_space=pltpu.VMEM), pl.BlockSpec(memory_space=pltpu.HBM)
    in_specs, ins = [near] * len(ins), list(ins)
    for place in far:
        ins[place] = pltpu.with_memory_space_constraint(ins[place], pltpu.HBM)
        in_specs[place] = away
    one = not isinstance(outs, list)
    return pl.pallas_call(
        kernel,
        out_shape=outs,
        in_specs=in_specs,
        out_specs=(away if far_out else near) if one else [near] * len(outs),
        scratch_shapes=[pltpu.VMEM(shape, jnp.bfloat16) for shape in scratch]
        + [pltpu.SemaphoreType.DMA((semaphores,))] * (semaphores > 0),
        compiler_params=pltpu.CompilerParams(vmem_limit_bytes=24 * 1024 * 1024),
        cost_estimate=pl.CostEstimate(flops=flops, bytes_accessed=4 * 1024 * 1024, transcendentals=0),
        name=name,
    )(*ins)


def block_scratch(frames, rows, width):
    return [(frames, rows, width, LANES), (frames, rows + 1, width, LANES), (frames - 1, rows, width, LANES)]


def shards(frames_in, weight_first, scale_first, weight_second, scale_second):
    frames, rows, cols, channels = frames_in.shape
    strips = lax.axis_size("strip")
    width = cols + TILE
    n_rows_h = rows + 1 if strips == 2 else rows + 2
    flops = frames * rows * cols * 27 * channels * channels
    bf16 = functools.partial(jax.ShapeDtypeStruct, dtype=jnp.bfloat16)
    f32 = functools.partial(jax.ShapeDtypeStruct, dtype=jnp.float32)

    plane_shape = bf16(weight_first.shape[1:])
    neighbour = swap(frames_in, "slab")
    own_in, middle, last = call(
        stage_kernel,
        "stage",
        [frames_in, weight_first],
        [bf16(frames_in.shape), plane_shape, plane_shape],
        semaphores=3,
        far=[0, 1],
    )
    edge_shape = bf16(Packed(frames, HALO, cols).shape)
    block, *edges = call(
        functools.partial(pack_kernel, strips),
        "pack",
        [own_in, neighbour],
        [bf16(Packed(HALO, rows, cols).shape)] + [edge_shape] * (1 if strips == 2 else 2),
    )
    ups = [(i, i + 1) for i in range(strips - 1)]
    downs = [(i + 1, i) for i in range(strips - 1)]
    ways = [[(0, 1), (1, 0)]] if strips == 2 else [ups, downs]
    before = [forward(block)]
    own_edges = [lax.ppermute(edge, "strip", way) for edge, way in zip(edges, ways)]
    for edge, way in zip(edges, ways):
        before.append(forward(edge, way))

    own, plane = call(
        functools.partial(own_kernel, strips, n_rows_h),
        "first_layer_own",
        [own_in, neighbour, *own_edges, middle, last, weight_first],
        [f32((frames, n_rows_h, width, channels)), plane_shape],
        block_scratch(frames, rows + 2 * HALO, width),
        semaphores=1,
        flops=flops,
        far=[-1],
    )
    h_shapes = [bf16(shape) for shape in block_scratch(frames, rows + 2, width)]
    h_lo, h_pairs, h_stacked, partial, *w2 = call(
        functools.partial(first_kernel, strips, n_rows_h, rows, cols),
        "first_layer",
        [*before, own, plane, middle, scale_first[None], weight_second],
        h_shapes + [bf16((HALO, rows + rows // 2, cols, LANES))] + [plane_shape] * 3,
        block_scratch(HALO, rows + 2 * HALO, width),
        semaphores=3,
        flops=flops,
        far=[-1],
    )
    sent = forward(partial)
    own = call(
        functools.partial(second_kernel, frames, rows, cols),
        "second_layer",
        [h_lo, h_pairs, h_stacked, *w2],
        f32((frames, rows, cols, channels)),
        flops=flops,
    )
    out = bf16(frames_in.shape)
    return call(
        finish_kernel,
        "finish",
        [sent, own, scale_second[None]],
        out,
        [out.shape],
        semaphores=frames,
        far_out=True,
    )


def solution(mesh):
    return jax.shard_map(
        shards,
        mesh=mesh,
        in_specs=(P(("groups", "frame"), "strip", "slab", None), P(), P(), P(), P()),
        out_specs=P(("groups", "frame"), "strip", "slab", None),
        check_vma=False,
    )
```

```python
import functools

import jax
import jax.numpy as jnp
from jax import lax
from jax.experimental import pallas as pl
from jax.experimental.pallas import tpu as pltpu
from jax.sharding import PartitionSpec as P

LANES = 128
TILE = 16
EPS = 1e-06


HALO = 2


def swap(x, axis):
    return lax.ppermute(x, axis, [(0, 1), (1, 0)])


def forward(x):
    steps = lax.axis_size("frame")
    return lax.ppermute(x, "frame", [(i, i + 1) for i in range(steps - 1)])


def if_earlier(build):
    pl.when(lax.axis_index("frame") > 0)(build)


class Packed:
    def __init__(self, frames, rows, cols):
        self.frames, self.rows, self.cols = frames, rows, cols
        self.high = frames * rows * cols
        self.beside = self.high + frames * (rows // 2) * cols
        self.tiles = -(-frames * rows * HALO // TILE)
        self.shape = (self.beside + 2 * self.tiles * TILE, LANES)

    def low_at(self, f, r):
        return slice((f * self.rows + r) * self.cols, (f * self.rows + r + 1) * self.cols)

    def high_at(self, f, r):
        start = self.high + (f * (self.rows // 2) + r // 2) * self.cols
        return slice(start, start + self.cols)

    def spot(self, f, r):
        cell = (f * self.rows + r) * HALO
        return cell // TILE, cell % TILE

    def beside_at(self, tile, high):
        start = self.beside + (2 * tile + high) * TILE
        return slice(start, start + TILE)

    def write(self, out, cells, tile_of):
        slab = lax.axis_index("slab")
        at = lax.broadcasted_iota(jnp.int32, (TILE, 1), 0)
        sums = [None] * self.tiles
        for f in range(self.frames):
            for r in range(self.rows):
                row = cells(f, r)
                out[self.low_at(f, r), :] = row[:, :LANES]
                rest = row.shape[-1] - LANES
                half = slice((r % 2) * rest, (r % 2 + 1) * rest)
                out[self.high_at(f, r), half] = row[:, LANES:]
                tile, place = self.spot(f, r)
                moved = pltpu.roll(tile_of(f, r).astype(jnp.float32), lax.rem(place + HALO * slab, TILE), 0)
                moved = jnp.where((at >= place) & (at < place + HALO), moved, 0.0)
                sums[tile] = moved if sums[tile] is None else sums[tile] + moved
        for tile, cells_beside in enumerate(sums):
            cells_beside = cells_beside.astype(jnp.bfloat16)
            out[self.beside_at(tile, 0), :] = cells_beside[:, :LANES]
            out[self.beside_at(tile, 1), :rest] = cells_beside[:, LANES:]

    def read(self, ref, f, r, rest):
        half = slice((r % 2) * rest, (r % 2 + 1) * rest)
        return ref[self.low_at(f, r), :], ref[self.high_at(f, r), half]

    def read_beside(self, ref, f, r, rest):
        return beside_from(ref, self.beside, (f * self.rows + r) * HALO, rest)


def beside_from(ref, start, cell, rest):
    slab = lax.axis_index("slab")
    parts = []
    for high, lanes in ((0, LANES), (1, rest)):
        at = start + (2 * (cell // TILE) + high) * TILE
        cells = ref[pl.ds(pl.multiple_of(at, TILE), TILE), :].astype(jnp.float32)
        cells = pltpu.roll(cells, lax.rem(2 * TILE - cell % TILE - HALO * slab, TILE), 0)
        parts.append(only_beside(cells).astype(jnp.bfloat16)[:, :lanes])
    return parts


def only_beside(tile):
    slab = lax.axis_index("slab")
    at = lax.broadcasted_iota(jnp.int32, tile.shape, 0)
    begin = slab * (TILE - HALO)
    return jnp.where((at >= begin) & (at < begin + HALO), tile, 0.0)


def fill(lo, pairs, stacked, frame, row, cols, low, high):
    rest = high.shape[-1]
    lo[frame, row, cols, :] = low
    pairs[frame, row + 1, cols, :rest] = high
    pairs[frame, row, cols, rest:] = high
    if frame < stacked.shape[0]:
        stacked[frame, row, cols, :rest] = high
    if frame > 0:
        stacked[frame - 1, row, cols, rest:] = high


def columns(taps, lo, pairs, stacked, row, rows):
    def flat(block):
        return block.reshape(-1, LANES)

    pieces = [flat(lo[f, pl.ds(row + b, rows)]) for f, _ in taps for b in range(3)]
    pieces += [flat(pairs[f, pl.ds(row + 1, rows)]) for f, _ in taps]
    for k in range(0, len(taps), 2):
        f = taps[k][0]
        if k + 1 < len(taps):
            pieces.append(flat(stacked[f, pl.ds(row + 2, rows)]))
        else:
            pieces.append(flat(pairs[f, pl.ds(row + 3, rows)]))
    return jnp.concatenate(pieces, axis=-1)


def planes(taps, weight, c):
    pieces = [weight[a][b, c, :LANES, :] for _, a in taps for b in range(3)]
    for _, a in taps:
        pieces += [weight[a][0, c, LANES:, :], weight[a][1, c, LANES:, :]]
    for _, a in taps:
        pieces.append(weight[a][2, c, LANES:, :])
    if len(taps) % 2:
        pieces.append(jnp.zeros_like(weight[a][0, c, LANES:, :]))
    return jnp.concatenate(pieces, axis=0)


def convolve(taps, weight, lefts):
    return [
        jnp.dot(lefts, planes(taps, weight, c), preferred_element_type=jnp.float32)
        for c in range(3)
    ]


def join(products, start, width):
    before, middle, after = [p[start : start + width] for p in products]
    return pltpu.roll(before, 1, 0) + middle + pltpu.roll(after, width - 1, 0)


def activate(y, gains):
    mean_square = jnp.sum(y * y, axis=-1, keepdims=True) * (1.0 / y.shape[-1])
    v = y * lax.rsqrt(mean_square + EPS) * gains
    return v / (1.0 + jnp.exp(-v))


def clear(buffers):
    for buffer in buffers:
        buffer[...] = jnp.zeros_like(buffer)


def facing(strips, rows):
    if strips == 2:
        return [jnp.where(lax.axis_index("strip") == 0, rows - HALO, 0)]
    return [rows - HALO, 0]


def at_top(strips):
    return [lax.axis_index("strip")] if strips == 2 else [1, 0]


def safe_rows(strips, rows):
    return (1 + lax.axis_index("strip"), rows - 1) if strips == 2 else (2, rows - 2)


def beside_of(neighbour, f, r, cols):
    start = pl.multiple_of(lax.axis_index("slab") * (cols - TILE), TILE)
    return neighbour[f, r, pl.ds(start, TILE), :]


def stage_kernel(own_far, weight_far, own, middle, last, arrived):
    copies = [
        pltpu.make_async_copy(own_far, own, arrived.at[0]),
        pltpu.make_async_copy(weight_far.at[2], last, arrived.at[1]),
        pltpu.make_async_copy(weight_far.at[1], middle, arrived.at[2]),
    ]
    for copy in copies:
        copy.start()
    for copy in copies:
        copy.wait()


def pack_kernel(strips, own, neighbour, block, *edges):
    frames, rows, cols, _ = own.shape
    whole = Packed(HALO, rows, cols)
    skip = frames - HALO
    whole.write(block, lambda f, r: own[f + skip, r], lambda f, r: beside_of(neighbour, f + skip, r, cols))
    for start, edge in zip(facing(strips, rows), edges):
        Packed(frames, HALO, cols).write(
            edge, lambda f, r: own[f, start + r], lambda f, r: beside_of(neighbour, f, start + r, cols)
        )


def own_beside(neighbour, f, r, cols):
    tile = only_beside(beside_of(neighbour, f, r, cols).astype(jnp.float32)).astype(jnp.bfloat16)
    return tile[:, :LANES], tile[:, LANES:]


def window(buffers, frames, top, rows, cols, own, halo):
    every, beside = slice(0, cols), slice(cols, cols + TILE)
    for f in range(frames):
        for j in range(HALO):
            for cells, row in ((own(f, (1 - top) * (rows - HALO) + j), HALO * top + j), (halo(f, j), HALO * (1 - top) + j)):
                fill(*buffers, f, row, every, *cells[:2])
                fill(*buffers, f, row, beside, *cells[2:])


def safe_kernel(strips, own, neighbour, middle, last, weight_far, out, plane, lo, pairs, stacked, arrived):
    frames, rows, cols, channels = own.shape
    width = cols + TILE
    copy = pltpu.make_async_copy(weight_far.at[0], plane, arrived.at[0])
    copy.start()
    if frames > 2:
        copy.wait()
    clear((lo, pairs, stacked))
    for f in range(frames):
        for r in range(rows):
            cells = own[f, r]
            fill(lo, pairs, stacked, f, r + HALO, slice(0, cols), cells[:, :LANES], cells[:, LANES:])
            fill(lo, pairs, stacked, f, r + HALO, slice(cols, width), *own_beside(neighbour, f, r, cols))
    start, count = safe_rows(strips, rows)
    for t in range(frames):
        taps = own_taps(t)
        products = convolve(taps, [plane, middle, last], columns(taps, lo, pairs, stacked, start, count))
        for r in range(count):
            out[t, r] = join(products, r * width, width)
    if frames <= 2:
        copy.wait()


def own_taps(t):
    return [(f, f - t + 2) for f in range(max(0, t - 2), t + 1)]


def earlier_taps(t):
    return [(f, f - t) for f in range(t, HALO)]


def hidden_row(y, gain, cols):
    width, slab = y.shape[0], lax.axis_index("slab")
    position = lax.broadcasted_iota(jnp.int32, (width, 1), 0)
    right = cols + (slab == 0).astype(jnp.int32)
    left = width - (slab == 1).astype(jnp.int32)
    return jnp.where((position < right) | (position >= left), activate(y, gain), 0.0)


def middle_kernel(strips, rows, cols, *refs):
    *refs, lo, pairs, stacked, near_lo, near_pairs, near_stacked, arrived = refs
    *refs, h_lo, h_pairs, h_stacked, edge_sums, w2_first, w2_middle, w2_last = refs
    own, neighbour, *edges, block, sums, plane, middle, last, gains, w2_far = refs
    frames, channels = own.shape[0], own.shape[-1]
    width, rest = cols + TILE, channels - LANES
    w2 = [w2_first, w2_middle, w2_last]
    copies = [pltpu.make_async_copy(w2_far.at[a], w2[a], arrived.at[a]) for a in range(3)]
    for copy in copies:
        copy.start()
    clear((lo, pairs, stacked, h_lo, h_pairs, h_stacked, near_pairs))
    whole, strip_block = Packed(HALO, rows, cols), Packed(frames, HALO, cols)

    @if_earlier
    def build():
        for f in range(HALO):
            for r in range(rows):
                fill(lo, pairs, stacked, f, r + HALO, slice(0, cols), *whole.read(block, f, r, rest))
                fill(lo, pairs, stacked, f, r + HALO, slice(cols, width), *whole.read_beside(block, f, r, rest))

    gain = gains[...]
    start, count = safe_rows(strips, rows)
    for t in range(frames):
        taps = earlier_taps(t)
        products = convolve(taps, [plane, middle], columns(taps, lo, pairs, stacked, start, count)) if taps else None
        for r in range(count):
            y = sums[t, r]
            if taps:
                y = y + join(products, r * width, width)
            h = hidden_row(y, gain, cols).astype(jnp.bfloat16)
            fill(h_lo, h_pairs, h_stacked, t, start + r, slice(0, width), h[:, :LANES], h[:, LANES:])

    near = (near_lo, near_pairs, near_stacked)
    for group, (edge, top) in enumerate(zip(edges, at_top(strips))):

        def own_row(f, r):
            cells = own[f, r]
            return cells[:, :LANES], cells[:, LANES:], *own_beside(neighbour, f, r, cols)

        def halo_row(f, j):
            return *strip_block.read(edge, f, j, rest), *strip_block.read_beside(edge, f, j, rest)

        window(near, frames, top, rows, cols, own_row, halo_row)
        for t in range(frames):
            taps = own_taps(t)
            products = convolve(taps, [plane, middle, last], columns(taps, *near, 0, HALO))
            for r in range(HALO):
                edge_sums[group, t, r] = join(products, r * width, width)
    for copy in copies:
        copy.wait()


def pass_kernel(strips, rows, cols, block, _, *edges):
    whole = Packed(HALO, rows, cols)
    for start, edge in zip(facing(strips, rows), edges):
        for f in range(HALO):
            low = pl.multiple_of((f * rows + start) * cols, TILE)
            edge[f * HALO * cols : (f + 1) * HALO * cols, :] = block[pl.ds(low, HALO * cols), :]
            high = pl.multiple_of(whole.high + (f * (rows // 2) + start // 2) * cols, TILE)
            at = HALO * HALO * cols + f * cols
            edge[at : at + cols, :] = block[pl.ds(high, cols), :]
        at = HALO * HALO * cols + HALO * cols
        edge[at:, :] = block[whole.beside :, :]


def edge_kernel(strips, rows, cols, *refs):
    *refs, near_lo, near_pairs, near_stacked = refs
    *refs, h_lo, h_pairs, h_stacked, partial = refs
    *edges, block, edge_sums, safe_lo, safe_pairs, safe_stacked, plane, middle, gains, w2_first, w2_middle = refs
    frames, channels = edge_sums.shape[1], edge_sums.shape[-1]
    width, rest = cols + TILE, channels - LANES
    strip = lax.axis_index("strip")
    whole, strip_block = Packed(HALO, rows, cols), Packed(HALO, HALO, cols)
    near = (near_lo, near_pairs, near_stacked)
    clear(near)
    for target, source in ((h_lo, safe_lo), (h_pairs, safe_pairs), (h_stacked, safe_stacked)):
        target[...] = source[...]
    gain = gains[...]
    for group, (edge, top) in enumerate(zip(edges, at_top(strips))):

        def own_row(f, r):
            low = pl.multiple_of((f * rows + r) * cols, TILE)
            high = pl.multiple_of(whole.high + (f * (rows // 2) + r // 2) * cols, TILE)
            pair = block[pl.ds(high, cols), :]
            return block[pl.ds(low, cols), :], pair, *beside_from(block, whole.beside, (f * rows + r) * HALO, rest)

        def halo_row(f, j):
            theirs = top * (rows - HALO) + j
            cell = (f * rows + theirs) * HALO
            return *strip_block.read(edge, f, j, rest), *beside_from(edge, strip_block.beside, cell, rest)

        def own_half(f, r, j):
            low, pair, *tile = own_row(f, r)
            return low, pair[:, (j % 2) * rest : (j % 2 + 1) * rest], *tile

        @if_earlier
        def build():
            every, beside = slice(0, cols), slice(cols, width)
            for f in range(HALO):
                for j in range(HALO):
                    mine = own_half(f, (1 - top) * (rows - HALO) + j, j)
                    for cells, row in ((mine, HALO * top + j), (halo_row(f, j), HALO * (1 - top) + j)):
                        fill(*near, f, row, every, *cells[:2])
                        fill(*near, f, row, beside, *cells[2:])

        for t in range(frames):
            taps = earlier_taps(t)
            products = convolve(taps, [plane, middle], columns(taps, *near, 0, HALO)) if taps else None
            for r in range(HALO):
                y = edge_sums[group, t, r]
                if taps:
                    y = y + join(products, r * width, width)
                h = hidden_row(y, gain, cols)
                if strips != 2 and r == 1 - top:
                    h = h * jnp.where(strip == (0 if top else strips - 1), 0.0, 1.0)
                h = h.astype(jnp.bfloat16)
                row = (1 - top) * rows + r
                fill(h_lo, h_pairs, h_stacked, t, row, slice(0, width), h[:, :LANES], h[:, LANES:])

    last = frames - 1
    for t, taps in enumerate(([(last - 1, 0), (last, 1)], [(last, 0)])):
        products = convolve(taps, [w2_first, w2_middle], columns(taps, h_lo, h_pairs, h_stacked, 0, rows))
        for r in range(rows):
            y = join(products, r * width, width)[:cols].astype(jnp.bfloat16)
            partial[t, r] = y[:, :LANES]
            half = r % 2
            partial[t, rows + r // 2, :, half * rest : (half + 1) * rest] = y[:, LANES:]


def second_kernel(frames, rows, cols, h_lo, h_pairs, h_stacked, *refs):
    *w2, out = refs
    width = cols + TILE
    for t in range(frames):
        taps = [(f, f - t + 2) for f in range(max(0, t - 2), t + 1)]
        products = convolve(taps, w2, columns(taps, h_lo, h_pairs, h_stacked, 0, rows))
        for r in range(rows):
            out[t, r] = join(products, r * width, width)[:cols]


def finish_kernel(partial, own, gains, out_far, out, left):
    frames, rows, cols, channels = out.shape
    rest = channels - LANES
    gain = gains[...]

    copies = [pltpu.make_async_copy(out.at[t], out_far.at[t], left.at[t]) for t in range(frames)]
    for t in range(frames):
        for r in range(rows):
            y = own[t, r]
            if t < HALO:
                half = r % 2
                high = partial[t, rows + r // 2, :, half * rest : (half + 1) * rest]
                sent = jnp.concatenate([partial[t, r], high], axis=-1)
                y = y + sent.astype(jnp.float32)
            out[t, r] = activate(y, gain).astype(jnp.bfloat16)
        copies[t].start()
    for copy in copies:
        copy.wait()


def call(kernel, name, ins, outs, scratch=(), semaphores=0, flops=0, far=(), far_out=False):
    near, away = pl.BlockSpec(memory_space=pltpu.VMEM), pl.BlockSpec(memory_space=pltpu.HBM)
    in_specs, ins = [near] * len(ins), list(ins)
    for place in far:
        ins[place] = pltpu.with_memory_space_constraint(ins[place], pltpu.HBM)
        in_specs[place] = away
    one = not isinstance(outs, list)
    return pl.pallas_call(
        kernel,
        out_shape=outs,
        in_specs=in_specs,
        out_specs=(away if far_out else near) if one else [near] * len(outs),
        scratch_shapes=[pltpu.VMEM(shape, jnp.bfloat16) for shape in scratch]
        + [pltpu.SemaphoreType.DMA((semaphores,))] * (semaphores > 0),
        compiler_params=pltpu.CompilerParams(vmem_limit_bytes=24 * 1024 * 1024),
        cost_estimate=pl.CostEstimate(flops=flops, bytes_accessed=4 * 1024 * 1024, transcendentals=0),
        name=name,
    )(*ins)


def block_scratch(frames, rows, width):
    return [(frames, rows, width, LANES), (frames, rows + 1, width, LANES), (frames - 1, rows, width, LANES)]


def shards(frames_in, weight_first, scale_first, weight_second, scale_second):
    frames, rows, cols, channels = frames_in.shape
    strips = lax.axis_size("strip")
    width = cols + TILE
    flops = frames * rows * cols * 27 * channels * channels
    bf16 = functools.partial(jax.ShapeDtypeStruct, dtype=jnp.bfloat16)
    f32 = functools.partial(jax.ShapeDtypeStruct, dtype=jnp.float32)

    plane_shape = bf16(weight_first.shape[1:])
    neighbour = swap(frames_in, "slab")
    own_in, middle, last = call(
        stage_kernel,
        "stage",
        [frames_in, weight_first],
        [bf16(frames_in.shape), plane_shape, plane_shape],
        semaphores=3,
        far=[0, 1],
    )
    edge_shape = bf16(Packed(frames, HALO, cols).shape)
    block, *edges = call(
        functools.partial(pack_kernel, strips),
        "pack",
        [own_in, neighbour],
        [bf16(Packed(HALO, rows, cols).shape)] + [edge_shape] * (1 if strips == 2 else 2),
    )
    ups = [(i, i + 1) for i in range(strips - 1)]
    downs = [(i + 1, i) for i in range(strips - 1)]
    ways = [[(0, 1), (1, 0)]] if strips == 2 else [ups, downs]
    before = forward(block)
    own_edges = [lax.ppermute(edge, "strip", way) for edge, way in zip(edges, ways)]
    sums, plane = call(
        functools.partial(safe_kernel, strips),
        "own_safe_rows",
        [own_in, neighbour, middle, last, weight_first],
        [f32((frames, safe_rows(strips, rows)[1], width, channels)), plane_shape],
        block_scratch(frames, rows + 2 * HALO, width),
        semaphores=1,
        flops=flops // 2,
        far=[-1],
    )
    passed = call(
        functools.partial(pass_kernel, strips, rows, cols),
        "pass_on",
        [before, sums],
        [bf16((Packed(HALO, HALO, cols).beside + 2 * TILE * Packed(HALO, rows, cols).tiles, LANES))] * len(ways),
    )
    before_edges = [lax.ppermute(edge, "strip", way) for edge, way in zip(passed, ways)]
    h_shapes = [bf16(shape) for shape in block_scratch(frames, rows + 2, width)]
    gain_first = scale_first[None]
    *safe, edge_sums, w2_first, w2_middle, w2_last = call(
        functools.partial(middle_kernel, strips, rows, cols),
        "safe_rows",
        [own_in, neighbour, *own_edges, before, sums, plane, middle, last, gain_first, weight_second],
        h_shapes + [f32((len(ways), frames, HALO, width, channels))] + [plane_shape] * 3,
        block_scratch(HALO, rows + 2 * HALO, width) + block_scratch(frames, 2 * HALO, width),
        semaphores=3,
        flops=flops // 2,
        far=[-1],
    )
    h_lo, h_pairs, h_stacked, partial = call(
        functools.partial(edge_kernel, strips, rows, cols),
        "edge_rows",
        [*before_edges, before, edge_sums, *safe, plane, middle, gain_first, w2_first, w2_middle],
        h_shapes + [bf16((HALO, rows + rows // 2, cols, LANES))],
        block_scratch(HALO, 2 * HALO, width),
        flops=flops,
    )
    w2 = [w2_first, w2_middle, w2_last]
    sent = forward(partial)
    own = call(
        functools.partial(second_kernel, frames, rows, cols),
        "second_layer",
        [h_lo, h_pairs, h_stacked, *w2],
        f32((frames, rows, cols, channels)),
        flops=flops,
    )
    out = bf16(frames_in.shape)
    return call(
        finish_kernel,
        "finish",
        [sent, own, scale_second[None]],
        out,
        [out.shape],
        semaphores=frames,
        far_out=True,
    )


def solution(mesh):
    return jax.shard_map(
        shards,
        mesh=mesh,
        in_specs=(P(("groups", "frame"), "strip", "slab", None), P(), P(), P(), P()),
        out_specs=P(("groups", "frame"), "strip", "slab", None),
        check_vma=False,
    )
```

```python
import functools

import jax
import jax.numpy as jnp
from jax import lax
from jax.experimental import pallas as pl
from jax.experimental.pallas import tpu as pltpu
from jax.sharding import PartitionSpec as P

LANES = 128
TILE = 16
EPS = 1e-06


HALO = 2


def swap(x, axis):
    return lax.ppermute(x, axis, [(0, 1), (1, 0)])


def forward(x, way=None):
    steps, count = lax.axis_size("frame"), lax.axis_size("strip")
    way = [(i, i) for i in range(count)] if way is None else way
    pairs = [(f * count + i, (f + 1) * count + j) for f in range(steps - 1) for i, j in way]
    return lax.ppermute(x, ("frame", "strip"), pairs)


def if_earlier(build):
    pl.when(lax.axis_index("frame") > 0)(build)


class Packed:
    def __init__(self, frames, rows, cols):
        self.frames, self.rows, self.cols = frames, rows, cols
        self.high = frames * rows * cols
        self.beside = self.high + frames * (rows // 2) * cols
        self.tiles = -(-frames * rows * HALO // TILE)
        self.shape = (self.beside + 2 * self.tiles * TILE, LANES)

    def low_at(self, f, r):
        return slice((f * self.rows + r) * self.cols, (f * self.rows + r + 1) * self.cols)

    def high_at(self, f, r):
        start = self.high + (f * (self.rows // 2) + r // 2) * self.cols
        return slice(start, start + self.cols)

    def spot(self, f, r):
        cell = (f * self.rows + r) * HALO
        return cell // TILE, cell % TILE

    def beside_at(self, tile, high):
        start = self.beside + (2 * tile + high) * TILE
        return slice(start, start + TILE)

    def write(self, out, cells, tile_of):
        slab = lax.axis_index("slab")
        at = lax.broadcasted_iota(jnp.int32, (TILE, 1), 0)
        sums = [None] * self.tiles
        for f in range(self.frames):
            for r in range(self.rows):
                row = cells(f, r)
                out[self.low_at(f, r), :] = row[:, :LANES]
                rest = row.shape[-1] - LANES
                half = slice((r % 2) * rest, (r % 2 + 1) * rest)
                out[self.high_at(f, r), half] = row[:, LANES:]
                tile, place = self.spot(f, r)
                moved = pltpu.roll(tile_of(f, r).astype(jnp.float32), lax.rem(place + HALO * slab, TILE), 0)
                moved = jnp.where((at >= place) & (at < place + HALO), moved, 0.0)
                sums[tile] = moved if sums[tile] is None else sums[tile] + moved
        for tile, cells_beside in enumerate(sums):
            cells_beside = cells_beside.astype(jnp.bfloat16)
            out[self.beside_at(tile, 0), :] = cells_beside[:, :LANES]
            out[self.beside_at(tile, 1), :rest] = cells_beside[:, LANES:]

    def read(self, ref, f, r, rest):
        half = slice((r % 2) * rest, (r % 2 + 1) * rest)
        return ref[self.low_at(f, r), :], ref[self.high_at(f, r), half]

    def read_beside(self, ref, f, r, rest):
        return beside_from(ref, self.beside, (f * self.rows + r) * HALO, rest)


def beside_from(ref, start, cell, rest):
    slab = lax.axis_index("slab")
    parts = []
    for high, lanes in ((0, LANES), (1, rest)):
        at = start + (2 * (cell // TILE) + high) * TILE
        cells = ref[pl.ds(pl.multiple_of(at, TILE), TILE), :].astype(jnp.float32)
        cells = pltpu.roll(cells, lax.rem(2 * TILE - cell % TILE - HALO * slab, TILE), 0)
        parts.append(only_beside(cells).astype(jnp.bfloat16)[:, :lanes])
    return parts


def only_beside(tile):
    slab = lax.axis_index("slab")
    at = lax.broadcasted_iota(jnp.int32, tile.shape, 0)
    begin = slab * (TILE - HALO)
    return jnp.where((at >= begin) & (at < begin + HALO), tile, 0.0)


def fill(lo, pairs, stacked, frame, row, cols, low, high):
    rest = high.shape[-1]
    lo[frame, row, cols, :] = low
    pairs[frame, row + 1, cols, :rest] = high
    pairs[frame, row, cols, rest:] = high
    if frame < stacked.shape[0]:
        stacked[frame, row, cols, :rest] = high
    if frame > 0:
        stacked[frame - 1, row, cols, rest:] = high


def columns(taps, lo, pairs, stacked, row, rows):
    def flat(block):
        return block.reshape(-1, LANES)

    pieces = [flat(lo[f, pl.ds(row + b, rows)]) for f, _ in taps for b in range(3)]
    pieces += [flat(pairs[f, pl.ds(row + 1, rows)]) for f, _ in taps]
    for k in range(0, len(taps), 2):
        f = taps[k][0]
        if k + 1 < len(taps):
            pieces.append(flat(stacked[f, pl.ds(row + 2, rows)]))
        else:
            pieces.append(flat(pairs[f, pl.ds(row + 3, rows)]))
    return jnp.concatenate(pieces, axis=-1)


def planes(taps, weight, c):
    pieces = [weight[a][b, c, :LANES, :] for _, a in taps for b in range(3)]
    for _, a in taps:
        pieces += [weight[a][0, c, LANES:, :], weight[a][1, c, LANES:, :]]
    for _, a in taps:
        pieces.append(weight[a][2, c, LANES:, :])
    if len(taps) % 2:
        pieces.append(jnp.zeros_like(weight[a][0, c, LANES:, :]))
    return jnp.concatenate(pieces, axis=0)


def convolve(taps, weight, lefts):
    return [
        jnp.dot(lefts, planes(taps, weight, c), preferred_element_type=jnp.float32)
        for c in range(3)
    ]


def join(products, start, width):
    before, middle, after = [p[start : start + width] for p in products]
    return pltpu.roll(before, 1, 0) + middle + pltpu.roll(after, width - 1, 0)


def activate(y, gains):
    mean_square = jnp.sum(y * y, axis=-1, keepdims=True) * (1.0 / y.shape[-1])
    v = y * lax.rsqrt(mean_square + EPS) * gains
    return v / (1.0 + jnp.exp(-v))


def clear(buffers):
    for buffer in buffers:
        buffer[...] = jnp.zeros_like(buffer)


def facing(strips, rows):
    if strips == 2:
        return [jnp.where(lax.axis_index("strip") == 0, rows - HALO, 0)]
    return [rows - HALO, 0]


def at_top(strips):
    return [lax.axis_index("strip")] if strips == 2 else [1, 0]


def safe_rows(strips, rows):
    return (1 + lax.axis_index("strip"), rows - 1) if strips == 2 else (2, rows - 2)


def beside_of(neighbour, f, r, cols):
    start = pl.multiple_of(lax.axis_index("slab") * (cols - TILE), TILE)
    return neighbour[f, r, pl.ds(start, TILE), :]


def stage_kernel(own_far, weight_far, own, middle, last, arrived):
    copies = [
        pltpu.make_async_copy(own_far, own, arrived.at[0]),
        pltpu.make_async_copy(weight_far.at[2], last, arrived.at[1]),
        pltpu.make_async_copy(weight_far.at[1], middle, arrived.at[2]),
    ]
    for copy in copies:
        copy.start()
    for copy in copies:
        copy.wait()


def pack_kernel(strips, own, neighbour, block, *edges):
    frames, rows, cols, _ = own.shape
    whole = Packed(HALO, rows, cols)
    skip = frames - HALO
    whole.write(block, lambda f, r: own[f + skip, r], lambda f, r: beside_of(neighbour, f + skip, r, cols))
    for start, edge in zip(facing(strips, rows), edges):
        Packed(frames, HALO, cols).write(
            edge, lambda f, r: own[f, start + r], lambda f, r: beside_of(neighbour, f, start + r, cols)
        )


def own_beside(neighbour, f, r, cols):
    tile = only_beside(beside_of(neighbour, f, r, cols).astype(jnp.float32)).astype(jnp.bfloat16)
    return tile[:, :LANES], tile[:, LANES:]


def window(buffers, frames, top, rows, cols, own, halo):
    every, beside = slice(0, cols), slice(cols, cols + TILE)
    for f in range(frames):
        for j in range(HALO):
            for cells, row in ((own(f, (1 - top) * (rows - HALO) + j), HALO * top + j), (halo(f, j), HALO * (1 - top) + j)):
                fill(*buffers, f, row, every, *cells[:2])
                fill(*buffers, f, row, beside, *cells[2:])


def safe_kernel(strips, own, neighbour, middle, last, weight_far, out, plane, lo, pairs, stacked, arrived):
    frames, rows, cols, channels = own.shape
    width = cols + TILE
    copy = pltpu.make_async_copy(weight_far.at[0], plane, arrived.at[0])
    copy.start()
    if frames > 2:
        copy.wait()
    clear((lo, pairs, stacked))
    for f in range(frames):
        for r in range(rows):
            cells = own[f, r]
            fill(lo, pairs, stacked, f, r + HALO, slice(0, cols), cells[:, :LANES], cells[:, LANES:])
            fill(lo, pairs, stacked, f, r + HALO, slice(cols, width), *own_beside(neighbour, f, r, cols))
    start, count = safe_rows(strips, rows)
    for t in range(frames):
        taps = own_taps(t)
        products = convolve(taps, [plane, middle, last], columns(taps, lo, pairs, stacked, start, count))
        for r in range(count):
            out[t, r] = join(products, r * width, width)
    if frames <= 2:
        copy.wait()


def own_taps(t):
    return [(f, f - t + 2) for f in range(max(0, t - 2), t + 1)]


def earlier_taps(t):
    return [(f, f - t) for f in range(t, HALO)]


def hidden_row(y, gain, cols):
    width, slab = y.shape[0], lax.axis_index("slab")
    position = lax.broadcasted_iota(jnp.int32, (width, 1), 0)
    right = cols + (slab == 0).astype(jnp.int32)
    left = width - (slab == 1).astype(jnp.int32)
    return jnp.where((position < right) | (position >= left), activate(y, gain), 0.0)


def middle_kernel(strips, rows, cols, *refs):
    *refs, lo, pairs, stacked, near_lo, near_pairs, near_stacked, arrived = refs
    *refs, h_lo, h_pairs, h_stacked, edge_sums, w2_first, w2_middle, w2_last = refs
    own, neighbour, *edges, block, sums, plane, middle, last, gains, w2_far = refs
    frames, channels = own.shape[0], own.shape[-1]
    width, rest = cols + TILE, channels - LANES
    w2 = [w2_first, w2_middle, w2_last]
    copies = [pltpu.make_async_copy(w2_far.at[a], w2[a], arrived.at[a]) for a in range(3)]
    for copy in copies:
        copy.start()
    clear((lo, pairs, stacked, h_lo, h_pairs, h_stacked, near_pairs))
    whole, strip_block = Packed(HALO, rows, cols), Packed(frames, HALO, cols)

    @if_earlier
    def build():
        for f in range(HALO):
            for r in range(rows):
                fill(lo, pairs, stacked, f, r + HALO, slice(0, cols), *whole.read(block, f, r, rest))
                fill(lo, pairs, stacked, f, r + HALO, slice(cols, width), *whole.read_beside(block, f, r, rest))

    gain = gains[...]
    start, count = safe_rows(strips, rows)
    for t in range(frames):
        taps = earlier_taps(t)
        products = convolve(taps, [plane, middle], columns(taps, lo, pairs, stacked, start, count)) if taps else None
        for r in range(count):
            y = sums[t, r]
            if taps:
                y = y + join(products, r * width, width)
            h = hidden_row(y, gain, cols).astype(jnp.bfloat16)
            fill(h_lo, h_pairs, h_stacked, t, start + r, slice(0, width), h[:, :LANES], h[:, LANES:])

    near = (near_lo, near_pairs, near_stacked)
    for group, (edge, top) in enumerate(zip(edges, at_top(strips))):

        def own_row(f, r):
            cells = own[f, r]
            return cells[:, :LANES], cells[:, LANES:], *own_beside(neighbour, f, r, cols)

        def halo_row(f, j):
            return *strip_block.read(edge, f, j, rest), *strip_block.read_beside(edge, f, j, rest)

        window(near, frames, top, rows, cols, own_row, halo_row)
        for t in range(frames):
            taps = own_taps(t)
            products = convolve(taps, [plane, middle, last], columns(taps, *near, 0, HALO))
            for r in range(HALO):
                edge_sums[group, t, r] = join(products, r * width, width)
    for copy in copies:
        copy.wait()


def edge_kernel(strips, rows, cols, *refs):
    *refs, near_lo, near_pairs, near_stacked = refs
    *refs, h_lo, h_pairs, h_stacked, partial = refs
    *edges, block, edge_sums, safe_lo, safe_pairs, safe_stacked, plane, middle, gains, w2_first, w2_middle = refs
    frames, channels = edge_sums.shape[1], edge_sums.shape[-1]
    width, rest = cols + TILE, channels - LANES
    strip = lax.axis_index("strip")
    whole, strip_block = Packed(HALO, rows, cols), Packed(frames, HALO, cols)
    near = (near_lo, near_pairs, near_stacked)
    clear(near)
    for target, source in ((h_lo, safe_lo), (h_pairs, safe_pairs), (h_stacked, safe_stacked)):
        target[...] = source[...]
    gain = gains[...]
    for group, (edge, top) in enumerate(zip(edges, at_top(strips))):

        def own_row(f, r):
            low = pl.multiple_of((f * rows + r) * cols, TILE)
            high = pl.multiple_of(whole.high + (f * (rows // 2) + r // 2) * cols, TILE)
            pair = block[pl.ds(high, cols), :]
            return block[pl.ds(low, cols), :], pair, *beside_from(block, whole.beside, (f * rows + r) * HALO, rest)

        def halo_row(f, j):
            sent = frames - HALO + f
            return *strip_block.read(edge, sent, j, rest), *strip_block.read_beside(edge, sent, j, rest)

        def own_half(f, r, j):
            low, pair, *tile = own_row(f, r)
            return low, pair[:, (j % 2) * rest : (j % 2 + 1) * rest], *tile

        @if_earlier
        def build():
            every, beside = slice(0, cols), slice(cols, width)
            for f in range(HALO):
                for j in range(HALO):
                    mine = own_half(f, (1 - top) * (rows - HALO) + j, j)
                    for cells, row in ((mine, HALO * top + j), (halo_row(f, j), HALO * (1 - top) + j)):
                        fill(*near, f, row, every, *cells[:2])
                        fill(*near, f, row, beside, *cells[2:])

        for t in range(frames):
            taps = earlier_taps(t)
            products = convolve(taps, [plane, middle], columns(taps, *near, 0, HALO)) if taps else None
            for r in range(HALO):
                y = edge_sums[group, t, r]
                if taps:
                    y = y + join(products, r * width, width)
                h = hidden_row(y, gain, cols)
                if strips != 2 and r == 1 - top:
                    h = h * jnp.where(strip == (0 if top else strips - 1), 0.0, 1.0)
                h = h.astype(jnp.bfloat16)
                row = (1 - top) * rows + r
                fill(h_lo, h_pairs, h_stacked, t, row, slice(0, width), h[:, :LANES], h[:, LANES:])

    last = frames - 1
    for t, taps in enumerate(([(last - 1, 0), (last, 1)], [(last, 0)])):
        products = convolve(taps, [w2_first, w2_middle], columns(taps, h_lo, h_pairs, h_stacked, 0, rows))
        for r in range(rows):
            y = join(products, r * width, width)[:cols].astype(jnp.bfloat16)
            partial[t, r] = y[:, :LANES]
            half = r % 2
            partial[t, rows + r // 2, :, half * rest : (half + 1) * rest] = y[:, LANES:]


def second_kernel(frames, rows, cols, h_lo, h_pairs, h_stacked, *refs):
    *w2, out = refs
    width = cols + TILE
    for t in range(frames):
        taps = [(f, f - t + 2) for f in range(max(0, t - 2), t + 1)]
        products = convolve(taps, w2, columns(taps, h_lo, h_pairs, h_stacked, 0, rows))
        for r in range(rows):
            out[t, r] = join(products, r * width, width)[:cols]


def finish_kernel(partial, own, gains, out_far, out, left):
    frames, rows, cols, channels = out.shape
    rest = channels - LANES
    gain = gains[...]

    copies = [pltpu.make_async_copy(out.at[t], out_far.at[t], left.at[t]) for t in range(frames)]
    for t in range(frames):
        for r in range(rows):
            y = own[t, r]
            if t < HALO:
                half = r % 2
                high = partial[t, rows + r // 2, :, half * rest : (half + 1) * rest]
                sent = jnp.concatenate([partial[t, r], high], axis=-1)
                y = y + sent.astype(jnp.float32)
            out[t, r] = activate(y, gain).astype(jnp.bfloat16)
        copies[t].start()
    for copy in copies:
        copy.wait()


def call(kernel, name, ins, outs, scratch=(), semaphores=0, flops=0, far=(), far_out=False):
    near, away = pl.BlockSpec(memory_space=pltpu.VMEM), pl.BlockSpec(memory_space=pltpu.HBM)
    in_specs, ins = [near] * len(ins), list(ins)
    for place in far:
        ins[place] = pltpu.with_memory_space_constraint(ins[place], pltpu.HBM)
        in_specs[place] = away
    one = not isinstance(outs, list)
    return pl.pallas_call(
        kernel,
        out_shape=outs,
        in_specs=in_specs,
        out_specs=(away if far_out else near) if one else [near] * len(outs),
        scratch_shapes=[pltpu.VMEM(shape, jnp.bfloat16) for shape in scratch]
        + [pltpu.SemaphoreType.DMA((semaphores,))] * (semaphores > 0),
        compiler_params=pltpu.CompilerParams(vmem_limit_bytes=24 * 1024 * 1024),
        cost_estimate=pl.CostEstimate(flops=flops, bytes_accessed=4 * 1024 * 1024, transcendentals=0),
        name=name,
    )(*ins)


def block_scratch(frames, rows, width):
    return [(frames, rows, width, LANES), (frames, rows + 1, width, LANES), (frames - 1, rows, width, LANES)]


def shards(frames_in, weight_first, scale_first, weight_second, scale_second):
    frames, rows, cols, channels = frames_in.shape
    strips = lax.axis_size("strip")
    width = cols + TILE
    flops = frames * rows * cols * 27 * channels * channels
    bf16 = functools.partial(jax.ShapeDtypeStruct, dtype=jnp.bfloat16)
    f32 = functools.partial(jax.ShapeDtypeStruct, dtype=jnp.float32)

    plane_shape = bf16(weight_first.shape[1:])
    neighbour = swap(frames_in, "slab")
    own_in, middle, last = call(
        stage_kernel,
        "stage",
        [frames_in, weight_first],
        [bf16(frames_in.shape), plane_shape, plane_shape],
        semaphores=3,
        far=[0, 1],
    )
    edge_shape = bf16(Packed(frames, HALO, cols).shape)
    block, *edges = call(
        functools.partial(pack_kernel, strips),
        "pack",
        [own_in, neighbour],
        [bf16(Packed(HALO, rows, cols).shape)] + [edge_shape] * (1 if strips == 2 else 2),
    )
    ups = [(i, i + 1) for i in range(strips - 1)]
    downs = [(i + 1, i) for i in range(strips - 1)]
    ways = [[(0, 1), (1, 0)]] if strips == 2 else [ups, downs]
    before = forward(block)
    own_edges = [lax.ppermute(edge, "strip", way) for edge, way in zip(edges, ways)]
    before_edges = [forward(edge, way) for edge, way in zip(edges, ways)]
    sums, plane = call(
        functools.partial(safe_kernel, strips),
        "own_safe_rows",
        [own_in, neighbour, middle, last, weight_first],
        [f32((frames, safe_rows(strips, rows)[1], width, channels)), plane_shape],
        block_scratch(frames, rows + 2 * HALO, width),
        semaphores=1,
        flops=flops // 2,
        far=[-1],
    )
    h_shapes = [bf16(shape) for shape in block_scratch(frames, rows + 2, width)]
    gain_first = scale_first[None]
    *safe, edge_sums, w2_first, w2_middle, w2_last = call(
        functools.partial(middle_kernel, strips, rows, cols),
        "safe_rows",
        [own_in, neighbour, *own_edges, before, sums, plane, middle, last, gain_first, weight_second],
        h_shapes + [f32((len(ways), frames, HALO, width, channels))] + [plane_shape] * 3,
        block_scratch(HALO, rows + 2 * HALO, width) + block_scratch(frames, 2 * HALO, width),
        semaphores=3,
        flops=flops // 2,
        far=[-1],
    )
    h_lo, h_pairs, h_stacked, partial = call(
        functools.partial(edge_kernel, strips, rows, cols),
        "edge_rows",
        [*before_edges, before, edge_sums, *safe, plane, middle, gain_first, w2_first, w2_middle],
        h_shapes + [bf16((HALO, rows + rows // 2, cols, LANES))],
        block_scratch(HALO, 2 * HALO, width),
        flops=flops,
    )
    w2 = [w2_first, w2_middle, w2_last]
    sent = forward(partial)
    own = call(
        functools.partial(second_kernel, frames, rows, cols),
        "second_layer",
        [h_lo, h_pairs, h_stacked, *w2],
        f32((frames, rows, cols, channels)),
        flops=flops,
    )
    out = bf16(frames_in.shape)
    return call(
        finish_kernel,
        "finish",
        [sent, own, scale_second[None]],
        out,
        [out.shape],
        semaphores=frames,
        far_out=True,
    )


def solution(mesh):
    return jax.shard_map(
        shards,
        mesh=mesh,
        in_specs=(P(("groups", "frame"), "strip", "slab", None), P(), P(), P(), P()),
        out_specs=P(("groups", "frame"), "strip", "slab", None),
        check_vma=False,
    )
```

```python
import functools

import jax
import jax.numpy as jnp
from jax import lax
from jax.experimental import pallas as pl
from jax.experimental.pallas import tpu as pltpu
from jax.sharding import PartitionSpec as P

LANES = 128
TILE = 16
EPS = 1e-06
MOVED = 64


HALO = 2


def swap(x, axis):
    return lax.ppermute(x, axis, [(0, 1), (1, 0)])


def forward(x, way=None):
    steps, count = lax.axis_size("frame"), lax.axis_size("strip")
    way = [(i, i) for i in range(count)] if way is None else way
    pairs = [(f * count + i, (f + 1) * count + j) for f in range(steps - 1) for i, j in way]
    return lax.ppermute(x, ("frame", "strip"), pairs)


def if_earlier(build):
    pl.when(lax.axis_index("frame") > 0)(build)


class Packed:
    def __init__(self, frames, rows, cols):
        self.frames, self.rows, self.cols = frames, rows, cols
        self.high = frames * rows * cols
        self.beside = self.high + frames * (rows // 2) * cols
        self.tiles = -(-frames * rows * HALO // TILE)
        self.shape = (self.beside + 2 * self.tiles * TILE, LANES)

    def low_at(self, f, r):
        return slice((f * self.rows + r) * self.cols, (f * self.rows + r + 1) * self.cols)

    def high_at(self, f, r):
        start = self.high + (f * (self.rows // 2) + r // 2) * self.cols
        return slice(start, start + self.cols)

    def spot(self, f, r):
        cell = (f * self.rows + r) * HALO
        return cell // TILE, cell % TILE

    def beside_at(self, tile, high):
        start = self.beside + (2 * tile + high) * TILE
        return slice(start, start + TILE)

    def write(self, out, cells, tile_of):
        slab = lax.axis_index("slab")
        at = lax.broadcasted_iota(jnp.int32, (TILE, 1), 0)
        sums = [None] * self.tiles
        for f in range(self.frames):
            for r in range(self.rows):
                row = cells(f, r)
                out[self.low_at(f, r), :] = row[:, :LANES]
                rest = row.shape[-1] - LANES
                half = slice((r % 2) * rest, (r % 2 + 1) * rest)
                out[self.high_at(f, r), half] = row[:, LANES:]
                tile, place = self.spot(f, r)
                moved = pltpu.roll(tile_of(f, r).astype(jnp.float32), lax.rem(place + HALO * slab, TILE), 0)
                moved = jnp.where((at >= place) & (at < place + HALO), moved, 0.0)
                sums[tile] = moved if sums[tile] is None else sums[tile] + moved
        for tile, cells_beside in enumerate(sums):
            cells_beside = cells_beside.astype(jnp.bfloat16)
            out[self.beside_at(tile, 0), :] = cells_beside[:, :LANES]
            out[self.beside_at(tile, 1), :rest] = cells_beside[:, LANES:]

    def read(self, ref, f, r, rest):
        half = slice((r % 2) * rest, (r % 2 + 1) * rest)
        return ref[self.low_at(f, r), :], ref[self.high_at(f, r), half]

    def read_beside(self, ref, f, r, rest):
        return beside_from(ref, self.beside, (f * self.rows + r) * HALO, rest)


def beside_from(ref, start, cell, rest):
    slab = lax.axis_index("slab")
    parts = []
    for high, lanes in ((0, LANES), (1, rest)):
        at = start + (2 * (cell // TILE) + high) * TILE
        cells = ref[pl.ds(pl.multiple_of(at, TILE), TILE), :].astype(jnp.float32)
        cells = pltpu.roll(cells, lax.rem(2 * TILE - cell % TILE - HALO * slab, TILE), 0)
        parts.append(only_beside(cells).astype(jnp.bfloat16)[:, :lanes])
    return parts


def only_beside(tile):
    slab = lax.axis_index("slab")
    at = lax.broadcasted_iota(jnp.int32, tile.shape, 0)
    begin = slab * (TILE - HALO)
    return jnp.where((at >= begin) & (at < begin + HALO), tile, 0.0)


def fill(lo, pairs, stacked, frame, row, cols, low, high):
    rest = high.shape[-1]
    lo[frame, row, cols, :] = low
    pairs[frame, row + 1, cols, :rest] = high
    pairs[frame, row, cols, rest:] = high
    if frame < stacked.shape[0]:
        stacked[frame, row, cols, :rest] = high
    if frame > 0:
        stacked[frame - 1, row, cols, rest:] = high


def columns(taps, lo, pairs, stacked, row, rows):
    def flat(block):
        return block.reshape(-1, LANES)

    pieces = [flat(lo[f, pl.ds(row + b, rows)]) for f, _ in taps for b in range(3)]
    pieces += [flat(pairs[f, pl.ds(row + 1, rows)]) for f, _ in taps]
    for k in range(0, len(taps), 2):
        f = taps[k][0]
        if k + 1 < len(taps):
            pieces.append(flat(stacked[f, pl.ds(row + 2, rows)]))
        else:
            pieces.append(flat(pairs[f, pl.ds(row + 3, rows)]))
    return jnp.concatenate(pieces, axis=-1)


def planes(taps, weight, c):
    pieces = [weight[a][b, c, :LANES, :] for _, a in taps for b in range(3)]
    for _, a in taps:
        pieces += [weight[a][0, c, LANES:, :], weight[a][1, c, LANES:, :]]
    for _, a in taps:
        pieces.append(weight[a][2, c, LANES:, :])
    if len(taps) % 2:
        pieces.append(jnp.zeros_like(weight[a][0, c, LANES:, :]))
    return jnp.concatenate(pieces, axis=0)


def convolve(taps, weight, lefts):
    return [
        jnp.dot(lefts, planes(taps, weight, c), preferred_element_type=jnp.float32)
        for c in range(3)
    ]


def join(products, start, width):
    before, middle, after = [p[start : start + width] for p in products]
    return pltpu.roll(before, 1, 0) + middle + pltpu.roll(after, width - 1, 0)


def activate(y, gains):
    mean_square = jnp.sum(y * y, axis=-1, keepdims=True) * (1.0 / y.shape[-1])
    v = y * lax.rsqrt(mean_square + EPS) * gains
    return v / (1.0 + jnp.exp(-v))


def clear(buffers):
    for buffer in buffers:
        buffer[...] = jnp.zeros_like(buffer)


def facing(strips, rows):
    if strips == 2:
        return [jnp.where(lax.axis_index("strip") == 0, rows - HALO, 0)]
    return [rows - HALO, 0]


def at_top(strips):
    return [lax.axis_index("strip")] if strips == 2 else [1, 0]


def safe_rows(strips, rows):
    return (1 + lax.axis_index("strip"), rows - 1) if strips == 2 else (2, rows - 2)


def beside_of(neighbour, f, r, cols):
    start = pl.multiple_of(lax.axis_index("slab") * (cols - TILE), TILE)
    return neighbour[f, r, pl.ds(start, TILE), :]


def stage_kernel(own_far, weight_far, own, weight, arrived):
    copies = [
        pltpu.make_async_copy(own_far, own, arrived.at[0]),
        pltpu.make_async_copy(weight_far, weight, arrived.at[1]),
    ]
    for copy in copies:
        copy.start()
    for copy in copies:
        copy.wait()


def pack_kernel(strips, own, neighbour, block, *edges):
    frames, rows, cols, _ = own.shape
    whole = Packed(HALO, rows, cols)
    skip = frames - HALO
    whole.write(block, lambda f, r: own[f + skip, r], lambda f, r: beside_of(neighbour, f + skip, r, cols))
    for start, edge in zip(facing(strips, rows), edges):
        Packed(frames, HALO, cols).write(
            edge, lambda f, r: own[f, start + r], lambda f, r: beside_of(neighbour, f, start + r, cols)
        )


def own_beside(neighbour, f, r, cols):
    tile = only_beside(beside_of(neighbour, f, r, cols).astype(jnp.float32)).astype(jnp.bfloat16)
    return tile[:, :LANES], tile[:, LANES:]


def split(weight):
    return [weight.at[a] for a in range(3)]


def all_taps(t):
    return [(t, 0), (t + 1, 1), (t + 2, 2)]


def hidden_row(y, gain, cols):
    width, slab = y.shape[0], lax.axis_index("slab")
    position = lax.broadcasted_iota(jnp.int32, (width, 1), 0)
    right = cols + (slab == 0).astype(jnp.int32)
    left = width - (slab == 1).astype(jnp.int32)
    return jnp.where((position < right) | (position >= left), activate(y, gain), 0.0)


def hidden_rows(strips, frames, buffers, start, count, weight, gain, cols):
    lefts = jnp.concatenate([columns(all_taps(t), *buffers, start, count) for t in range(frames)], axis=0)
    products = convolve(all_taps(0), split(weight), lefts)
    width = cols + TILE
    for t in range(frames):
        for r in range(count):
            yield t, r, hidden_row(join(products, (t * count + r) * width, width), gain, cols)


def safe_kernel(strips, own, neighbour, block, weight, gains, h_lo, h_pairs, h_stacked, lo, pairs, stacked):
    frames, rows, cols, channels = own.shape
    width, rest = cols + TILE, channels - LANES
    every, beside = slice(0, cols), slice(cols, width)
    clear((lo, pairs, stacked, h_lo, h_pairs, h_stacked))
    whole = Packed(HALO, rows, cols)

    @if_earlier
    def build():
        for f in range(HALO):
            for r in range(rows):
                fill(lo, pairs, stacked, f, r + HALO, every, *whole.read(block, f, r, rest))
                fill(lo, pairs, stacked, f, r + HALO, beside, *whole.read_beside(block, f, r, rest))

    for f in range(frames):
        for r in range(rows):
            cells = own[f, r]
            fill(lo, pairs, stacked, HALO + f, r + HALO, every, cells[:, :LANES], cells[:, LANES:])
            fill(lo, pairs, stacked, HALO + f, r + HALO, beside, *own_beside(neighbour, f, r, cols))
    start, count = safe_rows(strips, rows)
    for t, r, h in hidden_rows(strips, frames, (lo, pairs, stacked), start, count, weight, gains[...], cols):
        h = h.astype(jnp.bfloat16)
        fill(h_lo, h_pairs, h_stacked, t, start + r, slice(0, width), h[:, :LANES], h[:, LANES:])


def edge_kernel(strips, *refs):
    *refs, near_lo, near_pairs, near_stacked = refs
    *refs, h_lo, h_pairs, h_stacked, partial = refs
    *edges, own, neighbour, block, safe_lo, safe_pairs, safe_stacked, w1, gains, w2 = refs
    frames, rows, cols, channels = own.shape
    width, rest = cols + TILE, channels - LANES
    every, beside = slice(0, cols), slice(cols, width)
    strip = lax.axis_index("strip")
    whole, strip_block = Packed(HALO, rows, cols), Packed(frames, HALO, cols)
    near = (near_lo, near_pairs, near_stacked)
    clear(near)
    for target, source in ((h_lo, safe_lo), (h_pairs, safe_pairs), (h_stacked, safe_stacked)):
        target[...] = source[...]
    tops = at_top(strips)
    for own_edge, earlier_edge, top in zip(edges, edges[len(tops) :], tops):
        first, mine, theirs = (1 - top) * (rows - HALO), HALO * top, HALO * (1 - top)

        def put(frame, row, *cells):
            fill(*near, frame, row, every, *cells[:2])
            fill(*near, frame, row, beside, *cells[2:])

        def put_halo(frame, j, edge, f):
            cells = *strip_block.read(edge, f, j, rest), *strip_block.read_beside(edge, f, j, rest)
            put(frame, theirs + j, *cells)

        @if_earlier
        def build():
            for f in range(HALO):
                for j in range(HALO):
                    r = first + j
                    low = pl.multiple_of((f * rows + r) * cols, TILE)
                    high = pl.multiple_of(whole.high + (f * (rows // 2) + r // 2) * cols, TILE)
                    half = block[pl.ds(high, cols), :][:, (j % 2) * rest : (j % 2 + 1) * rest]
                    tile = beside_from(block, whole.beside, (f * rows + r) * HALO, rest)
                    put(f, mine + j, block[pl.ds(low, cols), :], half, *tile)
                    put_halo(f, j, earlier_edge, frames - HALO + f)

        for f in range(frames):
            for j in range(HALO):
                cells = own[f, first + j]
                tile = own_beside(neighbour, f, first + j, cols)
                put(HALO + f, mine + j, cells[:, :LANES], cells[:, LANES:], *tile)
                put_halo(HALO + f, j, own_edge, f)

        for t, r, h in hidden_rows(strips, frames, near, 0, HALO, w1, gains[...], cols):
            if strips != 2 and r == 1 - top:
                h = h * jnp.where(strip == (0 if top else strips - 1), 0.0, 1.0)
            h = h.astype(jnp.bfloat16)
            row = (1 - top) * rows + r
            fill(h_lo, h_pairs, h_stacked, t, row, slice(0, width), h[:, :LANES], h[:, LANES:])

    last = frames - 1
    for t, taps in enumerate(([(last - 1, 0), (last, 1)], [(last, 0)])):
        products = convolve(taps, split(w2), columns(taps, h_lo, h_pairs, h_stacked, 0, rows))
        for r in range(rows):
            y = join(products, r * width, width)[:cols].astype(jnp.bfloat16)
            partial[t, r] = y[:, :LANES]
            half = r % 2
            partial[t, rows + r // 2, :, half * rest : (half + 1) * rest] = y[:, LANES:]


def second_kernel(frames, rows, cols, h_lo, h_pairs, h_stacked, w2, out):
    width = cols + TILE
    for t in range(frames):
        taps = [(f, f - t + 2) for f in range(max(0, t - 2), t + 1)]
        products = convolve(taps, split(w2), columns(taps, h_lo, h_pairs, h_stacked, 0, rows))
        for r in range(rows):
            out[t, r] = join(products, r * width, width)[:cols]


def finish_kernel(partial, own, gains, out_far, out, left):
    frames, rows, cols, channels = out.shape
    rest = channels - LANES
    gain = gains[...]

    copies = [pltpu.make_async_copy(out.at[t], out_far.at[t], left.at[t]) for t in range(frames)]
    for t in range(frames):
        for r in range(rows):
            y = own[t, r]
            if t < HALO:
                half = r % 2
                high = partial[t, rows + r // 2, :, half * rest : (half + 1) * rest]
                sent = jnp.concatenate([partial[t, r], high], axis=-1)
                y = y + sent.astype(jnp.float32)
            out[t, r] = activate(y, gain).astype(jnp.bfloat16)
        copies[t].start()
    for copy in copies:
        copy.wait()


def call(kernel, name, ins, outs, scratch=(), semaphores=0, flops=0, moved=4, far=(), far_out=False):
    near, away = pl.BlockSpec(memory_space=pltpu.VMEM), pl.BlockSpec(memory_space=pltpu.HBM)
    in_specs, ins = [near] * len(ins), list(ins)
    for place in far:
        ins[place] = pltpu.with_memory_space_constraint(ins[place], pltpu.HBM)
        in_specs[place] = away
    one = not isinstance(outs, list)
    return pl.pallas_call(
        kernel,
        out_shape=outs,
        in_specs=in_specs,
        out_specs=(away if far_out else near) if one else [near] * len(outs),
        scratch_shapes=[pltpu.VMEM(shape, jnp.bfloat16) for shape in scratch]
        + [pltpu.SemaphoreType.DMA((semaphores,))] * (semaphores > 0),
        compiler_params=pltpu.CompilerParams(vmem_limit_bytes=24 * 1024 * 1024),
        cost_estimate=pl.CostEstimate(flops=flops, bytes_accessed=moved * 1024 * 1024, transcendentals=0),
        name=name,
    )(*ins)


def block_scratch(frames, rows, width):
    return [(frames, rows, width, LANES), (frames, rows + 1, width, LANES), (frames - 1, rows, width, LANES)]


def shards(frames_in, weight_first, scale_first, weight_second, scale_second):
    frames, rows, cols, channels = frames_in.shape
    strips = lax.axis_size("strip")
    width = cols + TILE
    flops = frames * rows * cols * 27 * channels * channels
    bf16 = functools.partial(jax.ShapeDtypeStruct, dtype=jnp.bfloat16)
    f32 = functools.partial(jax.ShapeDtypeStruct, dtype=jnp.float32)

    neighbour = swap(frames_in, "slab")
    own, weight_first = call(
        stage_kernel,
        "stage",
        [frames_in, weight_first],
        [bf16(frames_in.shape), bf16(weight_first.shape)],
        semaphores=2,
        far=[0, 1],
    )
    edge_shape = bf16(Packed(frames, HALO, cols).shape)
    block, *edges = call(
        functools.partial(pack_kernel, strips),
        "pack",
        [own, neighbour],
        [bf16(Packed(HALO, rows, cols).shape)] + [edge_shape] * (1 if strips == 2 else 2),
        moved=MOVED,
    )
    ups = [(i, i + 1) for i in range(strips - 1)]
    downs = [(i + 1, i) for i in range(strips - 1)]
    ways = [[(0, 1), (1, 0)]] if strips == 2 else [ups, downs]
    before = forward(block)
    own_edges = [lax.ppermute(edge, "strip", way) for edge, way in zip(edges, ways)]
    before_edges = [forward(edge, way) for edge, way in zip(edges, ways)]
    gain_first = scale_first[None]
    h_shapes = [bf16(shape) for shape in block_scratch(frames, rows + 2, width)]
    safe = call(
        functools.partial(safe_kernel, strips),
        "safe_rows",
        [own, neighbour, before, weight_first, gain_first],
        h_shapes,
        block_scratch(HALO + frames, rows + 2 * HALO, width),
        flops=flops,
    )
    h_lo, h_pairs, h_stacked, partial = call(
        functools.partial(edge_kernel, strips),
        "edge_rows",
        [*own_edges, *before_edges, own, neighbour, before, *safe, weight_first, gain_first, weight_second],
        h_shapes + [bf16((HALO, rows + rows // 2, cols, LANES))],
        block_scratch(HALO + frames, 2 * HALO, width),
        flops=flops,
    )
    sent = forward(partial)
    own = call(
        functools.partial(second_kernel, frames, rows, cols),
        "second_layer",
        [h_lo, h_pairs, h_stacked, weight_second],
        f32((frames, rows, cols, channels)),
        flops=flops,
    )
    out = bf16(frames_in.shape)
    return call(
        finish_kernel,
        "finish",
        [sent, own, scale_second[None]],
        out,
        [out.shape],
        semaphores=frames,
        far_out=True,
    )


def solution(mesh):
    return jax.shard_map(
        shards,
        mesh=mesh,
        in_specs=(P(("groups", "frame"), "strip", "slab", None), P(), P(), P(), P()),
        out_specs=P(("groups", "frame"), "strip", "slab", None),
        check_vma=False,
    )
```

```python
import functools

import jax
import jax.numpy as jnp
from jax import lax
from jax.experimental import pallas as pl
from jax.experimental.pallas import tpu as pltpu
from jax.sharding import PartitionSpec as P

LANES = 128
TILE = 16
EPS = 1e-06


HALO = 2


def swap(x, axis):
    return lax.ppermute(x, axis, [(0, 1), (1, 0)])


def forward(x, way=None):
    steps, count = lax.axis_size("frame"), lax.axis_size("strip")
    way = [(i, i) for i in range(count)] if way is None else way
    pairs = [(f * count + i, (f + 1) * count + j) for f in range(steps - 1) for i, j in way]
    return lax.ppermute(x, ("frame", "strip"), pairs)


def if_earlier(build):
    pl.when(lax.axis_index("frame") > 0)(build)


class Packed:
    def __init__(self, frames, rows, cols):
        self.frames, self.rows, self.cols = frames, rows, cols
        self.high = frames * rows * cols
        self.beside = self.high + frames * (rows // 2) * cols
        self.tiles = -(-frames * rows * HALO // TILE)
        self.shape = (self.beside + 2 * self.tiles * TILE, LANES)

    def low_at(self, f, r):
        return slice((f * self.rows + r) * self.cols, (f * self.rows + r + 1) * self.cols)

    def high_at(self, f, r):
        start = self.high + (f * (self.rows // 2) + r // 2) * self.cols
        return slice(start, start + self.cols)

    def spot(self, f, r):
        cell = (f * self.rows + r) * HALO
        return cell // TILE, cell % TILE

    def beside_at(self, tile, high):
        start = self.beside + (2 * tile + high) * TILE
        return slice(start, start + TILE)

    def write(self, out, cells, tile_of):
        slab = lax.axis_index("slab")
        at = lax.broadcasted_iota(jnp.int32, (TILE, 1), 0)
        sums = [None] * self.tiles
        for f in range(self.frames):
            for r in range(self.rows):
                row = cells(f, r)
                out[self.low_at(f, r), :] = row[:, :LANES]
                rest = row.shape[-1] - LANES
                half = slice((r % 2) * rest, (r % 2 + 1) * rest)
                out[self.high_at(f, r), half] = row[:, LANES:]
                tile, place = self.spot(f, r)
                moved = pltpu.roll(tile_of(f, r).astype(jnp.float32), lax.rem(place + HALO * slab, TILE), 0)
                moved = jnp.where((at >= place) & (at < place + HALO), moved, 0.0)
                sums[tile] = moved if sums[tile] is None else sums[tile] + moved
        for tile, cells_beside in enumerate(sums):
            cells_beside = cells_beside.astype(jnp.bfloat16)
            out[self.beside_at(tile, 0), :] = cells_beside[:, :LANES]
            out[self.beside_at(tile, 1), :rest] = cells_beside[:, LANES:]

    def read(self, ref, f, r, rest):
        half = slice((r % 2) * rest, (r % 2 + 1) * rest)
        return ref[self.low_at(f, r), :], ref[self.high_at(f, r), half]

    def read_beside(self, ref, f, r, rest):
        return beside_from(ref, self.beside, (f * self.rows + r) * HALO, rest)


def beside_from(ref, start, cell, rest):
    slab = lax.axis_index("slab")
    parts = []
    for high, lanes in ((0, LANES), (1, rest)):
        at = start + (2 * (cell // TILE) + high) * TILE
        cells = ref[pl.ds(pl.multiple_of(at, TILE), TILE), :].astype(jnp.float32)
        cells = pltpu.roll(cells, lax.rem(2 * TILE - cell % TILE - HALO * slab, TILE), 0)
        parts.append(only_beside(cells).astype(jnp.bfloat16)[:, :lanes])
    return parts


def only_beside(tile):
    slab = lax.axis_index("slab")
    at = lax.broadcasted_iota(jnp.int32, tile.shape, 0)
    begin = slab * (TILE - HALO)
    return jnp.where((at >= begin) & (at < begin + HALO), tile, 0.0)


def fill(lo, pairs, stacked, frame, row, cols, low, high):
    rest = high.shape[-1]
    lo[frame, row, cols, :] = low
    pairs[frame, row + 1, cols, :rest] = high
    pairs[frame, row, cols, rest:] = high
    if frame < stacked.shape[0]:
        stacked[frame, row, cols, :rest] = high
    if frame > 0:
        stacked[frame - 1, row, cols, rest:] = high


def columns(taps, lo, pairs, stacked, row, rows):
    def flat(block):
        return block.reshape(-1, LANES)

    pieces = [flat(lo[f, pl.ds(row + b, rows)]) for f, _ in taps for b in range(3)]
    pieces += [flat(pairs[f, pl.ds(row + 1, rows)]) for f, _ in taps]
    for k in range(0, len(taps), 2):
        f = taps[k][0]
        if k + 1 < len(taps):
            pieces.append(flat(stacked[f, pl.ds(row + 2, rows)]))
        else:
            pieces.append(flat(pairs[f, pl.ds(row + 3, rows)]))
    return jnp.concatenate(pieces, axis=-1)


def planes(taps, weight, c):
    pieces = [weight[a][b, c, :LANES, :] for _, a in taps for b in range(3)]
    for _, a in taps:
        pieces += [weight[a][0, c, LANES:, :], weight[a][1, c, LANES:, :]]
    for _, a in taps:
        pieces.append(weight[a][2, c, LANES:, :])
    if len(taps) % 2:
        pieces.append(jnp.zeros_like(weight[a][0, c, LANES:, :]))
    return jnp.concatenate(pieces, axis=0)


def convolve(taps, weight, lefts):
    return [
        jnp.dot(lefts, planes(taps, weight, c), preferred_element_type=jnp.float32)
        for c in range(3)
    ]


def join(products, start, width):
    before, middle, after = [p[start : start + width] for p in products]
    return pltpu.roll(before, 1, 0) + middle + pltpu.roll(after, width - 1, 0)


def activate(y, gains):
    mean_square = jnp.sum(y * y, axis=-1, keepdims=True) * (1.0 / y.shape[-1])
    v = y * lax.rsqrt(mean_square + EPS) * gains
    return v / (1.0 + jnp.exp(-v))


def clear(buffers):
    for buffer in buffers:
        buffer[...] = jnp.zeros_like(buffer)


def facing(strips, rows):
    if strips == 2:
        return [jnp.where(lax.axis_index("strip") == 0, rows - HALO, 0)]
    return [rows - HALO, 0]


def at_top(strips):
    return [lax.axis_index("strip")] if strips == 2 else [1, 0]


def safe_rows(strips, rows):
    return (1 + lax.axis_index("strip"), rows - 1) if strips == 2 else (2, rows - 2)


def beside_of(neighbour, f, r, cols):
    start = pl.multiple_of(lax.axis_index("slab") * (cols - TILE), TILE)
    return neighbour[f, r, pl.ds(start, TILE), :]


def stage_kernel(own_far, weight_far, own, middle, last, arrived):
    copies = [
        pltpu.make_async_copy(own_far, own, arrived.at[0]),
        pltpu.make_async_copy(weight_far.at[2], last, arrived.at[1]),
        pltpu.make_async_copy(weight_far.at[1], middle, arrived.at[2]),
    ]
    for copy in copies:
        copy.start()
    for copy in copies:
        copy.wait()


def pack_kernel(strips, own, neighbour, block, *edges):
    frames, rows, cols, _ = own.shape
    whole = Packed(HALO, rows, cols)
    skip = frames - HALO
    whole.write(block, lambda f, r: own[f + skip, r], lambda f, r: beside_of(neighbour, f + skip, r, cols))
    for start, edge in zip(facing(strips, rows), edges):
        Packed(frames, HALO, cols).write(
            edge, lambda f, r: own[f, start + r], lambda f, r: beside_of(neighbour, f, start + r, cols)
        )


def own_beside(neighbour, f, r, cols):
    tile = only_beside(beside_of(neighbour, f, r, cols).astype(jnp.float32)).astype(jnp.bfloat16)
    return tile[:, :LANES], tile[:, LANES:]


def window(buffers, frames, top, rows, cols, own, halo):
    every, beside = slice(0, cols), slice(cols, cols + TILE)
    for f in range(frames):
        for j in range(HALO):
            for cells, row in ((own(f, (1 - top) * (rows - HALO) + j), HALO * top + j), (halo(f, j), HALO * (1 - top) + j)):
                fill(*buffers, f, row, every, *cells[:2])
                fill(*buffers, f, row, beside, *cells[2:])


def edge_own_kernel(strips, *refs):
    *refs, near_lo, near_pairs, near_stacked, arrived = refs
    own, neighbour, *edges, middle, last, weight_far, edge_sums, plane = refs
    frames, rows, cols, channels = own.shape
    width, rest = cols + TILE, channels - LANES
    copy = pltpu.make_async_copy(weight_far.at[0], plane, arrived.at[0])
    copy.start()
    if frames > 2:
        copy.wait()
    strip_block = Packed(frames, HALO, cols)
    near = (near_lo, near_pairs, near_stacked)
    clear((near_pairs,))
    for group, (edge, top) in enumerate(zip(edges, at_top(strips))):

        def own_row(f, r):
            cells = own[f, r]
            return cells[:, :LANES], cells[:, LANES:], *own_beside(neighbour, f, r, cols)

        def halo_row(f, j):
            return *strip_block.read(edge, f, j, rest), *strip_block.read_beside(edge, f, j, rest)

        window(near, frames, top, rows, cols, own_row, halo_row)
        for t in range(frames):
            taps = own_taps(t)
            products = convolve(taps, [plane, middle, last], columns(taps, *near, 0, HALO))
            for r in range(HALO):
                edge_sums[group, t, r] = join(products, r * width, width)
    if frames <= 2:
        copy.wait()


def own_taps(t):
    return [(f, f - t + 2) for f in range(max(0, t - 2), t + 1)]


def earlier_taps(t):
    return [(f, f - t) for f in range(t, HALO)]


def hidden_row(y, gain, cols):
    width, slab = y.shape[0], lax.axis_index("slab")
    position = lax.broadcasted_iota(jnp.int32, (width, 1), 0)
    right = cols + (slab == 0).astype(jnp.int32)
    left = width - (slab == 1).astype(jnp.int32)
    return jnp.where((position < right) | (position >= left), activate(y, gain), 0.0)


def all_taps(t):
    return [(t, 0), (t + 1, 1), (t + 2, 2)]


def safe_sums(strips, rows):
    if strips == 2:
        strip = lax.axis_index("strip")
        return (HALO * strip, rows - HALO), ((1 - strip) * (rows - HALO), HALO)
    return (0, 0), (0, rows)


def partial_sums(frames, hidden, w2, start, count, rows, cols, partial):
    width, last = cols + TILE, frames - 1
    for t, taps in enumerate(([(last - 1, 0), (last, 1)], [(last, 0)])):
        products = convolve(taps, [w2.at[0], w2.at[1]], columns(taps, *hidden, start, count))
        for r in range(count):
            y = join(products, r * width, width)[:cols].astype(jnp.bfloat16)
            rest = y.shape[-1] - LANES
            partial[t, start + r] = y[:, :LANES]
            half = slice((r % 2) * rest, (r % 2 + 1) * rest)
            partial[t, rows + start // 2 + r // 2, :, half] = y[:, LANES:]


def safe_kernel(strips, *refs):
    *refs, lo, pairs, stacked = refs
    own, neighbour, block, plane, middle, last, gains, w2, h_lo, h_pairs, h_stacked, partial = refs
    frames, rows, cols, channels = own.shape
    width, rest = cols + TILE, channels - LANES
    every, beside = slice(0, cols), slice(cols, width)
    clear((lo, pairs, stacked, h_lo, h_pairs, h_stacked))
    whole = Packed(HALO, rows, cols)

    @if_earlier
    def build():
        for f in range(HALO):
            for r in range(rows):
                fill(lo, pairs, stacked, f, r + HALO, every, *whole.read(block, f, r, rest))
                fill(lo, pairs, stacked, f, r + HALO, beside, *whole.read_beside(block, f, r, rest))

    for f in range(frames):
        for r in range(rows):
            cells = own[f, r]
            fill(lo, pairs, stacked, HALO + f, r + HALO, every, cells[:, :LANES], cells[:, LANES:])
            fill(lo, pairs, stacked, HALO + f, r + HALO, beside, *own_beside(neighbour, f, r, cols))
    start, count = safe_rows(strips, rows)
    lefts = jnp.concatenate([columns(all_taps(t), lo, pairs, stacked, start, count) for t in range(frames)], axis=0)
    products = convolve(all_taps(0), [plane, middle, last], lefts)
    gain = gains[...]
    for t in range(frames):
        for r in range(count):
            h = hidden_row(join(products, (t * count + r) * width, width), gain, cols).astype(jnp.bfloat16)
            fill(h_lo, h_pairs, h_stacked, t, start + r, slice(0, width), h[:, :LANES], h[:, LANES:])
    (start, count), _ = safe_sums(strips, rows)
    if count:
        partial_sums(frames, (h_lo, h_pairs, h_stacked), w2, start, count, rows, cols, partial)


def edge_kernel(strips, rows, cols, *refs):
    *refs, near_lo, near_pairs, near_stacked = refs
    *refs, h_lo, h_pairs, h_stacked, partial = refs
    *edges, block, edge_sums, safe_lo, safe_pairs, safe_stacked, safe_partial, plane, middle, gains, w2 = refs
    frames, channels = edge_sums.shape[1], edge_sums.shape[-1]
    width, rest = cols + TILE, channels - LANES
    strip = lax.axis_index("strip")
    whole, strip_block = Packed(HALO, rows, cols), Packed(frames, HALO, cols)
    near = (near_lo, near_pairs, near_stacked)
    clear(near)
    for target, source in zip((h_lo, h_pairs, h_stacked, partial), (safe_lo, safe_pairs, safe_stacked, safe_partial)):
        target[...] = source[...]
    gain = gains[...]
    for group, (edge, top) in enumerate(zip(edges, at_top(strips))):

        def own_row(f, r):
            low = pl.multiple_of((f * rows + r) * cols, TILE)
            high = pl.multiple_of(whole.high + (f * (rows // 2) + r // 2) * cols, TILE)
            pair = block[pl.ds(high, cols), :]
            return block[pl.ds(low, cols), :], pair, *beside_from(block, whole.beside, (f * rows + r) * HALO, rest)

        def halo_row(f, j):
            sent = frames - HALO + f
            return *strip_block.read(edge, sent, j, rest), *strip_block.read_beside(edge, sent, j, rest)

        def own_half(f, r, j):
            low, pair, *tile = own_row(f, r)
            return low, pair[:, (j % 2) * rest : (j % 2 + 1) * rest], *tile

        @if_earlier
        def build():
            every, beside = slice(0, cols), slice(cols, width)
            for f in range(HALO):
                for j in range(HALO):
                    mine = own_half(f, (1 - top) * (rows - HALO) + j, j)
                    for cells, row in ((mine, HALO * top + j), (halo_row(f, j), HALO * (1 - top) + j)):
                        fill(*near, f, row, every, *cells[:2])
                        fill(*near, f, row, beside, *cells[2:])

        for t in range(frames):
            taps = earlier_taps(t)
            products = convolve(taps, [plane, middle], columns(taps, *near, 0, HALO)) if taps else None
            for r in range(HALO):
                y = edge_sums[group, t, r]
                if taps:
                    y = y + join(products, r * width, width)
                h = hidden_row(y, gain, cols)
                if strips != 2 and r == 1 - top:
                    h = h * jnp.where(strip == (0 if top else strips - 1), 0.0, 1.0)
                h = h.astype(jnp.bfloat16)
                row = (1 - top) * rows + r
                fill(h_lo, h_pairs, h_stacked, t, row, slice(0, width), h[:, :LANES], h[:, LANES:])

    _, (start, count) = safe_sums(strips, rows)
    partial_sums(frames, (h_lo, h_pairs, h_stacked), w2, start, count, rows, cols, partial)


def second_kernel(frames, rows, cols, h_lo, h_pairs, h_stacked, w2, out):
    width = cols + TILE
    for t in range(frames):
        taps = [(f, f - t + 2) for f in range(max(0, t - 2), t + 1)]
        products = convolve(taps, [w2.at[a] for a in range(3)], columns(taps, h_lo, h_pairs, h_stacked, 0, rows))
        for r in range(rows):
            out[t, r] = join(products, r * width, width)[:cols]


def finish_kernel(partial, own, gains, out_far, out, left):
    frames, rows, cols, channels = out.shape
    rest = channels - LANES
    gain = gains[...]

    copies = [pltpu.make_async_copy(out.at[t], out_far.at[t], left.at[t]) for t in range(frames)]
    for t in range(frames):
        for r in range(rows):
            y = own[t, r]
            if t < HALO:
                half = r % 2
                high = partial[t, rows + r // 2, :, half * rest : (half + 1) * rest]
                sent = jnp.concatenate([partial[t, r], high], axis=-1)
                y = y + sent.astype(jnp.float32)
            out[t, r] = activate(y, gain).astype(jnp.bfloat16)
        copies[t].start()
    for copy in copies:
        copy.wait()


def call(kernel, name, ins, outs, scratch=(), semaphores=0, flops=0, far=(), far_out=False):
    near, away = pl.BlockSpec(memory_space=pltpu.VMEM), pl.BlockSpec(memory_space=pltpu.HBM)
    in_specs, ins = [near] * len(ins), list(ins)
    for place in far:
        ins[place] = pltpu.with_memory_space_constraint(ins[place], pltpu.HBM)
        in_specs[place] = away
    one = not isinstance(outs, list)
    return pl.pallas_call(
        kernel,
        out_shape=outs,
        in_specs=in_specs,
        out_specs=(away if far_out else near) if one else [near] * len(outs),
        scratch_shapes=[pltpu.VMEM(shape, jnp.bfloat16) for shape in scratch]
        + [pltpu.SemaphoreType.DMA((semaphores,))] * (semaphores > 0),
        compiler_params=pltpu.CompilerParams(vmem_limit_bytes=24 * 1024 * 1024),
        cost_estimate=pl.CostEstimate(flops=flops, bytes_accessed=4 * 1024 * 1024, transcendentals=0),
        name=name,
    )(*ins)


def block_scratch(frames, rows, width):
    return [(frames, rows, width, LANES), (frames, rows + 1, width, LANES), (frames - 1, rows, width, LANES)]


def shards(frames_in, weight_first, scale_first, weight_second, scale_second):
    frames, rows, cols, channels = frames_in.shape
    strips = lax.axis_size("strip")
    width = cols + TILE
    flops = frames * rows * cols * 27 * channels * channels
    bf16 = functools.partial(jax.ShapeDtypeStruct, dtype=jnp.bfloat16)
    f32 = functools.partial(jax.ShapeDtypeStruct, dtype=jnp.float32)

    plane_shape = bf16(weight_first.shape[1:])
    neighbour = swap(frames_in, "slab")
    own_in, middle, last = call(
        stage_kernel,
        "stage",
        [frames_in, weight_first],
        [bf16(frames_in.shape), plane_shape, plane_shape],
        semaphores=3,
        far=[0, 1],
    )
    edge_shape = bf16(Packed(frames, HALO, cols).shape)
    block, *edges = call(
        functools.partial(pack_kernel, strips),
        "pack",
        [own_in, neighbour],
        [bf16(Packed(HALO, rows, cols).shape)] + [edge_shape] * (1 if strips == 2 else 2),
    )
    ups = [(i, i + 1) for i in range(strips - 1)]
    downs = [(i + 1, i) for i in range(strips - 1)]
    ways = [[(0, 1), (1, 0)]] if strips == 2 else [ups, downs]
    before = forward(block)
    own_edges = [lax.ppermute(edge, "strip", way) for edge, way in zip(edges, ways)]
    before_edges = [forward(edge, way) for edge, way in zip(edges, ways)]
    edge_sums, plane = call(
        functools.partial(edge_own_kernel, strips),
        "edge_rows_own",
        [own_in, neighbour, *own_edges, middle, last, weight_first],
        [f32((len(ways), frames, HALO, width, channels)), plane_shape],
        block_scratch(frames, 2 * HALO, width),
        semaphores=1,
        flops=flops // 4,
        far=[-1],
    )
    gain_first = scale_first[None]
    h_shapes = [bf16(shape) for shape in block_scratch(frames, rows + 2, width)]
    partial_shape = bf16((HALO, rows + rows // 2, cols, LANES))
    safe = call(
        functools.partial(safe_kernel, strips),
        "safe_rows",
        [own_in, neighbour, before, plane, middle, last, gain_first, weight_second],
        h_shapes + [partial_shape],
        block_scratch(HALO + frames, rows + 2 * HALO, width),
        flops=flops,
    )
    h_lo, h_pairs, h_stacked, partial = call(
        functools.partial(edge_kernel, strips, rows, cols),
        "edge_rows",
        [*before_edges, before, edge_sums, *safe, plane, middle, gain_first, weight_second],
        h_shapes + [partial_shape],
        block_scratch(HALO, 2 * HALO, width),
        flops=flops,
    )
    sent = forward(partial)
    own = call(
        functools.partial(second_kernel, frames, rows, cols),
        "second_layer",
        [h_lo, h_pairs, h_stacked, weight_second],
        f32((frames, rows, cols, channels)),
        flops=flops,
    )
    out = bf16(frames_in.shape)
    return call(
        finish_kernel,
        "finish",
        [sent, own, scale_second[None]],
        out,
        [out.shape],
        semaphores=frames,
        far_out=True,
    )


def solution(mesh):
    return jax.shard_map(
        shards,
        mesh=mesh,
        in_specs=(P(("groups", "frame"), "strip", "slab", None), P(), P(), P(), P()),
        out_specs=P(("groups", "frame"), "strip", "slab", None),
        check_vma=False,
    )
```

```python
import functools

import jax
import jax.numpy as jnp
from jax import lax
from jax.experimental import pallas as pl
from jax.experimental.pallas import tpu as pltpu
from jax.sharding import PartitionSpec as P

LANES = 128
TILE = 16
EPS = 1e-06


HALO = 2


def swap(x, axis):
    return lax.ppermute(x, axis, [(0, 1), (1, 0)])


def forward(x, way=None):
    steps, count = lax.axis_size("frame"), lax.axis_size("strip")
    way = [(i, i) for i in range(count)] if way is None else way
    pairs = [(f * count + i, (f + 1) * count + j) for f in range(steps - 1) for i, j in way]
    return lax.ppermute(x, ("frame", "strip"), pairs)


def if_earlier(build):
    pl.when(lax.axis_index("frame") > 0)(build)


class Packed:
    def __init__(self, frames, rows, cols):
        self.frames, self.rows, self.cols = frames, rows, cols
        self.high = frames * rows * cols
        self.beside = self.high + frames * (rows // 2) * cols
        self.tiles = -(-frames * rows * HALO // TILE)
        self.shape = (self.beside + 2 * self.tiles * TILE, LANES)

    def low_at(self, f, r):
        return slice((f * self.rows + r) * self.cols, (f * self.rows + r + 1) * self.cols)

    def high_at(self, f, r):
        start = self.high + (f * (self.rows // 2) + r // 2) * self.cols
        return slice(start, start + self.cols)

    def spot(self, f, r):
        cell = (f * self.rows + r) * HALO
        return cell // TILE, cell % TILE

    def beside_at(self, tile, high):
        start = self.beside + (2 * tile + high) * TILE
        return slice(start, start + TILE)

    def write(self, out, cells, tile_of):
        slab = lax.axis_index("slab")
        at = lax.broadcasted_iota(jnp.int32, (TILE, 1), 0)
        sums = [None] * self.tiles
        for f in range(self.frames):
            for r in range(self.rows):
                row = cells(f, r)
                out[self.low_at(f, r), :] = row[:, :LANES]
                rest = row.shape[-1] - LANES
                half = slice((r % 2) * rest, (r % 2 + 1) * rest)
                out[self.high_at(f, r), half] = row[:, LANES:]
                tile, place = self.spot(f, r)
                moved = pltpu.roll(tile_of(f, r).astype(jnp.float32), lax.rem(place + HALO * slab, TILE), 0)
                moved = jnp.where((at >= place) & (at < place + HALO), moved, 0.0)
                sums[tile] = moved if sums[tile] is None else sums[tile] + moved
        for tile, cells_beside in enumerate(sums):
            cells_beside = cells_beside.astype(jnp.bfloat16)
            out[self.beside_at(tile, 0), :] = cells_beside[:, :LANES]
            out[self.beside_at(tile, 1), :rest] = cells_beside[:, LANES:]

    def read(self, ref, f, r, rest):
        half = slice((r % 2) * rest, (r % 2 + 1) * rest)
        return ref[self.low_at(f, r), :], ref[self.high_at(f, r), half]

    def read_beside(self, ref, f, r, rest):
        return beside_from(ref, self.beside, (f * self.rows + r) * HALO, rest)


def beside_from(ref, start, cell, rest):
    slab = lax.axis_index("slab")
    parts = []
    for high, lanes in ((0, LANES), (1, rest)):
        at = start + (2 * (cell // TILE) + high) * TILE
        cells = ref[pl.ds(pl.multiple_of(at, TILE), TILE), :].astype(jnp.float32)
        cells = pltpu.roll(cells, lax.rem(2 * TILE - cell % TILE - HALO * slab, TILE), 0)
        parts.append(only_beside(cells).astype(jnp.bfloat16)[:, :lanes])
    return parts


def only_beside(tile):
    slab = lax.axis_index("slab")
    at = lax.broadcasted_iota(jnp.int32, tile.shape, 0)
    begin = slab * (TILE - HALO)
    return jnp.where((at >= begin) & (at < begin + HALO), tile, 0.0)


def fill(lo, pairs, stacked, frame, row, cols, low, high):
    rest = high.shape[-1]
    lo[frame, row, cols, :] = low
    pairs[frame, row + 1, cols, :rest] = high
    pairs[frame, row, cols, rest:] = high
    if frame < stacked.shape[0]:
        stacked[frame, row, cols, :rest] = high
    if frame > 0:
        stacked[frame - 1, row, cols, rest:] = high


def columns(taps, lo, pairs, stacked, row, rows):
    def flat(block):
        return block.reshape(-1, LANES)

    pieces = [flat(lo[f, pl.ds(row + b, rows)]) for f, _ in taps for b in range(3)]
    pieces += [flat(pairs[f, pl.ds(row + 1, rows)]) for f, _ in taps]
    for k in range(0, len(taps), 2):
        f = taps[k][0]
        if k + 1 < len(taps):
            pieces.append(flat(stacked[f, pl.ds(row + 2, rows)]))
        else:
            pieces.append(flat(pairs[f, pl.ds(row + 3, rows)]))
    return jnp.concatenate(pieces, axis=-1)


def planes(taps, weight, c):
    pieces = [weight[a][b, c, :LANES, :] for _, a in taps for b in range(3)]
    for _, a in taps:
        pieces += [weight[a][0, c, LANES:, :], weight[a][1, c, LANES:, :]]
    for _, a in taps:
        pieces.append(weight[a][2, c, LANES:, :])
    if len(taps) % 2:
        pieces.append(jnp.zeros_like(weight[a][0, c, LANES:, :]))
    return jnp.concatenate(pieces, axis=0)


def convolve(taps, weight, lefts):
    return [
        jnp.dot(lefts, planes(taps, weight, c), preferred_element_type=jnp.float32)
        for c in range(3)
    ]


def join(products, start, width):
    before, middle, after = [p[start : start + width] for p in products]
    return pltpu.roll(before, 1, 0) + middle + pltpu.roll(after, width - 1, 0)


def activate(y, gains):
    mean_square = jnp.sum(y * y, axis=-1, keepdims=True) * (1.0 / y.shape[-1])
    v = y * lax.rsqrt(mean_square + EPS) * gains
    return v / (1.0 + jnp.exp(-v))


def clear(buffers):
    for buffer in buffers:
        buffer[...] = jnp.zeros_like(buffer)


def clear_rows(buffers, above, below):
    lo, pairs, stacked = buffers
    for buffer, rows in ((lo, (above, below)), (pairs, (above, above + 1, below, below + 1)), (stacked, (above, below))):
        for row in rows:
            buffer[:, row] = jnp.zeros(buffer.shape[:1] + buffer.shape[2:], buffer.dtype)


def facing(strips, rows):
    if strips == 2:
        return [jnp.where(lax.axis_index("strip") == 0, rows - HALO, 0)]
    return [rows - HALO, 0]


def at_top(strips):
    return [lax.axis_index("strip")] if strips == 2 else [1, 0]


def safe_rows(strips, rows):
    return (1 + lax.axis_index("strip"), rows - 1) if strips == 2 else (2, rows - 2)


def beside_of(neighbour, f, r, cols):
    start = pl.multiple_of(lax.axis_index("slab") * (cols - TILE), TILE)
    return neighbour[f, r, pl.ds(start, TILE), :]


def stage_kernel(own_far, weight_far, own, middle, last, arrived):
    copies = [
        pltpu.make_async_copy(own_far, own, arrived.at[0]),
        pltpu.make_async_copy(weight_far.at[2], last, arrived.at[1]),
        pltpu.make_async_copy(weight_far.at[1], middle, arrived.at[2]),
    ]
    for copy in copies:
        copy.start()
    for copy in copies:
        copy.wait()


def pack_kernel(strips, own, neighbour, block, *edges):
    frames, rows, cols, _ = own.shape
    whole = Packed(HALO, rows, cols)
    skip = frames - HALO
    whole.write(block, lambda f, r: own[f + skip, r], lambda f, r: beside_of(neighbour, f + skip, r, cols))
    for start, edge in zip(facing(strips, rows), edges):
        Packed(frames, HALO, cols).write(
            edge, lambda f, r: own[f, start + r], lambda f, r: beside_of(neighbour, f, start + r, cols)
        )


def own_beside(neighbour, f, r, cols):
    tile = only_beside(beside_of(neighbour, f, r, cols).astype(jnp.float32)).astype(jnp.bfloat16)
    return tile[:, :LANES], tile[:, LANES:]


def window(buffers, frames, top, rows, cols, own, halo):
    every, beside = slice(0, cols), slice(cols, cols + TILE)
    for f in range(frames):
        for j in range(HALO):
            for cells, row in ((own(f, (1 - top) * (rows - HALO) + j), HALO * top + j), (halo(f, j), HALO * (1 - top) + j)):
                fill(*buffers, f, row, every, *cells[:2])
                fill(*buffers, f, row, beside, *cells[2:])


def edge_own_kernel(strips, *refs):
    *refs, near_lo, near_pairs, near_stacked, arrived = refs
    own, neighbour, *edges, middle, last, weight_far, edge_sums, plane = refs
    frames, rows, cols, channels = own.shape
    width, rest = cols + TILE, channels - LANES
    copy = pltpu.make_async_copy(weight_far.at[0], plane, arrived.at[0])
    copy.start()
    if frames > 2:
        copy.wait()
    strip_block = Packed(frames, HALO, cols)
    near = (near_lo, near_pairs, near_stacked)
    clear((near_pairs,))
    for group, (edge, top) in enumerate(zip(edges, at_top(strips))):

        def own_row(f, r):
            cells = own[f, r]
            return cells[:, :LANES], cells[:, LANES:], *own_beside(neighbour, f, r, cols)

        def halo_row(f, j):
            return *strip_block.read(edge, f, j, rest), *strip_block.read_beside(edge, f, j, rest)

        window(near, frames, top, rows, cols, own_row, halo_row)
        for t in range(frames):
            taps = own_taps(t)
            products = convolve(taps, [plane, middle, last], columns(taps, *near, 0, HALO))
            for r in range(HALO):
                edge_sums[group, t, r] = join(products, r * width, width)
    if frames <= 2:
        copy.wait()


def own_taps(t):
    return [(f, f - t + 2) for f in range(max(0, t - 2), t + 1)]


def earlier_taps(t):
    return [(f, f - t) for f in range(t, HALO)]


def hidden_row(y, gain, cols):
    width, slab = y.shape[0], lax.axis_index("slab")
    position = lax.broadcasted_iota(jnp.int32, (width, 1), 0)
    right = cols + (slab == 0).astype(jnp.int32)
    left = width - (slab == 1).astype(jnp.int32)
    return jnp.where((position < right) | (position >= left), activate(y, gain), 0.0)


def all_taps(t):
    return [(t, 0), (t + 1, 1), (t + 2, 2)]


def partial_sums(frames, hidden, w2, rows, cols, partial):
    width, last = cols + TILE, frames - 1
    for t, taps in enumerate(([(last - 1, 0), (last, 1)], [(last, 0)])):
        products = convolve(taps, w2, columns(taps, *hidden, 0, rows))
        for r in range(rows):
            y = join(products, r * width, width)[:cols].astype(jnp.bfloat16)
            rest = y.shape[-1] - LANES
            partial[t, r] = y[:, :LANES]
            half = slice((r % 2) * rest, (r % 2 + 1) * rest)
            partial[t, rows + r // 2, :, half] = y[:, LANES:]


def safe_kernel(strips, *refs):
    *refs, lo, pairs, stacked, arrived = refs
    own, neighbour, block, plane, middle, last, gains, w2_far, h_lo, h_pairs, h_stacked, *w2 = refs
    copies = [pltpu.make_async_copy(w2_far.at[a], w2[a], arrived.at[a]) for a in range(3)]
    for copy in copies:
        copy.start()
    frames, rows, cols, channels = own.shape
    width, rest = cols + TILE, channels - LANES
    every, beside = slice(0, cols), slice(cols, width)
    clear_rows((lo, pairs, stacked), HALO - 1, HALO + rows)
    clear_rows((h_lo, h_pairs, h_stacked), 0, rows + 1)
    whole = Packed(HALO, rows, cols)

    @pl.when(lax.axis_index("frame") == 0)
    def none_earlier():
        for buffer in (lo, pairs, stacked):
            buffer[:HALO] = jnp.zeros((HALO,) + buffer.shape[1:], buffer.dtype)

    @if_earlier
    def build():
        for f in range(HALO):
            for r in range(rows):
                fill(lo, pairs, stacked, f, r + HALO, every, *whole.read(block, f, r, rest))
                fill(lo, pairs, stacked, f, r + HALO, beside, *whole.read_beside(block, f, r, rest))

    for f in range(frames):
        for r in range(rows):
            cells = own[f, r]
            fill(lo, pairs, stacked, HALO + f, r + HALO, every, cells[:, :LANES], cells[:, LANES:])
            fill(lo, pairs, stacked, HALO + f, r + HALO, beside, *own_beside(neighbour, f, r, cols))
    start, count = safe_rows(strips, rows)
    lefts = jnp.concatenate([columns(all_taps(t), lo, pairs, stacked, start, count) for t in range(frames)], axis=0)
    products = convolve(all_taps(0), [plane, middle, last], lefts)
    gain = gains[...]
    for t in range(frames):
        for r in range(count):
            h = hidden_row(join(products, (t * count + r) * width, width), gain, cols).astype(jnp.bfloat16)
            fill(h_lo, h_pairs, h_stacked, t, start + r, slice(0, width), h[:, :LANES], h[:, LANES:])
    for copy in copies:
        copy.wait()


def edge_kernel(strips, rows, cols, *refs):
    *refs, near_lo, near_pairs, near_stacked = refs
    *refs, h_lo, h_pairs, h_stacked, partial = refs
    *edges, block, edge_sums, safe_lo, safe_pairs, safe_stacked, plane, middle, gains, w2_first, w2_middle = refs
    frames, channels = edge_sums.shape[1], edge_sums.shape[-1]
    width, rest = cols + TILE, channels - LANES
    strip = lax.axis_index("strip")
    whole, strip_block = Packed(HALO, rows, cols), Packed(frames, HALO, cols)
    near = (near_lo, near_pairs, near_stacked)
    clear(near)
    for target, source in zip((h_lo, h_pairs, h_stacked), (safe_lo, safe_pairs, safe_stacked)):
        target[...] = source[...]
    gain = gains[...]
    for group, (edge, top) in enumerate(zip(edges, at_top(strips))):

        def own_row(f, r):
            low = pl.multiple_of((f * rows + r) * cols, TILE)
            high = pl.multiple_of(whole.high + (f * (rows // 2) + r // 2) * cols, TILE)
            pair = block[pl.ds(high, cols), :]
            return block[pl.ds(low, cols), :], pair, *beside_from(block, whole.beside, (f * rows + r) * HALO, rest)

        def halo_row(f, j):
            sent = frames - HALO + f
            return *strip_block.read(edge, sent, j, rest), *strip_block.read_beside(edge, sent, j, rest)

        def own_half(f, r, j):
            low, pair, *tile = own_row(f, r)
            return low, pair[:, (j % 2) * rest : (j % 2 + 1) * rest], *tile

        @if_earlier
        def build():
            every, beside = slice(0, cols), slice(cols, width)
            for f in range(HALO):
                for j in range(HALO):
                    mine = own_half(f, (1 - top) * (rows - HALO) + j, j)
                    for cells, row in ((mine, HALO * top + j), (halo_row(f, j), HALO * (1 - top) + j)):
                        fill(*near, f, row, every, *cells[:2])
                        fill(*near, f, row, beside, *cells[2:])

        for t in range(frames):
            taps = earlier_taps(t)
            products = convolve(taps, [plane, middle], columns(taps, *near, 0, HALO)) if taps else None
            for r in range(HALO):
                y = edge_sums[group, t, r]
                if taps:
                    y = y + join(products, r * width, width)
                h = hidden_row(y, gain, cols)
                if strips != 2 and r == 1 - top:
                    h = h * jnp.where(strip == (0 if top else strips - 1), 0.0, 1.0)
                h = h.astype(jnp.bfloat16)
                row = (1 - top) * rows + r
                fill(h_lo, h_pairs, h_stacked, t, row, slice(0, width), h[:, :LANES], h[:, LANES:])

    partial_sums(frames, (h_lo, h_pairs, h_stacked), [w2_first, w2_middle], rows, cols, partial)


def second_kernel(frames, rows, cols, h_lo, h_pairs, h_stacked, *refs):
    *w2, out = refs
    width = cols + TILE
    for t in range(frames):
        taps = [(f, f - t + 2) for f in range(max(0, t - 2), t + 1)]
        products = convolve(taps, w2, columns(taps, h_lo, h_pairs, h_stacked, 0, rows))
        for r in range(rows):
            out[t, r] = join(products, r * width, width)[:cols]


def finish_kernel(partial, own, gains, out_far, out, left):
    frames, rows, cols, channels = out.shape
    rest = channels - LANES
    gain = gains[...]

    copies = [pltpu.make_async_copy(out.at[t], out_far.at[t], left.at[t]) for t in range(frames)]
    for t in range(frames):
        for r in range(rows):
            y = own[t, r]
            if t < HALO:
                half = r % 2
                high = partial[t, rows + r // 2, :, half * rest : (half + 1) * rest]
                sent = jnp.concatenate([partial[t, r], high], axis=-1)
                y = y + sent.astype(jnp.float32)
            out[t, r] = activate(y, gain).astype(jnp.bfloat16)
        copies[t].start()
    for copy in copies:
        copy.wait()


def call(kernel, name, ins, outs, scratch=(), semaphores=0, flops=0, far=(), far_out=False):
    near, away = pl.BlockSpec(memory_space=pltpu.VMEM), pl.BlockSpec(memory_space=pltpu.HBM)
    in_specs, ins = [near] * len(ins), list(ins)
    for place in far:
        ins[place] = pltpu.with_memory_space_constraint(ins[place], pltpu.HBM)
        in_specs[place] = away
    one = not isinstance(outs, list)
    return pl.pallas_call(
        kernel,
        out_shape=outs,
        in_specs=in_specs,
        out_specs=(away if far_out else near) if one else [near] * len(outs),
        scratch_shapes=[pltpu.VMEM(shape, jnp.bfloat16) for shape in scratch]
        + [pltpu.SemaphoreType.DMA((semaphores,))] * (semaphores > 0),
        compiler_params=pltpu.CompilerParams(vmem_limit_bytes=24 * 1024 * 1024),
        cost_estimate=pl.CostEstimate(flops=flops, bytes_accessed=4 * 1024 * 1024, transcendentals=0),
        name=name,
    )(*ins)


def block_scratch(frames, rows, width):
    return [(frames, rows, width, LANES), (frames, rows + 1, width, LANES), (frames - 1, rows, width, LANES)]


def shards(frames_in, weight_first, scale_first, weight_second, scale_second):
    frames, rows, cols, channels = frames_in.shape
    strips = lax.axis_size("strip")
    width = cols + TILE
    flops = frames * rows * cols * 27 * channels * channels
    bf16 = functools.partial(jax.ShapeDtypeStruct, dtype=jnp.bfloat16)
    f32 = functools.partial(jax.ShapeDtypeStruct, dtype=jnp.float32)

    plane_shape = bf16(weight_first.shape[1:])
    neighbour = swap(frames_in, "slab")
    own_in, middle, last = call(
        stage_kernel,
        "stage",
        [frames_in, weight_first],
        [bf16(frames_in.shape), plane_shape, plane_shape],
        semaphores=3,
        far=[0, 1],
    )
    edge_shape = bf16(Packed(frames, HALO, cols).shape)
    block, *edges = call(
        functools.partial(pack_kernel, strips),
        "pack",
        [own_in, neighbour],
        [bf16(Packed(HALO, rows, cols).shape)] + [edge_shape] * (1 if strips == 2 else 2),
    )
    ups = [(i, i + 1) for i in range(strips - 1)]
    downs = [(i + 1, i) for i in range(strips - 1)]
    ways = [[(0, 1), (1, 0)]] if strips == 2 else [ups, downs]
    before = forward(block)
    own_edges = [lax.ppermute(edge, "strip", way) for edge, way in zip(edges, ways)]
    before_edges = [forward(edge, way) for edge, way in zip(edges, ways)]
    edge_sums, plane = call(
        functools.partial(edge_own_kernel, strips),
        "edge_rows_own",
        [own_in, neighbour, *own_edges, middle, last, weight_first],
        [f32((len(ways), frames, HALO, width, channels)), plane_shape],
        block_scratch(frames, 2 * HALO, width),
        semaphores=1,
        flops=flops // 4,
        far=[-1],
    )
    gain_first = scale_first[None]
    h_shapes = [bf16(shape) for shape in block_scratch(frames, rows + 2, width)]
    partial_shape = bf16((HALO, rows + rows // 2, cols, LANES))
    *safe, w2_first, w2_middle, w2_last = call(
        functools.partial(safe_kernel, strips),
        "safe_rows",
        [own_in, neighbour, before, plane, middle, last, gain_first, weight_second],
        h_shapes + [plane_shape] * 3,
        block_scratch(HALO + frames, rows + 2 * HALO, width),
        semaphores=3,
        flops=flops,
        far=[-1],
    )
    h_lo, h_pairs, h_stacked, partial = call(
        functools.partial(edge_kernel, strips, rows, cols),
        "edge_rows",
        [*before_edges, before, edge_sums, *safe, plane, middle, gain_first, w2_first, w2_middle],
        h_shapes + [partial_shape],
        block_scratch(HALO, 2 * HALO, width),
        flops=flops,
    )
    sent = forward(partial)
    own = call(
        functools.partial(second_kernel, frames, rows, cols),
        "second_layer",
        [h_lo, h_pairs, h_stacked, w2_first, w2_middle, w2_last],
        f32((frames, rows, cols, channels)),
        flops=flops,
    )
    out = bf16(frames_in.shape)
    return call(
        finish_kernel,
        "finish",
        [sent, own, scale_second[None]],
        out,
        [out.shape],
        semaphores=frames,
        far_out=True,
    )


def solution(mesh):
    return jax.shard_map(
        shards,
        mesh=mesh,
        in_specs=(P(("groups", "frame"), "strip", "slab", None), P(), P(), P(), P()),
        out_specs=P(("groups", "frame"), "strip", "slab", None),
        check_vma=False,
    )
```

```python
import functools

import jax
import jax.numpy as jnp
from jax import lax
from jax.experimental import pallas as pl
from jax.experimental.pallas import tpu as pltpu
from jax.sharding import PartitionSpec as P

LANES = 128
TILE = 16
EPS = 1e-06


HALO = 2


def swap(x, axis):
    return lax.ppermute(x, axis, [(0, 1), (1, 0)])


def forward(x, way=None):
    steps, count = lax.axis_size("frame"), lax.axis_size("strip")
    way = [(i, i) for i in range(count)] if way is None else way
    pairs = [(f * count + i, (f + 1) * count + j) for f in range(steps - 1) for i, j in way]
    return lax.ppermute(x, ("frame", "strip"), pairs)


def if_earlier(build):
    pl.when(lax.axis_index("frame") > 0)(build)


class Packed:
    def __init__(self, frames, rows, cols):
        self.frames, self.rows, self.cols = frames, rows, cols
        self.high = frames * rows * cols
        self.beside = self.high + frames * (rows // 2) * cols
        self.tiles = -(-frames * rows * HALO // TILE)
        self.shape = (self.beside + 2 * self.tiles * TILE, LANES)

    def low_at(self, f, r):
        return slice((f * self.rows + r) * self.cols, (f * self.rows + r + 1) * self.cols)

    def high_at(self, f, r):
        start = self.high + (f * (self.rows // 2) + r // 2) * self.cols
        return slice(start, start + self.cols)

    def spot(self, f, r):
        cell = (f * self.rows + r) * HALO
        return cell // TILE, cell % TILE

    def beside_at(self, tile, high):
        start = self.beside + (2 * tile + high) * TILE
        return slice(start, start + TILE)

    def write(self, out, cells, tile_of):
        slab = lax.axis_index("slab")
        at = lax.broadcasted_iota(jnp.int32, (TILE, 1), 0)
        sums = [None] * self.tiles
        for f in range(self.frames):
            for r in range(self.rows):
                row = cells(f, r)
                out[self.low_at(f, r), :] = row[:, :LANES]
                rest = row.shape[-1] - LANES
                half = slice((r % 2) * rest, (r % 2 + 1) * rest)
                out[self.high_at(f, r), half] = row[:, LANES:]
                tile, place = self.spot(f, r)
                moved = pltpu.roll(tile_of(f, r).astype(jnp.float32), lax.rem(place + HALO * slab, TILE), 0)
                moved = jnp.where((at >= place) & (at < place + HALO), moved, 0.0)
                sums[tile] = moved if sums[tile] is None else sums[tile] + moved
        for tile, cells_beside in enumerate(sums):
            cells_beside = cells_beside.astype(jnp.bfloat16)
            out[self.beside_at(tile, 0), :] = cells_beside[:, :LANES]
            out[self.beside_at(tile, 1), :rest] = cells_beside[:, LANES:]

    def read(self, ref, f, r, rest):
        half = slice((r % 2) * rest, (r % 2 + 1) * rest)
        return ref[self.low_at(f, r), :], ref[self.high_at(f, r), half]

    def read_beside(self, ref, f, r, rest):
        return beside_from(ref, self.beside, (f * self.rows + r) * HALO, rest)


def beside_from(ref, start, cell, rest):
    slab = lax.axis_index("slab")
    parts = []
    for high, lanes in ((0, LANES), (1, rest)):
        at = start + (2 * (cell // TILE) + high) * TILE
        cells = ref[pl.ds(pl.multiple_of(at, TILE), TILE), :].astype(jnp.float32)
        cells = pltpu.roll(cells, lax.rem(2 * TILE - cell % TILE - HALO * slab, TILE), 0)
        parts.append(only_beside(cells).astype(jnp.bfloat16)[:, :lanes])
    return parts


def only_beside(tile):
    slab = lax.axis_index("slab")
    at = lax.broadcasted_iota(jnp.int32, tile.shape, 0)
    begin = slab * (TILE - HALO)
    return jnp.where((at >= begin) & (at < begin + HALO), tile, 0.0)


def fill(lo, pairs, stacked, frame, row, cols, low, high):
    rest = high.shape[-1]
    lo[frame, row, cols, :] = low
    pairs[frame, row + 1, cols, :rest] = high
    pairs[frame, row, cols, rest:] = high
    if frame < stacked.shape[0]:
        stacked[frame, row, cols, :rest] = high
    if frame > 0:
        stacked[frame - 1, row, cols, rest:] = high


def columns(taps, lo, pairs, stacked, row, rows):
    def flat(block):
        return block.reshape(-1, LANES)

    pieces = [flat(lo[f, pl.ds(row + b, rows)]) for f, _ in taps for b in range(3)]
    pieces += [flat(pairs[f, pl.ds(row + 1, rows)]) for f, _ in taps]
    for k in range(0, len(taps), 2):
        f = taps[k][0]
        if k + 1 < len(taps):
            pieces.append(flat(stacked[f, pl.ds(row + 2, rows)]))
        else:
            pieces.append(flat(pairs[f, pl.ds(row + 3, rows)]))
    return jnp.concatenate(pieces, axis=-1)


def planes(taps, weight, c):
    pieces = [weight[a][b, c, :LANES, :] for _, a in taps for b in range(3)]
    for _, a in taps:
        pieces += [weight[a][0, c, LANES:, :], weight[a][1, c, LANES:, :]]
    for _, a in taps:
        pieces.append(weight[a][2, c, LANES:, :])
    if len(taps) % 2:
        pieces.append(jnp.zeros_like(weight[a][0, c, LANES:, :]))
    return jnp.concatenate(pieces, axis=0)


def convolve(taps, weight, lefts):
    return [
        jnp.dot(lefts, planes(taps, weight, c), preferred_element_type=jnp.float32)
        for c in range(3)
    ]


def join(products, start, width):
    before, middle, after = [p[start : start + width] for p in products]
    return pltpu.roll(before, 1, 0) + middle + pltpu.roll(after, width - 1, 0)


def activate(y, gains):
    mean_square = jnp.sum(y * y, axis=-1, keepdims=True) * (1.0 / y.shape[-1])
    v = y * lax.rsqrt(mean_square + EPS) * gains
    return v / (1.0 + jnp.exp(-v))


def clear(buffers):
    for buffer in buffers:
        buffer[...] = jnp.zeros_like(buffer)


def clear_rows(buffers, above, below):
    lo, pairs, stacked = buffers
    for buffer, rows in ((lo, (above, below)), (pairs, (above, above + 1, below, below + 1)), (stacked, (above, below))):
        for row in rows:
            buffer[:, row] = jnp.zeros(buffer.shape[:1] + buffer.shape[2:], buffer.dtype)


def facing(strips, rows):
    if strips == 2:
        return [jnp.where(lax.axis_index("strip") == 0, rows - HALO, 0)]
    return [rows - HALO, 0]


def at_top(strips):
    return [lax.axis_index("strip")] if strips == 2 else [1, 0]


def safe_rows(strips, rows):
    return (1 + lax.axis_index("strip"), rows - 1) if strips == 2 else (2, rows - 2)


def beside_of(neighbour, f, r, cols):
    start = pl.multiple_of(lax.axis_index("slab") * (cols - TILE), TILE)
    return neighbour[f, r, pl.ds(start, TILE), :]


def stage_kernel(own_far, weight_far, own, middle, last, arrived):
    copies = [
        pltpu.make_async_copy(own_far, own, arrived.at[0]),
        pltpu.make_async_copy(weight_far.at[2], last, arrived.at[1]),
        pltpu.make_async_copy(weight_far.at[1], middle, arrived.at[2]),
    ]
    for copy in copies:
        copy.start()
    for copy in copies:
        copy.wait()


def pack_kernel(strips, own, neighbour, block, *edges):
    frames, rows, cols, _ = own.shape
    whole = Packed(HALO, rows, cols)
    skip = frames - HALO
    whole.write(block, lambda f, r: own[f + skip, r], lambda f, r: beside_of(neighbour, f + skip, r, cols))
    for start, edge in zip(facing(strips, rows), edges):
        Packed(frames, HALO, cols).write(
            edge, lambda f, r: own[f, start + r], lambda f, r: beside_of(neighbour, f, start + r, cols)
        )


def own_beside(neighbour, f, r, cols):
    tile = only_beside(beside_of(neighbour, f, r, cols).astype(jnp.float32)).astype(jnp.bfloat16)
    return tile[:, :LANES], tile[:, LANES:]


def window(buffers, frames, top, rows, cols, own, halo):
    every, beside = slice(0, cols), slice(cols, cols + TILE)
    for f in range(frames):
        found = []
        for j in range(HALO):
            found.append((HALO * top + j, own(f, (1 - top) * (rows - HALO) + j)))
            found.append((HALO * (1 - top) + j, halo(f, j)))
        for row, cells in found:
            fill(*buffers, f, row, every, *cells[:2])
            fill(*buffers, f, row, beside, *cells[2:])


def edge_own_kernel(strips, *refs):
    *refs, near_lo, near_pairs, near_stacked, arrived = refs
    own, neighbour, *edges, middle, last, weight_far, edge_sums, plane = refs
    frames, rows, cols, channels = own.shape
    width, rest = cols + TILE, channels - LANES
    copy = pltpu.make_async_copy(weight_far.at[0], plane, arrived.at[0])
    copy.start()
    if frames > 2:
        copy.wait()
    strip_block = Packed(frames, HALO, cols)
    near = (near_lo, near_pairs, near_stacked)
    clear((near_pairs,))
    for group, (edge, top) in enumerate(zip(edges, at_top(strips))):

        def own_row(f, r):
            cells = own[f, r]
            return cells[:, :LANES], cells[:, LANES:], *own_beside(neighbour, f, r, cols)

        def halo_row(f, j):
            return *strip_block.read(edge, f, j, rest), *strip_block.read_beside(edge, f, j, rest)

        window(near, frames, top, rows, cols, own_row, halo_row)
        for t in range(frames):
            taps = own_taps(t)
            products = convolve(taps, [plane, middle, last], columns(taps, *near, 0, HALO))
            for r in range(HALO):
                edge_sums[group, t, r] = join(products, r * width, width)
    if frames <= 2:
        copy.wait()


def own_taps(t):
    return [(f, f - t + 2) for f in range(max(0, t - 2), t + 1)]


def earlier_taps(t):
    return [(f, f - t) for f in range(t, HALO)]


def hidden_row(y, gain, cols):
    width, slab = y.shape[0], lax.axis_index("slab")
    position = lax.broadcasted_iota(jnp.int32, (width, 1), 0)
    right = cols + (slab == 0).astype(jnp.int32)
    left = width - (slab == 1).astype(jnp.int32)
    return jnp.where((position < right) | (position >= left), activate(y, gain), 0.0)


def all_taps(t):
    return [(t, 0), (t + 1, 1), (t + 2, 2)]


def partial_sums(frames, hidden, w2, rows, cols, partial):
    width, last = cols + TILE, frames - 1
    for t, taps in enumerate(([(last - 1, 0), (last, 1)], [(last, 0)])):
        products = convolve(taps, w2, columns(taps, *hidden, 0, rows))
        for r in range(rows):
            y = join(products, r * width, width)[:cols].astype(jnp.bfloat16)
            rest = y.shape[-1] - LANES
            partial[t, r] = y[:, :LANES]
            half = slice((r % 2) * rest, (r % 2 + 1) * rest)
            partial[t, rows + r // 2, :, half] = y[:, LANES:]


def safe_kernel(strips, *refs):
    *refs, lo, pairs, stacked, arrived = refs
    own, neighbour, block, plane, middle, last, gains, w2_far, h_lo, h_pairs, h_stacked, *w2 = refs
    copies = [pltpu.make_async_copy(w2_far.at[a], w2[a], arrived.at[a]) for a in range(3)]
    for copy in copies:
        copy.start()
    frames, rows, cols, channels = own.shape
    width, rest = cols + TILE, channels - LANES
    every, beside = slice(0, cols), slice(cols, width)
    clear_rows((lo, pairs, stacked), HALO - 1, HALO + rows)
    clear_rows((h_lo, h_pairs, h_stacked), 0, rows + 1)
    whole = Packed(HALO, rows, cols)

    @pl.when(lax.axis_index("frame") == 0)
    def none_earlier():
        for buffer in (lo, pairs, stacked):
            buffer[:HALO] = jnp.zeros((HALO,) + buffer.shape[1:], buffer.dtype)

    def put(frame, rows_of):
        for r, cells in enumerate(rows_of):
            fill(lo, pairs, stacked, frame, r + HALO, every, *cells[:2])
            fill(lo, pairs, stacked, frame, r + HALO, beside, *cells[2:])

    @if_earlier
    def build():
        for f in range(HALO):
            put(f, [(*whole.read(block, f, r, rest), *whole.read_beside(block, f, r, rest)) for r in range(rows)])

    for f in range(frames):
        cells = [own[f, r] for r in range(rows)]
        tiles = [own_beside(neighbour, f, r, cols) for r in range(rows)]
        put(HALO + f, [(c[:, :LANES], c[:, LANES:], *tile) for c, tile in zip(cells, tiles)])
    start, count = safe_rows(strips, rows)
    lefts = jnp.concatenate([columns(all_taps(t), lo, pairs, stacked, start, count) for t in range(frames)], axis=0)
    products = convolve(all_taps(0), [plane, middle, last], lefts)
    gain = gains[...]
    for t in range(frames):
        for r in range(count):
            h = hidden_row(join(products, (t * count + r) * width, width), gain, cols).astype(jnp.bfloat16)
            fill(h_lo, h_pairs, h_stacked, t, start + r, slice(0, width), h[:, :LANES], h[:, LANES:])
    for copy in copies:
        copy.wait()


def edge_kernel(strips, rows, cols, *refs):
    *refs, near_lo, near_pairs, near_stacked = refs
    *refs, h_lo, h_pairs, h_stacked, partial = refs
    *edges, block, edge_sums, safe_lo, safe_pairs, safe_stacked, plane, middle, gains, w2_first, w2_middle = refs
    frames, channels = edge_sums.shape[1], edge_sums.shape[-1]
    width, rest = cols + TILE, channels - LANES
    strip = lax.axis_index("strip")
    whole, strip_block = Packed(HALO, rows, cols), Packed(frames, HALO, cols)
    near = (near_lo, near_pairs, near_stacked)
    clear(near)
    for target, source in zip((h_lo, h_pairs, h_stacked), (safe_lo, safe_pairs, safe_stacked)):
        target[...] = source[...]
    gain = gains[...]
    for group, (edge, top) in enumerate(zip(edges, at_top(strips))):

        def own_row(f, r):
            low = pl.multiple_of((f * rows + r) * cols, TILE)
            high = pl.multiple_of(whole.high + (f * (rows // 2) + r // 2) * cols, TILE)
            pair = block[pl.ds(high, cols), :]
            return block[pl.ds(low, cols), :], pair, *beside_from(block, whole.beside, (f * rows + r) * HALO, rest)

        def halo_row(f, j):
            sent = frames - HALO + f
            return *strip_block.read(edge, sent, j, rest), *strip_block.read_beside(edge, sent, j, rest)

        def own_half(f, r, j):
            low, pair, *tile = own_row(f, r)
            return low, pair[:, (j % 2) * rest : (j % 2 + 1) * rest], *tile

        @if_earlier
        def build():
            every, beside = slice(0, cols), slice(cols, width)
            found = []
            for f in range(HALO):
                for j in range(HALO):
                    mine = own_half(f, (1 - top) * (rows - HALO) + j, j)
                    found += [(f, HALO * top + j, mine), (f, HALO * (1 - top) + j, halo_row(f, j))]
            for f, row, cells in found:
                fill(*near, f, row, every, *cells[:2])
                fill(*near, f, row, beside, *cells[2:])

        sums = [[edge_sums[group, t, r] for r in range(HALO)] for t in range(frames)]
        found = []
        for t in range(frames):
            taps = earlier_taps(t)
            products = convolve(taps, [plane, middle], columns(taps, *near, 0, HALO)) if taps else None
            for r in range(HALO):
                y = sums[t][r]
                if taps:
                    y = y + join(products, r * width, width)
                h = hidden_row(y, gain, cols)
                if strips != 2 and r == 1 - top:
                    h = h * jnp.where(strip == (0 if top else strips - 1), 0.0, 1.0)
                found.append((t, (1 - top) * rows + r, h.astype(jnp.bfloat16)))
        for t, row, h in found:
            fill(h_lo, h_pairs, h_stacked, t, row, slice(0, width), h[:, :LANES], h[:, LANES:])

    partial_sums(frames, (h_lo, h_pairs, h_stacked), [w2_first, w2_middle], rows, cols, partial)


def second_kernel(frames, rows, cols, h_lo, h_pairs, h_stacked, *refs):
    *w2, out = refs
    width = cols + TILE
    for t in range(frames):
        taps = [(f, f - t + 2) for f in range(max(0, t - 2), t + 1)]
        products = convolve(taps, w2, columns(taps, h_lo, h_pairs, h_stacked, 0, rows))
        for r in range(rows):
            out[t, r] = join(products, r * width, width)[:cols]


def finish_kernel(partial, own, gains, out_far, out, left):
    frames, rows, cols, channels = out.shape
    rest = channels - LANES
    gain = gains[...]

    sums = []
    for t in range(frames):
        y = own[t]
        if t < HALO:
            halves = [partial[t, rows + r // 2, :, (r % 2) * rest : (r % 2 + 1) * rest] for r in range(rows)]
            sent = [jnp.concatenate([partial[t, r], halves[r]], axis=-1) for r in range(rows)]
            y = y + jnp.stack(sent).astype(jnp.float32)
        sums.append(y.reshape(rows * cols, channels))
    results = [activate(y, gain).astype(jnp.bfloat16) for y in sums]
    copies = [pltpu.make_async_copy(out.at[t], out_far.at[t], left.at[t]) for t in range(frames)]
    for t in range(frames):
        out[t] = results[t].reshape(rows, cols, channels)
        copies[t].start()
    for copy in copies:
        copy.wait()


def call(kernel, name, ins, outs, scratch=(), semaphores=0, flops=0, far=(), far_out=False):
    near, away = pl.BlockSpec(memory_space=pltpu.VMEM), pl.BlockSpec(memory_space=pltpu.HBM)
    in_specs, ins = [near] * len(ins), list(ins)
    for place in far:
        ins[place] = pltpu.with_memory_space_constraint(ins[place], pltpu.HBM)
        in_specs[place] = away
    one = not isinstance(outs, list)
    return pl.pallas_call(
        kernel,
        out_shape=outs,
        in_specs=in_specs,
        out_specs=(away if far_out else near) if one else [near] * len(outs),
        scratch_shapes=[pltpu.VMEM(shape, jnp.bfloat16) for shape in scratch]
        + [pltpu.SemaphoreType.DMA((semaphores,))] * (semaphores > 0),
        compiler_params=pltpu.CompilerParams(vmem_limit_bytes=24 * 1024 * 1024),
        cost_estimate=pl.CostEstimate(flops=flops, bytes_accessed=4 * 1024 * 1024, transcendentals=0),
        name=name,
    )(*ins)


def block_scratch(frames, rows, width):
    return [(frames, rows, width, LANES), (frames, rows + 1, width, LANES), (frames - 1, rows, width, LANES)]


def shards(frames_in, weight_first, scale_first, weight_second, scale_second):
    frames, rows, cols, channels = frames_in.shape
    strips = lax.axis_size("strip")
    width = cols + TILE
    flops = frames * rows * cols * 27 * channels * channels
    bf16 = functools.partial(jax.ShapeDtypeStruct, dtype=jnp.bfloat16)
    f32 = functools.partial(jax.ShapeDtypeStruct, dtype=jnp.float32)

    plane_shape = bf16(weight_first.shape[1:])
    neighbour = swap(frames_in, "slab")
    own_in, middle, last = call(
        stage_kernel,
        "stage",
        [frames_in, weight_first],
        [bf16(frames_in.shape), plane_shape, plane_shape],
        semaphores=3,
        far=[0, 1],
    )
    edge_shape = bf16(Packed(frames, HALO, cols).shape)
    block, *edges = call(
        functools.partial(pack_kernel, strips),
        "pack",
        [own_in, neighbour],
        [bf16(Packed(HALO, rows, cols).shape)] + [edge_shape] * (1 if strips == 2 else 2),
    )
    ups = [(i, i + 1) for i in range(strips - 1)]
    downs = [(i + 1, i) for i in range(strips - 1)]
    ways = [[(0, 1), (1, 0)]] if strips == 2 else [ups, downs]
    before = forward(block)
    own_edges = [lax.ppermute(edge, "strip", way) for edge, way in zip(edges, ways)]
    before_edges = [forward(edge, way) for edge, way in zip(edges, ways)]
    edge_sums, plane = call(
        functools.partial(edge_own_kernel, strips),
        "edge_rows_own",
        [own_in, neighbour, *own_edges, middle, last, weight_first],
        [f32((len(ways), frames, HALO, width, channels)), plane_shape],
        block_scratch(frames, 2 * HALO, width),
        semaphores=1,
        flops=flops // 4,
        far=[-1],
    )
    gain_first = scale_first[None]
    h_shapes = [bf16(shape) for shape in block_scratch(frames, rows + 2, width)]
    partial_shape = bf16((HALO, rows + rows // 2, cols, LANES))
    *safe, w2_first, w2_middle, w2_last = call(
        functools.partial(safe_kernel, strips),
        "safe_rows",
        [own_in, neighbour, before, plane, middle, last, gain_first, weight_second],
        h_shapes + [plane_shape] * 3,
        block_scratch(HALO + frames, rows + 2 * HALO, width),
        semaphores=3,
        flops=flops,
        far=[-1],
    )
    h_lo, h_pairs, h_stacked, partial = call(
        functools.partial(edge_kernel, strips, rows, cols),
        "edge_rows",
        [*before_edges, before, edge_sums, *safe, plane, middle, gain_first, w2_first, w2_middle],
        h_shapes + [partial_shape],
        block_scratch(HALO, 2 * HALO, width),
        flops=flops,
    )
    sent = forward(partial)
    own = call(
        functools.partial(second_kernel, frames, rows, cols),
        "second_layer",
        [h_lo, h_pairs, h_stacked, w2_first, w2_middle, w2_last],
        f32((frames, rows, cols, channels)),
        flops=flops,
    )
    out = bf16(frames_in.shape)
    return call(
        finish_kernel,
        "finish",
        [sent, own, scale_second[None]],
        out,
        [out.shape],
        semaphores=frames,
        far_out=True,
    )


def solution(mesh):
    return jax.shard_map(
        shards,
        mesh=mesh,
        in_specs=(P(("groups", "frame"), "strip", "slab", None), P(), P(), P(), P()),
        out_specs=P(("groups", "frame"), "strip", "slab", None),
        check_vma=False,
    )
```

```python
import functools

import jax
import jax.numpy as jnp
from jax import lax
from jax.experimental import pallas as pl
from jax.experimental.pallas import tpu as pltpu
from jax.sharding import PartitionSpec as P

LANES = 128
TILE = 16
EPS = 1e-06


HALO = 2


def swap(x, axis):
    return lax.ppermute(x, axis, [(0, 1), (1, 0)])


def forward(x, way=None):
    steps, count = lax.axis_size("frame"), lax.axis_size("strip")
    way = [(i, i) for i in range(count)] if way is None else way
    pairs = [(f * count + i, (f + 1) * count + j) for f in range(steps - 1) for i, j in way]
    return lax.ppermute(x, ("frame", "strip"), pairs)


def if_earlier(build):
    pl.when(lax.axis_index("frame") > 0)(build)


class Packed:
    def __init__(self, frames, rows, cols):
        self.frames, self.rows, self.cols = frames, rows, cols
        self.high = frames * rows * cols
        self.beside = self.high + frames * (rows // 2) * cols
        self.tiles = -(-frames * rows * HALO // TILE)
        self.shape = (self.beside + 2 * self.tiles * TILE, LANES)

    def low_at(self, f, r):
        return slice((f * self.rows + r) * self.cols, (f * self.rows + r + 1) * self.cols)

    def high_at(self, f, r):
        start = self.high + (f * (self.rows // 2) + r // 2) * self.cols
        return slice(start, start + self.cols)

    def spot(self, f, r):
        cell = (f * self.rows + r) * HALO
        return cell // TILE, cell % TILE

    def beside_at(self, tile, high):
        start = self.beside + (2 * tile + high) * TILE
        return slice(start, start + TILE)

    def write(self, out, cells, tile_of):
        slab = lax.axis_index("slab")
        at = lax.broadcasted_iota(jnp.int32, (TILE, 1), 0)
        sums = [None] * self.tiles
        for f in range(self.frames):
            for r in range(self.rows):
                row = cells(f, r)
                out[self.low_at(f, r), :] = row[:, :LANES]
                rest = row.shape[-1] - LANES
                half = slice((r % 2) * rest, (r % 2 + 1) * rest)
                out[self.high_at(f, r), half] = row[:, LANES:]
                tile, place = self.spot(f, r)
                moved = pltpu.roll(tile_of(f, r).astype(jnp.float32), lax.rem(place + HALO * slab, TILE), 0)
                moved = jnp.where((at >= place) & (at < place + HALO), moved, 0.0)
                sums[tile] = moved if sums[tile] is None else sums[tile] + moved
        for tile, cells_beside in enumerate(sums):
            cells_beside = cells_beside.astype(jnp.bfloat16)
            out[self.beside_at(tile, 0), :] = cells_beside[:, :LANES]
            out[self.beside_at(tile, 1), :rest] = cells_beside[:, LANES:]

    def read(self, ref, f, r, rest):
        half = slice((r % 2) * rest, (r % 2 + 1) * rest)
        return ref[self.low_at(f, r), :], ref[self.high_at(f, r), half]

    def read_beside(self, ref, f, r, rest):
        return beside_from(ref, self.beside, (f * self.rows + r) * HALO, rest)


def beside_from(ref, start, cell, rest):
    slab = lax.axis_index("slab")
    parts = []
    for high, lanes in ((0, LANES), (1, rest)):
        at = start + (2 * (cell // TILE) + high) * TILE
        cells = ref[pl.ds(pl.multiple_of(at, TILE), TILE), :].astype(jnp.float32)
        cells = pltpu.roll(cells, lax.rem(2 * TILE - cell % TILE - HALO * slab, TILE), 0)
        parts.append(only_beside(cells).astype(jnp.bfloat16)[:, :lanes])
    return parts


def only_beside(tile):
    slab = lax.axis_index("slab")
    at = lax.broadcasted_iota(jnp.int32, tile.shape, 0)
    begin = slab * (TILE - HALO)
    return jnp.where((at >= begin) & (at < begin + HALO), tile, 0.0)


def fill(lo, pairs, stacked, frame, row, cols, low, high):
    rest = high.shape[-1]
    lo[frame, row, cols, :] = low
    pairs[frame, row + 1, cols, :rest] = high
    pairs[frame, row, cols, rest:] = high
    if frame < stacked.shape[0]:
        stacked[frame, row, cols, :rest] = high
    if frame > 0:
        stacked[frame - 1, row, cols, rest:] = high


def columns(taps, lo, pairs, stacked, row, rows):
    def flat(block):
        return block.reshape(-1, LANES)

    pieces = [flat(lo[f, pl.ds(row + b, rows)]) for f, _ in taps for b in range(3)]
    pieces += [flat(pairs[f, pl.ds(row + 1, rows)]) for f, _ in taps]
    for k in range(0, len(taps), 2):
        f = taps[k][0]
        if k + 1 < len(taps):
            pieces.append(flat(stacked[f, pl.ds(row + 2, rows)]))
        else:
            pieces.append(flat(pairs[f, pl.ds(row + 3, rows)]))
    return jnp.concatenate(pieces, axis=-1)


def planes(taps, weight, c):
    pieces = [weight[a][b, c, :LANES, :] for _, a in taps for b in range(3)]
    for _, a in taps:
        pieces += [weight[a][0, c, LANES:, :], weight[a][1, c, LANES:, :]]
    for _, a in taps:
        pieces.append(weight[a][2, c, LANES:, :])
    if len(taps) % 2:
        pieces.append(jnp.zeros_like(weight[a][0, c, LANES:, :]))
    return jnp.concatenate(pieces, axis=0)


def convolve(taps, weight, lefts):
    return [
        jnp.dot(lefts, planes(taps, weight, c), preferred_element_type=jnp.float32)
        for c in range(3)
    ]


def join(products, start, width):
    before, middle, after = [p[start : start + width] for p in products]
    return pltpu.roll(before, 1, 0) + middle + pltpu.roll(after, width - 1, 0)


def activate(y, gains):
    mean_square = jnp.sum(y * y, axis=-1, keepdims=True) * (1.0 / y.shape[-1])
    v = y * lax.rsqrt(mean_square + EPS) * gains
    return v / (1.0 + jnp.exp(-v))


def clear(buffers):
    for buffer in buffers:
        buffer[...] = jnp.zeros_like(buffer)


def clear_rows(buffers, above, below):
    lo, pairs, stacked = buffers
    for buffer, rows in ((lo, (above, below)), (pairs, (above, above + 1, below, below + 1)), (stacked, (above, below))):
        for row in rows:
            buffer[:, row] = jnp.zeros(buffer.shape[:1] + buffer.shape[2:], buffer.dtype)


def facing(strips, rows):
    if strips == 2:
        return [jnp.where(lax.axis_index("strip") == 0, rows - HALO, 0)]
    return [rows - HALO, 0]


def at_top(strips):
    return [lax.axis_index("strip")] if strips == 2 else [1, 0]


def safe_rows(strips, rows):
    return (1 + lax.axis_index("strip"), rows - 1) if strips == 2 else (2, rows - 2)


def beside_of(neighbour, f, r, cols):
    start = pl.multiple_of(lax.axis_index("slab") * (cols - TILE), TILE)
    return neighbour[f, r, pl.ds(start, TILE), :]


def stage_kernel(own_far, weight_far, own, middle, last, arrived):
    copies = [
        pltpu.make_async_copy(own_far, own, arrived.at[0]),
        pltpu.make_async_copy(weight_far.at[2], last, arrived.at[1]),
        pltpu.make_async_copy(weight_far.at[1], middle, arrived.at[2]),
    ]
    for copy in copies:
        copy.start()
    for copy in copies:
        copy.wait()


def pack_kernel(strips, own, neighbour, block, *edges):
    frames, rows, cols, _ = own.shape
    whole = Packed(HALO, rows, cols)
    skip = frames - HALO
    whole.write(block, lambda f, r: own[f + skip, r], lambda f, r: beside_of(neighbour, f + skip, r, cols))
    for start, edge in zip(facing(strips, rows), edges):
        Packed(frames, HALO, cols).write(
            edge, lambda f, r: own[f, start + r], lambda f, r: beside_of(neighbour, f, start + r, cols)
        )


def own_beside(neighbour, f, r, cols):
    tile = only_beside(beside_of(neighbour, f, r, cols).astype(jnp.float32)).astype(jnp.bfloat16)
    return tile[:, :LANES], tile[:, LANES:]


def window(buffers, frames, top, rows, cols, own, halo):
    every, beside = slice(0, cols), slice(cols, cols + TILE)
    for f in range(frames):
        found = []
        for j in range(HALO):
            found.append((HALO * top + j, own(f, (1 - top) * (rows - HALO) + j)))
            found.append((HALO * (1 - top) + j, halo(f, j)))
        for row, cells in found:
            fill(*buffers, f, row, every, *cells[:2])
            fill(*buffers, f, row, beside, *cells[2:])


def edge_own_kernel(strips, *refs):
    *refs, arrived = refs
    if strips == 2:
        *refs, edge = refs
        own, neighbour, gathered, middle, last, weight_far, edge_sums, plane, *near = refs
        landed = pltpu.make_async_copy(gathered.at[1 - lax.axis_index("strip")], edge, arrived.at[1])
        landed.start()
        edges = [edge]
    else:
        own, neighbour, *edges, middle, last, weight_far, edge_sums, plane, near_lo, near_pairs, near_stacked = refs
        near = [near_lo, near_pairs, near_stacked]
    frames, rows, cols, channels = own.shape
    width, rest = cols + TILE, channels - LANES
    copy = pltpu.make_async_copy(weight_far.at[0], plane, arrived.at[0])
    copy.start()
    if frames > 2:
        copy.wait()
    strip_block = Packed(frames, HALO, cols)
    clear((near[1],))
    if strips == 2:
        landed.wait()
    for group, (edge, top) in enumerate(zip(edges, at_top(strips))):

        def own_row(f, r):
            cells = own[f, r]
            return cells[:, :LANES], cells[:, LANES:], *own_beside(neighbour, f, r, cols)

        def halo_row(f, j):
            return *strip_block.read(edge, f, j, rest), *strip_block.read_beside(edge, f, j, rest)

        window(near, frames, top, rows, cols, own_row, halo_row)
        for t in range(frames):
            taps = own_taps(t)
            products = convolve(taps, [plane, middle, last], columns(taps, *near, 0, HALO))
            for r in range(HALO):
                edge_sums[group, t, r] = join(products, r * width, width)
    if frames <= 2:
        copy.wait()


def own_taps(t):
    return [(f, f - t + 2) for f in range(max(0, t - 2), t + 1)]


def earlier_taps(t):
    return [(f, f - t) for f in range(t, HALO)]


def hidden_row(y, gain, cols):
    width, slab = y.shape[0], lax.axis_index("slab")
    position = lax.broadcasted_iota(jnp.int32, (width, 1), 0)
    right = cols + (slab == 0).astype(jnp.int32)
    left = width - (slab == 1).astype(jnp.int32)
    return jnp.where((position < right) | (position >= left), activate(y, gain), 0.0)


def all_taps(t):
    return [(t, 0), (t + 1, 1), (t + 2, 2)]


def partial_sums(frames, hidden, w2, rows, cols, partial):
    width, last = cols + TILE, frames - 1
    for t, taps in enumerate(([(last - 1, 0), (last, 1)], [(last, 0)])):
        products = convolve(taps, w2, columns(taps, *hidden, 0, rows))
        for r in range(rows):
            y = join(products, r * width, width)[:cols].astype(jnp.bfloat16)
            rest = y.shape[-1] - LANES
            partial[t, r] = y[:, :LANES]
            half = slice((r % 2) * rest, (r % 2 + 1) * rest)
            partial[t, rows + r // 2, :, half] = y[:, LANES:]


def safe_kernel(strips, *refs):
    *refs, lo, pairs, stacked, arrived = refs
    own, neighbour, block, plane, middle, last, gains, w2_far, h_lo, h_pairs, h_stacked, *w2 = refs
    copies = [pltpu.make_async_copy(w2_far.at[a], w2[a], arrived.at[a]) for a in range(3)]
    for copy in copies:
        copy.start()
    frames, rows, cols, channels = own.shape
    width, rest = cols + TILE, channels - LANES
    every, beside = slice(0, cols), slice(cols, width)
    clear_rows((lo, pairs, stacked), HALO - 1, HALO + rows)
    clear_rows((h_lo, h_pairs, h_stacked), 0, rows + 1)
    whole = Packed(HALO, rows, cols)

    @pl.when(lax.axis_index("frame") == 0)
    def none_earlier():
        for buffer in (lo, pairs, stacked):
            buffer[:HALO] = jnp.zeros((HALO,) + buffer.shape[1:], buffer.dtype)

    def put(frame, rows_of):
        for r, cells in enumerate(rows_of):
            fill(lo, pairs, stacked, frame, r + HALO, every, *cells[:2])
            fill(lo, pairs, stacked, frame, r + HALO, beside, *cells[2:])

    @if_earlier
    def build():
        for f in range(HALO):
            put(f, [(*whole.read(block, f, r, rest), *whole.read_beside(block, f, r, rest)) for r in range(rows)])

    for f in range(frames):
        cells = [own[f, r] for r in range(rows)]
        tiles = [own_beside(neighbour, f, r, cols) for r in range(rows)]
        put(HALO + f, [(c[:, :LANES], c[:, LANES:], *tile) for c, tile in zip(cells, tiles)])
    start, count = safe_rows(strips, rows)
    lefts = jnp.concatenate([columns(all_taps(t), lo, pairs, stacked, start, count) for t in range(frames)], axis=0)
    products = convolve(all_taps(0), [plane, middle, last], lefts)
    gain = gains[...]
    for t in range(frames):
        for r in range(count):
            h = hidden_row(join(products, (t * count + r) * width, width), gain, cols).astype(jnp.bfloat16)
            fill(h_lo, h_pairs, h_stacked, t, start + r, slice(0, width), h[:, :LANES], h[:, LANES:])
    for copy in copies:
        copy.wait()


def edge_kernel(strips, rows, cols, *refs):
    *refs, near_lo, near_pairs, near_stacked = refs
    *refs, h_lo, h_pairs, h_stacked, partial = refs
    *edges, block, edge_sums, safe_lo, safe_pairs, safe_stacked, plane, middle, gains, w2_first, w2_middle = refs
    frames, channels = edge_sums.shape[1], edge_sums.shape[-1]
    width, rest = cols + TILE, channels - LANES
    strip = lax.axis_index("strip")
    whole, strip_block = Packed(HALO, rows, cols), Packed(frames, HALO, cols)
    near = (near_lo, near_pairs, near_stacked)
    clear(near)
    for target, source in zip((h_lo, h_pairs, h_stacked), (safe_lo, safe_pairs, safe_stacked)):
        target[...] = source[...]
    gain = gains[...]
    for group, (edge, top) in enumerate(zip(edges, at_top(strips))):

        def own_row(f, r):
            low = pl.multiple_of((f * rows + r) * cols, TILE)
            high = pl.multiple_of(whole.high + (f * (rows // 2) + r // 2) * cols, TILE)
            pair = block[pl.ds(high, cols), :]
            return block[pl.ds(low, cols), :], pair, *beside_from(block, whole.beside, (f * rows + r) * HALO, rest)

        def halo_row(f, j):
            sent = frames - HALO + f
            return *strip_block.read(edge, sent, j, rest), *strip_block.read_beside(edge, sent, j, rest)

        def own_half(f, r, j):
            low, pair, *tile = own_row(f, r)
            return low, pair[:, (j % 2) * rest : (j % 2 + 1) * rest], *tile

        @if_earlier
        def build():
            every, beside = slice(0, cols), slice(cols, width)
            found = []
            for f in range(HALO):
                for j in range(HALO):
                    mine = own_half(f, (1 - top) * (rows - HALO) + j, j)
                    found += [(f, HALO * top + j, mine), (f, HALO * (1 - top) + j, halo_row(f, j))]
            for f, row, cells in found:
                fill(*near, f, row, every, *cells[:2])
                fill(*near, f, row, beside, *cells[2:])

        sums = [[edge_sums[group, t, r] for r in range(HALO)] for t in range(frames)]
        found = []
        for t in range(frames):
            taps = earlier_taps(t)
            products = convolve(taps, [plane, middle], columns(taps, *near, 0, HALO)) if taps else None
            for r in range(HALO):
                y = sums[t][r]
                if taps:
                    y = y + join(products, r * width, width)
                h = hidden_row(y, gain, cols)
                if strips != 2 and r == 1 - top:
                    h = h * jnp.where(strip == (0 if top else strips - 1), 0.0, 1.0)
                found.append((t, (1 - top) * rows + r, h.astype(jnp.bfloat16)))
        for t, row, h in found:
            fill(h_lo, h_pairs, h_stacked, t, row, slice(0, width), h[:, :LANES], h[:, LANES:])

    partial_sums(frames, (h_lo, h_pairs, h_stacked), [w2_first, w2_middle], rows, cols, partial)


def second_kernel(frames, rows, cols, h_lo, h_pairs, h_stacked, *refs):
    *w2, out = refs
    width = cols + TILE
    for t in range(frames):
        taps = [(f, f - t + 2) for f in range(max(0, t - 2), t + 1)]
        products = convolve(taps, w2, columns(taps, h_lo, h_pairs, h_stacked, 0, rows))
        for r in range(rows):
            out[t, r] = join(products, r * width, width)[:cols]


def finish_kernel(partial, own, gains, out_far, out, left):
    frames, rows, cols, channels = out.shape
    rest = channels - LANES
    gain = gains[...]

    sums = []
    for t in range(frames):
        y = own[t]
        if t < HALO:
            halves = [partial[t, rows + r // 2, :, (r % 2) * rest : (r % 2 + 1) * rest] for r in range(rows)]
            sent = [jnp.concatenate([partial[t, r], halves[r]], axis=-1) for r in range(rows)]
            y = y + jnp.stack(sent).astype(jnp.float32)
        sums.append(y.reshape(rows * cols, channels))
    results = [activate(y, gain).astype(jnp.bfloat16) for y in sums]
    copies = [pltpu.make_async_copy(out.at[t], out_far.at[t], left.at[t]) for t in range(frames)]
    for t in range(frames):
        out[t] = results[t].reshape(rows, cols, channels)
        copies[t].start()
    for copy in copies:
        copy.wait()


def call(kernel, name, ins, outs, scratch=(), semaphores=0, flops=0, far=(), far_out=False):
    near, away = pl.BlockSpec(memory_space=pltpu.VMEM), pl.BlockSpec(memory_space=pltpu.HBM)
    in_specs, ins = [near] * len(ins), list(ins)
    for place in far:
        ins[place] = pltpu.with_memory_space_constraint(ins[place], pltpu.HBM)
        in_specs[place] = away
    one = not isinstance(outs, list)
    return pl.pallas_call(
        kernel,
        out_shape=outs,
        in_specs=in_specs,
        out_specs=(away if far_out else near) if one else [near] * len(outs),
        scratch_shapes=[pltpu.VMEM(shape, jnp.bfloat16) for shape in scratch]
        + [pltpu.SemaphoreType.DMA((semaphores,))] * (semaphores > 0),
        compiler_params=pltpu.CompilerParams(vmem_limit_bytes=24 * 1024 * 1024),
        cost_estimate=pl.CostEstimate(flops=flops, bytes_accessed=4 * 1024 * 1024, transcendentals=0),
        name=name,
    )(*ins)


def block_scratch(frames, rows, width):
    return [(frames, rows, width, LANES), (frames, rows + 1, width, LANES), (frames - 1, rows, width, LANES)]


def shards(frames_in, weight_first, scale_first, weight_second, scale_second):
    frames, rows, cols, channels = frames_in.shape
    strips = lax.axis_size("strip")
    width = cols + TILE
    flops = frames * rows * cols * 27 * channels * channels
    bf16 = functools.partial(jax.ShapeDtypeStruct, dtype=jnp.bfloat16)
    f32 = functools.partial(jax.ShapeDtypeStruct, dtype=jnp.float32)

    plane_shape = bf16(weight_first.shape[1:])
    neighbour = swap(frames_in, "slab")
    own_in, middle, last = call(
        stage_kernel,
        "stage",
        [frames_in, weight_first],
        [bf16(frames_in.shape), plane_shape, plane_shape],
        semaphores=3,
        far=[0, 1],
    )
    edge_shape = bf16(Packed(frames, HALO, cols).shape)
    block, *edges = call(
        functools.partial(pack_kernel, strips),
        "pack",
        [own_in, neighbour],
        [bf16(Packed(HALO, rows, cols).shape)] + [edge_shape] * (1 if strips == 2 else 2),
    )
    ups = [(i, i + 1) for i in range(strips - 1)]
    downs = [(i + 1, i) for i in range(strips - 1)]
    ways = [[(0, 1), (1, 0)]] if strips == 2 else [ups, downs]
    before = forward(block)
    if strips == 2:
        own_edges = [lax.all_gather(edges[0], "strip")]
    else:
        own_edges = [lax.ppermute(edge, "strip", way) for edge, way in zip(edges, ways)]
    before_edges = [forward(edge, way) for edge, way in zip(edges, ways)]
    edge_sums, plane = call(
        functools.partial(edge_own_kernel, strips),
        "edge_rows_own",
        [own_in, neighbour, *own_edges, middle, last, weight_first],
        [f32((len(ways), frames, HALO, width, channels)), plane_shape],
        block_scratch(frames, 2 * HALO, width) + [edge_shape.shape] * (strips == 2),
        semaphores=2,
        flops=flops // 4,
        far=[2, -1] if strips == 2 else [-1],
    )
    gain_first = scale_first[None]
    h_shapes = [bf16(shape) for shape in block_scratch(frames, rows + 2, width)]
    partial_shape = bf16((HALO, rows + rows // 2, cols, LANES))
    *safe, w2_first, w2_middle, w2_last = call(
        functools.partial(safe_kernel, strips),
        "safe_rows",
        [own_in, neighbour, before, plane, middle, last, gain_first, weight_second],
        h_shapes + [plane_shape] * 3,
        block_scratch(HALO + frames, rows + 2 * HALO, width),
        semaphores=3,
        flops=flops,
        far=[-1],
    )
    h_lo, h_pairs, h_stacked, partial = call(
        functools.partial(edge_kernel, strips, rows, cols),
        "edge_rows",
        [*before_edges, before, edge_sums, *safe, plane, middle, gain_first, w2_first, w2_middle],
        h_shapes + [partial_shape],
        block_scratch(HALO, 2 * HALO, width),
        flops=flops,
    )
    sent = forward(partial)
    own = call(
        functools.partial(second_kernel, frames, rows, cols),
        "second_layer",
        [h_lo, h_pairs, h_stacked, w2_first, w2_middle, w2_last],
        f32((frames, rows, cols, channels)),
        flops=flops,
    )
    out = bf16(frames_in.shape)
    return call(
        finish_kernel,
        "finish",
        [sent, own, scale_second[None]],
        out,
        [out.shape],
        semaphores=frames,
        far_out=True,
    )


def solution(mesh):
    return jax.shard_map(
        shards,
        mesh=mesh,
        in_specs=(P(("groups", "frame"), "strip", "slab", None), P(), P(), P(), P()),
        out_specs=P(("groups", "frame"), "strip", "slab", None),
        check_vma=False,
    )
```

```python
import functools

import jax
import jax.numpy as jnp
from jax import lax
from jax.experimental import pallas as pl
from jax.experimental.pallas import tpu as pltpu
from jax.sharding import PartitionSpec as P

LANES = 128
TILE = 16
EPS = 1e-06


HALO = 2


def swap(x, axis):
    return lax.ppermute(x, axis, [(0, 1), (1, 0)])


def forward(x, way=None):
    steps, count = lax.axis_size("frame"), lax.axis_size("strip")
    way = [(i, i) for i in range(count)] if way is None else way
    pairs = [(f * count + i, (f + 1) * count + j) for f in range(steps - 1) for i, j in way]
    return lax.ppermute(x, ("frame", "strip"), pairs)


def if_earlier(build):
    pl.when(lax.axis_index("frame") > 0)(build)


class Packed:
    def __init__(self, frames, rows, cols):
        self.frames, self.rows, self.cols = frames, rows, cols
        self.high = frames * rows * cols
        self.beside = self.high + frames * (rows // 2) * cols
        self.tiles = -(-frames * rows * HALO // TILE)
        self.shape = (self.beside + 2 * self.tiles * TILE, LANES)

    def low_at(self, f, r):
        return slice((f * self.rows + r) * self.cols, (f * self.rows + r + 1) * self.cols)

    def high_at(self, f, r):
        start = self.high + (f * (self.rows // 2) + r // 2) * self.cols
        return slice(start, start + self.cols)

    def spot(self, f, r):
        cell = (f * self.rows + r) * HALO
        return cell // TILE, cell % TILE

    def beside_at(self, tile, high):
        start = self.beside + (2 * tile + high) * TILE
        return slice(start, start + TILE)

    def write(self, out, cells, tile_of):
        slab = lax.axis_index("slab")
        at = lax.broadcasted_iota(jnp.int32, (TILE, 1), 0)
        sums = [None] * self.tiles
        for f in range(self.frames):
            for r in range(self.rows):
                row = cells(f, r)
                out[self.low_at(f, r), :] = row[:, :LANES]
                rest = row.shape[-1] - LANES
                half = slice((r % 2) * rest, (r % 2 + 1) * rest)
                out[self.high_at(f, r), half] = row[:, LANES:]
                tile, place = self.spot(f, r)
                moved = pltpu.roll(tile_of(f, r).astype(jnp.float32), lax.rem(place + HALO * slab, TILE), 0)
                moved = jnp.where((at >= place) & (at < place + HALO), moved, 0.0)
                sums[tile] = moved if sums[tile] is None else sums[tile] + moved
        for tile, cells_beside in enumerate(sums):
            cells_beside = cells_beside.astype(jnp.bfloat16)
            out[self.beside_at(tile, 0), :] = cells_beside[:, :LANES]
            out[self.beside_at(tile, 1), :rest] = cells_beside[:, LANES:]

    def read(self, ref, f, r, rest):
        half = slice((r % 2) * rest, (r % 2 + 1) * rest)
        return ref[self.low_at(f, r), :], ref[self.high_at(f, r), half]

    def read_beside(self, ref, f, r, rest):
        return beside_from(ref, self.beside, (f * self.rows + r) * HALO, rest)


def beside_from(ref, start, cell, rest):
    slab = lax.axis_index("slab")
    parts = []
    for high, lanes in ((0, LANES), (1, rest)):
        at = start + (2 * (cell // TILE) + high) * TILE
        cells = ref[pl.ds(pl.multiple_of(at, TILE), TILE), :].astype(jnp.float32)
        cells = pltpu.roll(cells, lax.rem(2 * TILE - cell % TILE - HALO * slab, TILE), 0)
        parts.append(only_beside(cells).astype(jnp.bfloat16)[:, :lanes])
    return parts


def only_beside(tile):
    slab = lax.axis_index("slab")
    at = lax.broadcasted_iota(jnp.int32, tile.shape, 0)
    begin = slab * (TILE - HALO)
    return jnp.where((at >= begin) & (at < begin + HALO), tile, 0.0)


def fill(lo, pairs, stacked, frame, row, cols, low, high):
    rest = high.shape[-1]
    lo[frame, row, cols, :] = low
    pairs[frame, row + 1, cols, :rest] = high
    pairs[frame, row, cols, rest:] = high
    if frame < stacked.shape[0]:
        stacked[frame, row, cols, :rest] = high
    if frame > 0:
        stacked[frame - 1, row, cols, rest:] = high


def columns(taps, lo, pairs, stacked, row, rows):
    def flat(block):
        return block.reshape(-1, LANES)

    pieces = [flat(lo[f, pl.ds(row + b, rows)]) for f, _ in taps for b in range(3)]
    pieces += [flat(pairs[f, pl.ds(row + 1, rows)]) for f, _ in taps]
    for k in range(0, len(taps), 2):
        f = taps[k][0]
        if k + 1 < len(taps):
            pieces.append(flat(stacked[f, pl.ds(row + 2, rows)]))
        else:
            pieces.append(flat(pairs[f, pl.ds(row + 3, rows)]))
    return jnp.concatenate(pieces, axis=-1)


def planes(taps, weight, c):
    pieces = [weight[a][b, c, :LANES, :] for _, a in taps for b in range(3)]
    for _, a in taps:
        pieces += [weight[a][0, c, LANES:, :], weight[a][1, c, LANES:, :]]
    for _, a in taps:
        pieces.append(weight[a][2, c, LANES:, :])
    if len(taps) % 2:
        pieces.append(jnp.zeros_like(weight[a][0, c, LANES:, :]))
    return jnp.concatenate(pieces, axis=0)


def convolve(taps, weight, lefts):
    return [
        jnp.dot(lefts, planes(taps, weight, c), preferred_element_type=jnp.float32)
        for c in range(3)
    ]


def join(products, start, width):
    before, middle, after = [p[start : start + width] for p in products]
    return pltpu.roll(before, 1, 0) + middle + pltpu.roll(after, width - 1, 0)


def activate(y, gains):
    mean_square = jnp.sum(y * y, axis=-1, keepdims=True) * (1.0 / y.shape[-1])
    v = y * lax.rsqrt(mean_square + EPS) * gains
    return v / (1.0 + jnp.exp(-v))


def clear(buffers):
    for buffer in buffers:
        buffer[...] = jnp.zeros_like(buffer)


def clear_rows(buffers, above, below):
    lo, pairs, stacked = buffers
    for buffer, rows in ((lo, (above, below)), (pairs, (above, above + 1, below, below + 1)), (stacked, (above, below))):
        for row in rows:
            buffer[:, row] = jnp.zeros(buffer.shape[:1] + buffer.shape[2:], buffer.dtype)


def facing(strips, rows):
    if strips == 2:
        return [jnp.where(lax.axis_index("strip") == 0, rows - HALO, 0)]
    return [rows - HALO, 0]


def at_top(strips):
    return [lax.axis_index("strip")] if strips == 2 else [1, 0]


def safe_rows(strips, rows):
    return (1 + lax.axis_index("strip"), rows - 1) if strips == 2 else (2, rows - 2)


def beside_of(neighbour, f, r, cols):
    start = pl.multiple_of(lax.axis_index("slab") * (cols - TILE), TILE)
    return neighbour[f, r, pl.ds(start, TILE), :]


def stage_kernel(own_far, weight_far, own, middle, last, arrived):
    copies = [
        pltpu.make_async_copy(own_far, own, arrived.at[0]),
        pltpu.make_async_copy(weight_far.at[2], last, arrived.at[1]),
        pltpu.make_async_copy(weight_far.at[1], middle, arrived.at[2]),
    ]
    for copy in copies:
        copy.start()
    for copy in copies:
        copy.wait()


def pack_kernel(strips, own, neighbour, block, *edges):
    frames, rows, cols, _ = own.shape
    whole = Packed(HALO, rows, cols)
    skip = frames - HALO
    whole.write(block, lambda f, r: own[f + skip, r], lambda f, r: beside_of(neighbour, f + skip, r, cols))
    for start, edge in zip(facing(strips, rows), edges):
        Packed(frames, HALO, cols).write(
            edge, lambda f, r: own[f, start + r], lambda f, r: beside_of(neighbour, f, start + r, cols)
        )


def own_beside(neighbour, f, r, cols):
    tile = only_beside(beside_of(neighbour, f, r, cols).astype(jnp.float32)).astype(jnp.bfloat16)
    return tile[:, :LANES], tile[:, LANES:]


def window(buffers, skip, frames, top, rows, cols, own, halo):
    every, beside = slice(0, cols), slice(cols, cols + TILE)
    for f in range(frames):
        found = []
        for j in range(HALO):
            found.append((HALO * top + j, own(f, (1 - top) * (rows - HALO) + j)))
            found.append((HALO * (1 - top) + j, halo(f, j)))
        for row, cells in found:
            fill(*buffers, skip + f, row, every, *cells[:2])
            fill(*buffers, skip + f, row, beside, *cells[2:])


def edge_own_kernel(strips, *refs):
    *refs, near_lo, near_pairs, near_stacked, arrived = refs
    own, neighbour, *edges, middle, last, weight_far, edge_sums, plane = refs
    frames, rows, cols, channels = own.shape
    width, rest = cols + TILE, channels - LANES
    copy = pltpu.make_async_copy(weight_far.at[0], plane, arrived.at[0])
    copy.start()
    if frames > 2:
        copy.wait()
    strip_block = Packed(frames, HALO, cols)
    near = (near_lo, near_pairs, near_stacked)
    span = min(frames, 3)
    zeros = span - 1
    clear((near_pairs,))
    for buffer in (near_lo, near_stacked):
        buffer[:zeros] = jnp.zeros((zeros,) + buffer.shape[1:], buffer.dtype)
    for group, (edge, top) in enumerate(zip(edges, at_top(strips))):

        def own_row(f, r):
            cells = own[f, r]
            return cells[:, :LANES], cells[:, LANES:], *own_beside(neighbour, f, r, cols)

        def halo_row(f, j):
            return *strip_block.read(edge, f, j, rest), *strip_block.read_beside(edge, f, j, rest)

        window(near, zeros, frames, top, rows, cols, own_row, halo_row)
        lefts = [columns([(t + k, 3 - span + k) for k in range(span)], *near, 0, HALO) for t in range(frames)]
        taps = [(k, 3 - span + k) for k in range(span)]
        products = convolve(taps, [plane, middle, last], jnp.concatenate(lefts, axis=0))
        for t in range(frames):
            for r in range(HALO):
                edge_sums[group, t, r] = join(products, (t * HALO + r) * width, width)
    if frames <= 2:
        copy.wait()


def own_taps(t):
    return [(f, f - t + 2) for f in range(max(0, t - 2), t + 1)]


def earlier_taps(t):
    return [(f, f - t) for f in range(t, HALO)]


def hidden_row(y, gain, cols):
    width, slab = y.shape[0], lax.axis_index("slab")
    position = lax.broadcasted_iota(jnp.int32, (width, 1), 0)
    right = cols + (slab == 0).astype(jnp.int32)
    left = width - (slab == 1).astype(jnp.int32)
    return jnp.where((position < right) | (position >= left), activate(y, gain), 0.0)


def all_taps(t):
    return [(t, 0), (t + 1, 1), (t + 2, 2)]


def partial_sums(frames, hidden, w2, rows, cols, partial):
    width, last = cols + TILE, frames - 1
    for t, taps in enumerate(([(last - 1, 0), (last, 1)], [(last, 0)])):
        products = convolve(taps, w2, columns(taps, *hidden, 0, rows))
        for r in range(rows):
            y = join(products, r * width, width)[:cols].astype(jnp.bfloat16)
            rest = y.shape[-1] - LANES
            partial[t, r] = y[:, :LANES]
            half = slice((r % 2) * rest, (r % 2 + 1) * rest)
            partial[t, rows + r // 2, :, half] = y[:, LANES:]


def safe_kernel(strips, *refs):
    *refs, lo, pairs, stacked, arrived = refs
    own, neighbour, block, plane, middle, last, gains, w2_far, h_lo, h_pairs, h_stacked, *w2 = refs
    copies = [pltpu.make_async_copy(w2_far.at[a], w2[a], arrived.at[a]) for a in range(3)]
    for copy in copies:
        copy.start()
    frames, rows, cols, channels = own.shape
    width, rest = cols + TILE, channels - LANES
    every, beside = slice(0, cols), slice(cols, width)
    clear_rows((lo, pairs, stacked), HALO - 1, HALO + rows)
    clear_rows((h_lo, h_pairs, h_stacked), 0, rows + 1)
    whole = Packed(HALO, rows, cols)

    @pl.when(lax.axis_index("frame") == 0)
    def none_earlier():
        for buffer in (lo, pairs, stacked):
            buffer[:HALO] = jnp.zeros((HALO,) + buffer.shape[1:], buffer.dtype)

    def put(frame, rows_of):
        for r, cells in enumerate(rows_of):
            fill(lo, pairs, stacked, frame, r + HALO, every, *cells[:2])
            fill(lo, pairs, stacked, frame, r + HALO, beside, *cells[2:])

    @if_earlier
    def build():
        for f in range(HALO):
            put(f, [(*whole.read(block, f, r, rest), *whole.read_beside(block, f, r, rest)) for r in range(rows)])

    for f in range(frames):
        cells = [own[f, r] for r in range(rows)]
        tiles = [own_beside(neighbour, f, r, cols) for r in range(rows)]
        put(HALO + f, [(c[:, :LANES], c[:, LANES:], *tile) for c, tile in zip(cells, tiles)])
    start, count = safe_rows(strips, rows)
    lefts = jnp.concatenate([columns(all_taps(t), lo, pairs, stacked, start, count) for t in range(frames)], axis=0)
    products = convolve(all_taps(0), [plane, middle, last], lefts)
    gain = gains[...]
    for t in range(frames):
        for r in range(count):
            h = hidden_row(join(products, (t * count + r) * width, width), gain, cols).astype(jnp.bfloat16)
            fill(h_lo, h_pairs, h_stacked, t, start + r, slice(0, width), h[:, :LANES], h[:, LANES:])
    for copy in copies:
        copy.wait()


def edge_kernel(strips, rows, cols, *refs):
    *refs, near_lo, near_pairs, near_stacked = refs
    *refs, h_lo, h_pairs, h_stacked, partial = refs
    *edges, block, edge_sums, safe_lo, safe_pairs, safe_stacked, plane, middle, gains, w2_first, w2_middle = refs
    frames, channels = edge_sums.shape[1], edge_sums.shape[-1]
    width, rest = cols + TILE, channels - LANES
    strip = lax.axis_index("strip")
    whole, strip_block = Packed(HALO, rows, cols), Packed(frames, HALO, cols)
    near = (near_lo, near_pairs, near_stacked)
    none = jnp.zeros(near_lo.shape[1:], near_lo.dtype)
    near_lo[HALO] = none
    near_stacked[HALO - 1] = none
    clear((near_pairs,))

    @pl.when(lax.axis_index("frame") == 0)
    def none_earlier():
        clear((near_lo, near_stacked))

    gain = gains[...]
    for group, (edge, top) in enumerate(zip(edges, at_top(strips))):

        def own_row(f, r):
            low = pl.multiple_of((f * rows + r) * cols, TILE)
            high = pl.multiple_of(whole.high + (f * (rows // 2) + r // 2) * cols, TILE)
            pair = block[pl.ds(high, cols), :]
            return block[pl.ds(low, cols), :], pair, *beside_from(block, whole.beside, (f * rows + r) * HALO, rest)

        def halo_row(f, j):
            sent = frames - HALO + f
            return *strip_block.read(edge, sent, j, rest), *strip_block.read_beside(edge, sent, j, rest)

        def own_half(f, r, j):
            low, pair, *tile = own_row(f, r)
            return low, pair[:, (j % 2) * rest : (j % 2 + 1) * rest], *tile

        @if_earlier
        def build():
            every, beside = slice(0, cols), slice(cols, width)
            found = []
            for f in range(HALO):
                for j in range(HALO):
                    mine = own_half(f, (1 - top) * (rows - HALO) + j, j)
                    found += [(f, HALO * top + j, mine), (f, HALO * (1 - top) + j, halo_row(f, j))]
            for f, row, cells in found:
                fill(*near, f, row, every, *cells[:2])
                fill(*near, f, row, beside, *cells[2:])

        sums = [[edge_sums[group, t, r] for r in range(HALO)] for t in range(frames)]
        found = []
        lefts = [columns([(t, 0), (t + 1, 1)], *near, 0, HALO) for t in range(HALO)]
        products = convolve([(0, 0), (1, 1)], [plane, middle], jnp.concatenate(lefts, axis=0))
        for t in range(frames):
            for r in range(HALO):
                y = sums[t][r]
                if t < HALO:
                    y = y + join(products, (t * HALO + r) * width, width)
                h = hidden_row(y, gain, cols)
                if strips != 2 and r == 1 - top:
                    h = h * jnp.where(strip == (0 if top else strips - 1), 0.0, 1.0)
                found.append((t, (1 - top) * rows + r, h.astype(jnp.bfloat16)))
        for t, row, h in found:
            fill(h_lo, h_pairs, h_stacked, t, row, slice(0, width), h[:, :LANES], h[:, LANES:])

    partial_sums(frames, (h_lo, h_pairs, h_stacked), [w2_first, w2_middle], rows, cols, partial)


def second_kernel(frames, rows, cols, h_lo, h_pairs, h_stacked, *refs):
    *w2, out = refs
    width = cols + TILE
    for t in range(frames):
        taps = [(f, f - t + 2) for f in range(max(0, t - 2), t + 1)]
        products = convolve(taps, w2, columns(taps, h_lo, h_pairs, h_stacked, 0, rows))
        for r in range(rows):
            out[t, r] = join(products, r * width, width)[:cols]


def finish_kernel(partial, own, gains, out_far, out, left):
    frames, rows, cols, channels = out.shape
    rest = channels - LANES
    gain = gains[...]

    sums = []
    for t in range(frames):
        y = own[t]
        if t < HALO:
            halves = [partial[t, rows + r // 2, :, (r % 2) * rest : (r % 2 + 1) * rest] for r in range(rows)]
            sent = [jnp.concatenate([partial[t, r], halves[r]], axis=-1) for r in range(rows)]
            y = y + jnp.stack(sent).astype(jnp.float32)
        sums.append(y.reshape(rows * cols, channels))
    results = [activate(y, gain).astype(jnp.bfloat16) for y in sums]
    copies = [pltpu.make_async_copy(out.at[t], out_far.at[t], left.at[t]) for t in range(frames)]
    for t in range(frames):
        out[t] = results[t].reshape(rows, cols, channels)
        copies[t].start()
    for copy in copies:
        copy.wait()


def call(kernel, name, ins, outs, scratch=(), semaphores=0, flops=0, far=(), far_out=False, alias=None):
    near, away = pl.BlockSpec(memory_space=pltpu.VMEM), pl.BlockSpec(memory_space=pltpu.HBM)
    in_specs, ins = [near] * len(ins), list(ins)
    for place in far:
        ins[place] = pltpu.with_memory_space_constraint(ins[place], pltpu.HBM)
        in_specs[place] = away
    one = not isinstance(outs, list)
    return pl.pallas_call(
        kernel,
        out_shape=outs,
        in_specs=in_specs,
        out_specs=(away if far_out else near) if one else [near] * len(outs),
        scratch_shapes=[pltpu.VMEM(shape, jnp.bfloat16) for shape in scratch]
        + [pltpu.SemaphoreType.DMA((semaphores,))] * (semaphores > 0),
        input_output_aliases=alias or {},
        compiler_params=pltpu.CompilerParams(vmem_limit_bytes=24 * 1024 * 1024),
        cost_estimate=pl.CostEstimate(flops=flops, bytes_accessed=4 * 1024 * 1024, transcendentals=0),
        name=name,
    )(*ins)


def block_scratch(frames, rows, width):
    return [(frames, rows, width, LANES), (frames, rows + 1, width, LANES), (frames - 1, rows, width, LANES)]


def shards(frames_in, weight_first, scale_first, weight_second, scale_second):
    frames, rows, cols, channels = frames_in.shape
    strips = lax.axis_size("strip")
    width = cols + TILE
    flops = frames * rows * cols * 27 * channels * channels
    bf16 = functools.partial(jax.ShapeDtypeStruct, dtype=jnp.bfloat16)
    f32 = functools.partial(jax.ShapeDtypeStruct, dtype=jnp.float32)

    plane_shape = bf16(weight_first.shape[1:])
    neighbour = swap(frames_in, "slab")
    own_in, middle, last = call(
        stage_kernel,
        "stage",
        [frames_in, weight_first],
        [bf16(frames_in.shape), plane_shape, plane_shape],
        semaphores=3,
        far=[0, 1],
    )
    edge_shape = bf16(Packed(frames, HALO, cols).shape)
    block, *edges = call(
        functools.partial(pack_kernel, strips),
        "pack",
        [own_in, neighbour],
        [bf16(Packed(HALO, rows, cols).shape)] + [edge_shape] * (1 if strips == 2 else 2),
    )
    ups = [(i, i + 1) for i in range(strips - 1)]
    downs = [(i + 1, i) for i in range(strips - 1)]
    ways = [[(0, 1), (1, 0)]] if strips == 2 else [ups, downs]
    before = forward(block)
    own_edges = [lax.ppermute(edge, "strip", way) for edge, way in zip(edges, ways)]
    before_edges = [forward(edge, way) for edge, way in zip(edges, ways)]
    edge_sums, plane = call(
        functools.partial(edge_own_kernel, strips),
        "edge_rows_own",
        [own_in, neighbour, *own_edges, middle, last, weight_first],
        [f32((len(ways), frames, HALO, width, channels)), plane_shape],
        block_scratch(frames + min(frames, 3) - 1, 2 * HALO, width),
        semaphores=1,
        flops=flops // 4,
        far=[-1],
    )
    gain_first = scale_first[None]
    h_shapes = [bf16(shape) for shape in block_scratch(frames, rows + 2, width)]
    partial_shape = bf16((HALO, rows + rows // 2, cols, LANES))
    *safe, w2_first, w2_middle, w2_last = call(
        functools.partial(safe_kernel, strips),
        "safe_rows",
        [own_in, neighbour, before, plane, middle, last, gain_first, weight_second],
        h_shapes + [plane_shape] * 3,
        block_scratch(HALO + frames, rows + 2 * HALO, width),
        semaphores=3,
        flops=flops,
        far=[-1],
    )
    h_lo, h_pairs, h_stacked, partial = call(
        functools.partial(edge_kernel, strips, rows, cols),
        "edge_rows",
        [*before_edges, before, edge_sums, *safe, plane, middle, gain_first, w2_first, w2_middle],
        h_shapes + [partial_shape],
        block_scratch(HALO + 1, 2 * HALO, width),
        flops=flops,
        alias={len(before_edges) + 2 + k: k for k in range(3)},
    )
    sent = forward(partial)
    own = call(
        functools.partial(second_kernel, frames, rows, cols),
        "second_layer",
        [h_lo, h_pairs, h_stacked, w2_first, w2_middle, w2_last],
        f32((frames, rows, cols, channels)),
        flops=flops,
    )
    out = bf16(frames_in.shape)
    return call(
        finish_kernel,
        "finish",
        [sent, own, scale_second[None]],
        out,
        [out.shape],
        semaphores=frames,
        far_out=True,
    )


def solution(mesh):
    return jax.shard_map(
        shards,
        mesh=mesh,
        in_specs=(P(("groups", "frame"), "strip", "slab", None), P(), P(), P(), P()),
        out_specs=P(("groups", "frame"), "strip", "slab", None),
        check_vma=False,
    )
```

```python
import functools

import jax
import jax.numpy as jnp
from jax import lax
from jax.experimental import pallas as pl
from jax.experimental.pallas import tpu as pltpu
from jax.sharding import PartitionSpec as P

LANES = 128
TILE = 16
EPS = 1e-06


HALO = 2


def swap(x, axis):
    return lax.ppermute(x, axis, [(0, 1), (1, 0)])


def forward(x, way=None):
    steps, count = lax.axis_size("frame"), lax.axis_size("strip")
    way = [(i, i) for i in range(count)] if way is None else way
    pairs = [(f * count + i, (f + 1) * count + j) for f in range(steps - 1) for i, j in way]
    return lax.ppermute(x, ("frame", "strip"), pairs)


def if_earlier(build):
    pl.when(lax.axis_index("frame") > 0)(build)


class Packed:
    def __init__(self, frames, rows, cols):
        self.frames, self.rows, self.cols = frames, rows, cols
        self.high = frames * rows * cols
        self.beside = self.high + frames * (rows // 2) * cols
        self.tiles = -(-frames * rows * HALO // TILE)
        self.shape = (self.beside + 2 * self.tiles * TILE, LANES)

    def low_at(self, f, r):
        return slice((f * self.rows + r) * self.cols, (f * self.rows + r + 1) * self.cols)

    def high_at(self, f, r):
        start = self.high + (f * (self.rows // 2) + r // 2) * self.cols
        return slice(start, start + self.cols)

    def spot(self, f, r):
        cell = (f * self.rows + r) * HALO
        return cell // TILE, cell % TILE

    def beside_at(self, tile, high):
        start = self.beside + (2 * tile + high) * TILE
        return slice(start, start + TILE)

    def write(self, out, cells, tile_of):
        slab = lax.axis_index("slab")
        at = lax.broadcasted_iota(jnp.int32, (TILE, 1), 0)
        sums = [None] * self.tiles
        for f in range(self.frames):
            for r in range(self.rows):
                row = cells(f, r)
                out[self.low_at(f, r), :] = row[:, :LANES]
                rest = row.shape[-1] - LANES
                half = slice((r % 2) * rest, (r % 2 + 1) * rest)
                out[self.high_at(f, r), half] = row[:, LANES:]
                tile, place = self.spot(f, r)
                moved = pltpu.roll(tile_of(f, r).astype(jnp.float32), lax.rem(place + HALO * slab, TILE), 0)
                moved = jnp.where((at >= place) & (at < place + HALO), moved, 0.0)
                sums[tile] = moved if sums[tile] is None else sums[tile] + moved
        for tile, cells_beside in enumerate(sums):
            cells_beside = cells_beside.astype(jnp.bfloat16)
            out[self.beside_at(tile, 0), :] = cells_beside[:, :LANES]
            out[self.beside_at(tile, 1), :rest] = cells_beside[:, LANES:]

    def read(self, ref, f, r, rest):
        half = slice((r % 2) * rest, (r % 2 + 1) * rest)
        return ref[self.low_at(f, r), :], ref[self.high_at(f, r), half]

    def read_beside(self, ref, f, r, rest):
        return beside_from(ref, self.beside, (f * self.rows + r) * HALO, rest)


def beside_from(ref, start, cell, rest):
    slab = lax.axis_index("slab")
    parts = []
    for high, lanes in ((0, LANES), (1, rest)):
        at = start + (2 * (cell // TILE) + high) * TILE
        cells = ref[pl.ds(pl.multiple_of(at, TILE), TILE), :].astype(jnp.float32)
        cells = pltpu.roll(cells, lax.rem(2 * TILE - cell % TILE - HALO * slab, TILE), 0)
        parts.append(only_beside(cells).astype(jnp.bfloat16)[:, :lanes])
    return parts


def only_beside(tile):
    slab = lax.axis_index("slab")
    at = lax.broadcasted_iota(jnp.int32, tile.shape, 0)
    begin = slab * (TILE - HALO)
    return jnp.where((at >= begin) & (at < begin + HALO), tile, 0.0)


def fill(lo, pairs, stacked, frame, row, cols, low, high):
    rest = high.shape[-1]
    lo[frame, row, cols, :] = low
    pairs[frame, row + 1, cols, :rest] = high
    pairs[frame, row, cols, rest:] = high
    if frame < stacked.shape[0]:
        stacked[frame, row, cols, :rest] = high
    if frame > 0:
        stacked[frame - 1, row, cols, rest:] = high


def columns(taps, lo, pairs, stacked, row, rows):
    def flat(block):
        return block.reshape(-1, LANES)

    pieces = [flat(lo[f, pl.ds(row + b, rows)]) for f, _ in taps for b in range(3)]
    pieces += [flat(pairs[f, pl.ds(row + 1, rows)]) for f, _ in taps]
    for k in range(0, len(taps), 2):
        f = taps[k][0]
        if k + 1 < len(taps):
            pieces.append(flat(stacked[f, pl.ds(row + 2, rows)]))
        else:
            pieces.append(flat(pairs[f, pl.ds(row + 3, rows)]))
    return jnp.concatenate(pieces, axis=-1)


def planes(taps, weight, c):
    pieces = [weight[a][b, c, :LANES, :] for _, a in taps for b in range(3)]
    for _, a in taps:
        pieces += [weight[a][0, c, LANES:, :], weight[a][1, c, LANES:, :]]
    for _, a in taps:
        pieces.append(weight[a][2, c, LANES:, :])
    if len(taps) % 2:
        pieces.append(jnp.zeros_like(weight[a][0, c, LANES:, :]))
    return jnp.concatenate(pieces, axis=0)


def convolve(taps, weight, lefts):
    return [
        jnp.dot(lefts, planes(taps, weight, c), preferred_element_type=jnp.float32)
        for c in range(3)
    ]


def join(products, start, width):
    before, middle, after = [p[start : start + width] for p in products]
    return pltpu.roll(before, 1, 0) + middle + pltpu.roll(after, width - 1, 0)


def activate(y, gains):
    mean_square = jnp.sum(y * y, axis=-1, keepdims=True) * (1.0 / y.shape[-1])
    v = y * lax.rsqrt(mean_square + EPS) * gains
    return v / (1.0 + jnp.exp(-v))


def clear(buffers):
    for buffer in buffers:
        buffer[...] = jnp.zeros_like(buffer)


def clear_rows(buffers, above, below):
    lo, pairs, stacked = buffers
    for buffer, rows in ((lo, (above, below)), (pairs, (above, above + 1, below, below + 1)), (stacked, (above, below))):
        for row in rows:
            buffer[:, row] = jnp.zeros(buffer.shape[:1] + buffer.shape[2:], buffer.dtype)


def facing(strips, rows):
    if strips == 2:
        return [jnp.where(lax.axis_index("strip") == 0, rows - HALO, 0)]
    return [rows - HALO, 0]


def at_top(strips):
    return [lax.axis_index("strip")] if strips == 2 else [1, 0]


def safe_rows(strips, rows):
    return (1 + lax.axis_index("strip"), rows - 1) if strips == 2 else (2, rows - 2)


def beside_of(neighbour, f, r, cols):
    start = pl.multiple_of(lax.axis_index("slab") * (cols - TILE), TILE)
    return neighbour[f, r, pl.ds(start, TILE), :]


def stage_kernel(own_far, weight_far, own, middle, last, arrived):
    copies = [
        pltpu.make_async_copy(own_far, own, arrived.at[0]),
        pltpu.make_async_copy(weight_far.at[2], last, arrived.at[1]),
        pltpu.make_async_copy(weight_far.at[1], middle, arrived.at[2]),
    ]
    for copy in copies:
        copy.start()
    for copy in copies:
        copy.wait()


def pack_kernel(strips, own, neighbour, block, *edges):
    frames, rows, cols, _ = own.shape
    whole = Packed(HALO, rows, cols)
    skip = frames - HALO
    whole.write(block, lambda f, r: own[f + skip, r], lambda f, r: beside_of(neighbour, f + skip, r, cols))
    for start, edge in zip(facing(strips, rows), edges):
        Packed(frames, HALO, cols).write(
            edge, lambda f, r: own[f, start + r], lambda f, r: beside_of(neighbour, f, start + r, cols)
        )


def own_beside(neighbour, f, r, cols):
    tile = only_beside(beside_of(neighbour, f, r, cols).astype(jnp.float32)).astype(jnp.bfloat16)
    return tile[:, :LANES], tile[:, LANES:]


def window(buffers, skip, frames, top, rows, cols, own, halo):
    every, beside = slice(0, cols), slice(cols, cols + TILE)
    for f in range(frames):
        found = []
        for j in range(HALO):
            found.append((HALO * top + j, own(f, (1 - top) * (rows - HALO) + j)))
            found.append((HALO * (1 - top) + j, halo(f, j)))
        for row, cells in found:
            fill(*buffers, skip + f, row, every, *cells[:2])
            fill(*buffers, skip + f, row, beside, *cells[2:])


def edge_own_kernel(strips, *refs):
    *refs, near_lo, near_pairs, near_stacked, arrived = refs
    own, neighbour, *edges, middle, last, weight_far, edge_sums, plane = refs
    frames, rows, cols, channels = own.shape
    width, rest = cols + TILE, channels - LANES
    copy = pltpu.make_async_copy(weight_far.at[0], plane, arrived.at[0])
    copy.start()
    if frames > 2:
        copy.wait()
    strip_block = Packed(frames, HALO, cols)
    near = (near_lo, near_pairs, near_stacked)
    span = min(frames, 3)
    zeros = span - 1
    clear((near_pairs,))
    for buffer in (near_lo, near_stacked):
        buffer[:zeros] = jnp.zeros((zeros,) + buffer.shape[1:], buffer.dtype)
    for group, (edge, top) in enumerate(zip(edges, at_top(strips))):

        def own_row(f, r):
            cells = own[f, r]
            return cells[:, :LANES], cells[:, LANES:], *own_beside(neighbour, f, r, cols)

        def halo_row(f, j):
            return *strip_block.read(edge, f, j, rest), *strip_block.read_beside(edge, f, j, rest)

        window(near, zeros, frames, top, rows, cols, own_row, halo_row)
        lefts = [columns([(t + k, 3 - span + k) for k in range(span)], *near, 0, HALO) for t in range(frames)]
        taps = [(k, 3 - span + k) for k in range(span)]
        products = convolve(taps, [plane, middle, last], jnp.concatenate(lefts, axis=0))
        for t in range(frames):
            for r in range(HALO):
                edge_sums[group, t, r] = join(products, (t * HALO + r) * width, width)
    if frames <= 2:
        copy.wait()


def own_taps(t):
    return [(f, f - t + 2) for f in range(max(0, t - 2), t + 1)]


def earlier_taps(t):
    return [(f, f - t) for f in range(t, HALO)]


def hidden_row(y, gain, cols):
    width, slab = y.shape[0], lax.axis_index("slab")
    position = lax.broadcasted_iota(jnp.int32, (width, 1), 0)
    right = cols + (slab == 0).astype(jnp.int32)
    left = width - (slab == 1).astype(jnp.int32)
    return jnp.where((position < right) | (position >= left), activate(y, gain), 0.0)


def all_taps(t):
    return [(t, 0), (t + 1, 1), (t + 2, 2)]


def partial_sums(frames, hidden, w2, rows, cols, partial):
    width, last = cols + TILE, frames - 1
    for t, taps in enumerate(([(last - 1, 0), (last, 1)], [(last, 0)])):
        products = convolve(taps, w2, columns(taps, *hidden, 0, rows))
        for r in range(rows):
            y = join(products, r * width, width)[:cols].astype(jnp.bfloat16)
            rest = y.shape[-1] - LANES
            partial[t, r] = y[:, :LANES]
            half = slice((r % 2) * rest, (r % 2 + 1) * rest)
            partial[t, rows + r // 2, :, half] = y[:, LANES:]


def safe_kernel(strips, *refs):
    *refs, lo, pairs, stacked, arrived = refs
    own, neighbour, block, plane, middle, last, gains, w2_far, h_lo, h_pairs, h_stacked, *w2 = refs
    copies = [pltpu.make_async_copy(w2_far.at[a], w2[a], arrived.at[a]) for a in range(3)]
    for copy in copies:
        copy.start()
    frames, rows, cols, channels = own.shape
    width, rest = cols + TILE, channels - LANES
    every, beside = slice(0, cols), slice(cols, width)
    clear_rows((lo, pairs, stacked), HALO - 1, HALO + rows)
    clear_rows((h_lo, h_pairs, h_stacked), 0, rows + 1)
    whole = Packed(HALO, rows, cols)

    @pl.when(lax.axis_index("frame") == 0)
    def none_earlier():
        for buffer in (lo, pairs, stacked):
            buffer[:HALO] = jnp.zeros((HALO,) + buffer.shape[1:], buffer.dtype)

    def put(frame, rows_of):
        for r, cells in enumerate(rows_of):
            fill(lo, pairs, stacked, frame, r + HALO, every, *cells[:2])
            fill(lo, pairs, stacked, frame, r + HALO, beside, *cells[2:])

    @if_earlier
    def build():
        for f in range(HALO):
            put(f, [(*whole.read(block, f, r, rest), *whole.read_beside(block, f, r, rest)) for r in range(rows)])

    for f in range(frames):
        cells = [own[f, r] for r in range(rows)]
        tiles = [own_beside(neighbour, f, r, cols) for r in range(rows)]
        put(HALO + f, [(c[:, :LANES], c[:, LANES:], *tile) for c, tile in zip(cells, tiles)])
    start, count = safe_rows(strips, rows)
    lefts = jnp.concatenate([columns(all_taps(t), lo, pairs, stacked, start, count) for t in range(frames)], axis=0)
    products = convolve(all_taps(0), [plane, middle, last], lefts)
    gain = gains[...]
    for t in range(frames):
        for r in range(count):
            h = hidden_row(join(products, (t * count + r) * width, width), gain, cols).astype(jnp.bfloat16)
            fill(h_lo, h_pairs, h_stacked, t, start + r, slice(0, width), h[:, :LANES], h[:, LANES:])
    for copy in copies:
        copy.wait()


def edge_kernel(strips, rows, cols, *refs):
    *refs, near_lo, near_pairs, near_stacked = refs
    *refs, h_lo, h_pairs, h_stacked, partial = refs
    *edges, block, edge_sums, safe_lo, safe_pairs, safe_stacked, plane, middle, gains, w2_first, w2_middle = refs
    frames, channels = edge_sums.shape[1], edge_sums.shape[-1]
    width, rest = cols + TILE, channels - LANES
    strip = lax.axis_index("strip")
    whole, strip_block = Packed(HALO, rows, cols), Packed(frames, HALO, cols)
    near = (near_lo, near_pairs, near_stacked)
    near_pairs[:, 2 * HALO] = jnp.zeros(near_pairs.shape[:1] + near_pairs.shape[2:], near_pairs.dtype)

    @pl.when(lax.axis_index("frame") == 0)
    def none_earlier():
        clear(near)

    gain = gains[...]
    for group, (edge, top) in enumerate(zip(edges, at_top(strips))):

        def own_row(f, r):
            low = pl.multiple_of((f * rows + r) * cols, TILE)
            high = pl.multiple_of(whole.high + (f * (rows // 2) + r // 2) * cols, TILE)
            pair = block[pl.ds(high, cols), :]
            return block[pl.ds(low, cols), :], pair, *beside_from(block, whole.beside, (f * rows + r) * HALO, rest)

        def halo_row(f, j):
            sent = frames - HALO + f
            return *strip_block.read(edge, sent, j, rest), *strip_block.read_beside(edge, sent, j, rest)

        def own_half(f, r, j):
            low, pair, *tile = own_row(f, r)
            return low, pair[:, (j % 2) * rest : (j % 2 + 1) * rest], *tile

        @if_earlier
        def build():
            every, beside = slice(0, cols), slice(cols, width)
            found = []
            for f in range(HALO):
                for j in range(HALO):
                    mine = own_half(f, (1 - top) * (rows - HALO) + j, j)
                    found += [(f, HALO * top + j, mine), (f, HALO * (1 - top) + j, halo_row(f, j))]
            for f, row, cells in found:
                fill(*near, f, row, every, *cells[:2])
                fill(*near, f, row, beside, *cells[2:])

        sums = [[edge_sums[group, t, r] for r in range(HALO)] for t in range(frames)]
        found = []
        for t in range(frames):
            taps = earlier_taps(t)
            products = convolve(taps, [plane, middle], columns(taps, *near, 0, HALO)) if taps else None
            for r in range(HALO):
                y = sums[t][r]
                if taps:
                    y = y + join(products, r * width, width)
                h = hidden_row(y, gain, cols)
                if strips != 2 and r == 1 - top:
                    h = h * jnp.where(strip == (0 if top else strips - 1), 0.0, 1.0)
                found.append((t, (1 - top) * rows + r, h.astype(jnp.bfloat16)))
        for t, row, h in found:
            fill(h_lo, h_pairs, h_stacked, t, row, slice(0, width), h[:, :LANES], h[:, LANES:])

    partial_sums(frames, (h_lo, h_pairs, h_stacked), [w2_first, w2_middle], rows, cols, partial)


def second_kernel(frames, rows, cols, h_lo, h_pairs, h_stacked, *refs):
    *w2, out = refs
    width = cols + TILE
    for t in range(frames):
        taps = [(f, f - t + 2) for f in range(max(0, t - 2), t + 1)]
        products = convolve(taps, w2, columns(taps, h_lo, h_pairs, h_stacked, 0, rows))
        for r in range(rows):
            out[t, r] = join(products, r * width, width)[:cols]


def finish_kernel(partial, own, gains, out_far, out, left):
    frames, rows, cols, channels = out.shape
    rest = channels - LANES
    gain = gains[...]

    sums = []
    for t in range(frames):
        y = own[t]
        if t < HALO:
            halves = [partial[t, rows + r // 2, :, (r % 2) * rest : (r % 2 + 1) * rest] for r in range(rows)]
            sent = [jnp.concatenate([partial[t, r], halves[r]], axis=-1) for r in range(rows)]
            y = y + jnp.stack(sent).astype(jnp.float32)
        sums.append(y.reshape(rows * cols, channels))
    results = [activate(y, gain).astype(jnp.bfloat16) for y in sums]
    copies = [pltpu.make_async_copy(out.at[t], out_far.at[t], left.at[t]) for t in range(frames)]
    for t in range(frames):
        out[t] = results[t].reshape(rows, cols, channels)
        copies[t].start()
    for copy in copies:
        copy.wait()


def call(kernel, name, ins, outs, scratch=(), semaphores=0, flops=0, far=(), far_out=False, alias=None):
    near, away = pl.BlockSpec(memory_space=pltpu.VMEM), pl.BlockSpec(memory_space=pltpu.HBM)
    in_specs, ins = [near] * len(ins), list(ins)
    for place in far:
        ins[place] = pltpu.with_memory_space_constraint(ins[place], pltpu.HBM)
        in_specs[place] = away
    one = not isinstance(outs, list)
    return pl.pallas_call(
        kernel,
        out_shape=outs,
        in_specs=in_specs,
        out_specs=(away if far_out else near) if one else [near] * len(outs),
        scratch_shapes=[pltpu.VMEM(shape, jnp.bfloat16) for shape in scratch]
        + [pltpu.SemaphoreType.DMA((semaphores,))] * (semaphores > 0),
        input_output_aliases=alias or {},
        compiler_params=pltpu.CompilerParams(vmem_limit_bytes=24 * 1024 * 1024),
        cost_estimate=pl.CostEstimate(flops=flops, bytes_accessed=4 * 1024 * 1024, transcendentals=0),
        name=name,
    )(*ins)


def block_scratch(frames, rows, width):
    return [(frames, rows, width, LANES), (frames, rows + 1, width, LANES), (frames - 1, rows, width, LANES)]


def shards(frames_in, weight_first, scale_first, weight_second, scale_second):
    frames, rows, cols, channels = frames_in.shape
    strips = lax.axis_size("strip")
    width = cols + TILE
    flops = frames * rows * cols * 27 * channels * channels
    bf16 = functools.partial(jax.ShapeDtypeStruct, dtype=jnp.bfloat16)
    f32 = functools.partial(jax.ShapeDtypeStruct, dtype=jnp.float32)

    plane_shape = bf16(weight_first.shape[1:])
    neighbour = swap(frames_in, "slab")
    own_in, middle, last = call(
        stage_kernel,
        "stage",
        [frames_in, weight_first],
        [bf16(frames_in.shape), plane_shape, plane_shape],
        semaphores=3,
        far=[0, 1],
    )
    edge_shape = bf16(Packed(frames, HALO, cols).shape)
    block, *edges = call(
        functools.partial(pack_kernel, strips),
        "pack",
        [own_in, neighbour],
        [bf16(Packed(HALO, rows, cols).shape)] + [edge_shape] * (1 if strips == 2 else 2),
    )
    ups = [(i, i + 1) for i in range(strips - 1)]
    downs = [(i + 1, i) for i in range(strips - 1)]
    ways = [[(0, 1), (1, 0)]] if strips == 2 else [ups, downs]
    before = forward(block)
    own_edges = [lax.ppermute(edge, "strip", way) for edge, way in zip(edges, ways)]
    before_edges = [forward(edge, way) for edge, way in zip(edges, ways)]
    edge_sums, plane = call(
        functools.partial(edge_own_kernel, strips),
        "edge_rows_own",
        [own_in, neighbour, *own_edges, middle, last, weight_first],
        [f32((len(ways), frames, HALO, width, channels)), plane_shape],
        block_scratch(frames + min(frames, 3) - 1, 2 * HALO, width),
        semaphores=1,
        flops=flops // 4,
        far=[-1],
    )
    gain_first = scale_first[None]
    h_shapes = [bf16(shape) for shape in block_scratch(frames, rows + 2, width)]
    partial_shape = bf16((HALO, rows + rows // 2, cols, LANES))
    *safe, w2_first, w2_middle, w2_last = call(
        functools.partial(safe_kernel, strips),
        "safe_rows",
        [own_in, neighbour, before, plane, middle, last, gain_first, weight_second],
        h_shapes + [plane_shape] * 3,
        block_scratch(HALO + frames, rows + 2 * HALO, width),
        semaphores=3,
        flops=flops,
        far=[-1],
    )
    h_lo, h_pairs, h_stacked, partial = call(
        functools.partial(edge_kernel, strips, rows, cols),
        "edge_rows",
        [*before_edges, before, edge_sums, *safe, plane, middle, gain_first, w2_first, w2_middle],
        h_shapes + [partial_shape],
        block_scratch(HALO, 2 * HALO, width),
        flops=flops,
        alias={len(before_edges) + 2 + k: k for k in range(3)},
    )
    sent = forward(partial)
    own = call(
        functools.partial(second_kernel, frames, rows, cols),
        "second_layer",
        [h_lo, h_pairs, h_stacked, w2_first, w2_middle, w2_last],
        f32((frames, rows, cols, channels)),
        flops=flops,
    )
    out = bf16(frames_in.shape)
    return call(
        finish_kernel,
        "finish",
        [sent, own, scale_second[None]],
        out,
        [out.shape],
        semaphores=frames,
        far_out=True,
    )


def solution(mesh):
    return jax.shard_map(
        shards,
        mesh=mesh,
        in_specs=(P(("groups", "frame"), "strip", "slab", None), P(), P(), P(), P()),
        out_specs=P(("groups", "frame"), "strip", "slab", None),
        check_vma=False,
    )
```

```python
import functools

import jax
import jax.numpy as jnp
from jax import lax
from jax.experimental import pallas as pl
from jax.experimental.pallas import tpu as pltpu
from jax.sharding import PartitionSpec as P

LANES = 128
TILE = 16
EPS = 1e-06


HALO = 2


def swap(x, axis):
    return lax.ppermute(x, axis, [(0, 1), (1, 0)])


def forward(x, way=None):
    steps, count = lax.axis_size("frame"), lax.axis_size("strip")
    way = [(i, i) for i in range(count)] if way is None else way
    pairs = [(f * count + i, (f + 1) * count + j) for f in range(steps - 1) for i, j in way]
    return lax.ppermute(x, ("frame", "strip"), pairs)


def if_earlier(build):
    pl.when(lax.axis_index("frame") > 0)(build)


class Packed:
    def __init__(self, frames, rows, cols):
        self.frames, self.rows, self.cols = frames, rows, cols
        self.high = frames * rows * cols
        self.beside = self.high + frames * (rows // 2) * cols
        self.tiles = -(-frames * rows * HALO // TILE)
        self.shape = (self.beside + 2 * self.tiles * TILE, LANES)

    def low_at(self, f, r):
        return slice((f * self.rows + r) * self.cols, (f * self.rows + r + 1) * self.cols)

    def high_at(self, f, r):
        start = self.high + (f * (self.rows // 2) + r // 2) * self.cols
        return slice(start, start + self.cols)

    def spot(self, f, r):
        cell = (f * self.rows + r) * HALO
        return cell // TILE, cell % TILE

    def beside_at(self, tile, high):
        start = self.beside + (2 * tile + high) * TILE
        return slice(start, start + TILE)

    def write(self, out, cells, tile_of):
        slab = lax.axis_index("slab")
        at = lax.broadcasted_iota(jnp.int32, (TILE, 1), 0)
        sums = [None] * self.tiles
        for f in range(self.frames):
            for r in range(self.rows):
                row = cells(f, r)
                out[self.low_at(f, r), :] = row[:, :LANES]
                rest = row.shape[-1] - LANES
                half = slice((r % 2) * rest, (r % 2 + 1) * rest)
                out[self.high_at(f, r), half] = row[:, LANES:]
                tile, place = self.spot(f, r)
                moved = pltpu.roll(tile_of(f, r).astype(jnp.float32), lax.rem(place + HALO * slab, TILE), 0)
                moved = jnp.where((at >= place) & (at < place + HALO), moved, 0.0)
                sums[tile] = moved if sums[tile] is None else sums[tile] + moved
        for tile, cells_beside in enumerate(sums):
            cells_beside = cells_beside.astype(jnp.bfloat16)
            out[self.beside_at(tile, 0), :] = cells_beside[:, :LANES]
            out[self.beside_at(tile, 1), :rest] = cells_beside[:, LANES:]

    def read(self, ref, f, r, rest):
        half = slice((r % 2) * rest, (r % 2 + 1) * rest)
        return ref[self.low_at(f, r), :], ref[self.high_at(f, r), half]

    def read_beside(self, ref, f, r, rest):
        return beside_from(ref, self.beside, (f * self.rows + r) * HALO, rest)


def beside_from(ref, start, cell, rest):
    slab = lax.axis_index("slab")
    parts = []
    for high, lanes in ((0, LANES), (1, rest)):
        at = start + (2 * (cell // TILE) + high) * TILE
        cells = ref[pl.ds(pl.multiple_of(at, TILE), TILE), :].astype(jnp.float32)
        cells = pltpu.roll(cells, lax.rem(2 * TILE - cell % TILE - HALO * slab, TILE), 0)
        parts.append(only_beside(cells).astype(jnp.bfloat16)[:, :lanes])
    return parts


def only_beside(tile):
    slab = lax.axis_index("slab")
    at = lax.broadcasted_iota(jnp.int32, tile.shape, 0)
    begin = slab * (TILE - HALO)
    return jnp.where((at >= begin) & (at < begin + HALO), tile, 0.0)


def fill(lo, pairs, stacked, frame, row, cols, low, high):
    rest = high.shape[-1]
    lo[frame, row, cols, :] = low
    pairs[frame, row + 1, cols, :rest] = high
    pairs[frame, row, cols, rest:] = high
    if frame < stacked.shape[0]:
        stacked[frame, row, cols, :rest] = high
    if frame > 0:
        stacked[frame - 1, row, cols, rest:] = high


def columns(taps, lo, pairs, stacked, row, rows):
    def flat(block):
        return block.reshape(-1, LANES)

    pieces = [flat(lo[f, pl.ds(row + b, rows)]) for f, _ in taps for b in range(3)]
    pieces += [flat(pairs[f, pl.ds(row + 1, rows)]) for f, _ in taps]
    for k in range(0, len(taps), 2):
        f = taps[k][0]
        if k + 1 < len(taps):
            pieces.append(flat(stacked[f, pl.ds(row + 2, rows)]))
        else:
            pieces.append(flat(pairs[f, pl.ds(row + 3, rows)]))
    return jnp.concatenate(pieces, axis=-1)


def planes(taps, weight, c):
    pieces = [weight[a][b, c, :LANES, :] for _, a in taps for b in range(3)]
    for _, a in taps:
        pieces += [weight[a][0, c, LANES:, :], weight[a][1, c, LANES:, :]]
    for _, a in taps:
        pieces.append(weight[a][2, c, LANES:, :])
    if len(taps) % 2:
        pieces.append(jnp.zeros_like(weight[a][0, c, LANES:, :]))
    return jnp.concatenate(pieces, axis=0)


def convolve(taps, weight, lefts):
    return [
        jnp.dot(lefts, planes(taps, weight, c), preferred_element_type=jnp.float32)
        for c in range(3)
    ]


def join(products, start, width):
    before, middle, after = [p[start : start + width] for p in products]
    return pltpu.roll(before, 1, 0) + middle + pltpu.roll(after, width - 1, 0)


def activate(y, gains):
    mean_square = jnp.sum(y * y, axis=-1, keepdims=True) * (1.0 / y.shape[-1])
    v = y * lax.rsqrt(mean_square + EPS) * gains
    return v / (1.0 + jnp.exp(-v))


def clear(buffers):
    for buffer in buffers:
        buffer[...] = jnp.zeros_like(buffer)


def clear_rows(buffers, above, below):
    lo, pairs, stacked = buffers
    for buffer, rows in ((lo, (above, below)), (pairs, (above, above + 1, below, below + 1)), (stacked, (above, below))):
        for row in rows:
            buffer[:, row] = jnp.zeros(buffer.shape[:1] + buffer.shape[2:], buffer.dtype)


def facing(strips, rows):
    if strips == 2:
        return [jnp.where(lax.axis_index("strip") == 0, rows - HALO, 0)]
    return [rows - HALO, 0]


def at_top(strips):
    return [lax.axis_index("strip")] if strips == 2 else [1, 0]


def safe_rows(strips, rows):
    return (1 + lax.axis_index("strip"), rows - 1) if strips == 2 else (2, rows - 2)


def beside_of(neighbour, f, r, cols):
    start = pl.multiple_of(lax.axis_index("slab") * (cols - TILE), TILE)
    return neighbour[f, r, pl.ds(start, TILE), :]


def stage_kernel(own_far, weight_far, own, middle, last, arrived):
    copies = [
        pltpu.make_async_copy(own_far, own, arrived.at[0]),
        pltpu.make_async_copy(weight_far.at[2], last, arrived.at[1]),
        pltpu.make_async_copy(weight_far.at[1], middle, arrived.at[2]),
    ]
    for copy in copies:
        copy.start()
    for copy in copies:
        copy.wait()


def pack_kernel(strips, own, neighbour, block, *edges):
    frames, rows, cols, _ = own.shape
    whole = Packed(HALO, rows, cols)
    skip = frames - HALO
    whole.write(block, lambda f, r: own[f + skip, r], lambda f, r: beside_of(neighbour, f + skip, r, cols))
    for start, edge in zip(facing(strips, rows), edges):
        Packed(frames, HALO, cols).write(
            edge, lambda f, r: own[f, start + r], lambda f, r: beside_of(neighbour, f, start + r, cols)
        )


def own_beside(neighbour, f, r, cols):
    tile = only_beside(beside_of(neighbour, f, r, cols).astype(jnp.float32)).astype(jnp.bfloat16)
    return tile[:, :LANES], tile[:, LANES:]


def window(buffers, skip, frames, top, rows, cols, own, halo):
    every, beside = slice(0, cols), slice(cols, cols + TILE)
    for f in range(frames):
        found = []
        for j in range(HALO):
            found.append((HALO * top + j, own(f, (1 - top) * (rows - HALO) + j)))
            found.append((HALO * (1 - top) + j, halo(f, j)))
        for row, cells in found:
            fill(*buffers, skip + f, row, every, *cells[:2])
            fill(*buffers, skip + f, row, beside, *cells[2:])


def edge_own_kernel(strips, *refs):
    *refs, near_lo, near_pairs, near_stacked, arrived = refs
    own, neighbour, *edges, middle, last, weight_far, edge_sums, plane = refs
    frames, rows, cols, channels = own.shape
    width, rest = cols + TILE, channels - LANES
    copy = pltpu.make_async_copy(weight_far.at[0], plane, arrived.at[0])
    copy.start()
    if frames > 2:
        copy.wait()
    strip_block = Packed(frames, HALO, cols)
    near = (near_lo, near_pairs, near_stacked)
    span = min(frames, 3)
    zeros = span - 1
    clear((near_pairs,))
    for buffer in (near_lo, near_stacked):
        buffer[:zeros] = jnp.zeros((zeros,) + buffer.shape[1:], buffer.dtype)
    for group, (edge, top) in enumerate(zip(edges, at_top(strips))):

        def own_row(f, r):
            cells = own[f, r]
            return cells[:, :LANES], cells[:, LANES:], *own_beside(neighbour, f, r, cols)

        def halo_row(f, j):
            return *strip_block.read(edge, f, j, rest), *strip_block.read_beside(edge, f, j, rest)

        window(near, zeros, frames, top, rows, cols, own_row, halo_row)
        lefts = [columns([(t + k, 3 - span + k) for k in range(span)], *near, 0, HALO) for t in range(frames)]
        taps = [(k, 3 - span + k) for k in range(span)]
        products = convolve(taps, [plane, middle, last], jnp.concatenate(lefts, axis=0))
        for t in range(frames):
            for r in range(HALO):
                edge_sums[group, t, r] = join(products, (t * HALO + r) * width, width)
    if frames <= 2:
        copy.wait()


def own_taps(t):
    return [(f, f - t + 2) for f in range(max(0, t - 2), t + 1)]


def earlier_taps(t):
    return [(f, f - t) for f in range(t, HALO)]


def hidden_row(y, gain, cols):
    width, slab = y.shape[0], lax.axis_index("slab")
    position = lax.broadcasted_iota(jnp.int32, (width, 1), 0)
    right = cols + (slab == 0).astype(jnp.int32)
    left = width - (slab == 1).astype(jnp.int32)
    return jnp.where((position < right) | (position >= left), activate(y, gain), 0.0)


def all_taps(t):
    return [(t, 0), (t + 1, 1), (t + 2, 2)]


def safe_sums(strips, rows):
    if strips == 2:
        strip = lax.axis_index("strip")
        return (HALO * strip, rows - HALO), ((1 - strip) * (rows - HALO), HALO)
    return (0, 0), (0, rows)


def partial_sums(frames, hidden, w2, start, count, cols, partial):
    width, last = cols + TILE, frames - 1
    rows = partial.shape[1] * 2 // 3
    for t, taps in enumerate(([(last - 1, 0), (last, 1)], [(last, 0)])):
        products = convolve(taps, w2, columns(taps, *hidden, start, count))
        for r in range(count):
            y = join(products, r * width, width)[:cols].astype(jnp.bfloat16)
            rest = y.shape[-1] - LANES
            partial[t, start + r] = y[:, :LANES]
            half = slice((r % 2) * rest, (r % 2 + 1) * rest)
            partial[t, rows + start // 2 + r // 2, :, half] = y[:, LANES:]


def safe_kernel(strips, *refs):
    *refs, lo, pairs, stacked, arrived = refs
    own, neighbour, block, plane, middle, last, gains, w2_far, h_lo, h_pairs, h_stacked, partial, w2_first, w2_middle, w2_last = refs
    w2 = [w2_first, w2_middle, w2_last]
    copies = [pltpu.make_async_copy(w2_far.at[a], w2[a], arrived.at[a]) for a in range(3)]
    for copy in copies:
        copy.start()
    frames, rows, cols, channels = own.shape
    width, rest = cols + TILE, channels - LANES
    every, beside = slice(0, cols), slice(cols, width)
    clear_rows((lo, pairs, stacked), HALO - 1, HALO + rows)
    clear_rows((h_lo, h_pairs, h_stacked), 0, rows + 1)
    whole = Packed(HALO, rows, cols)

    @pl.when(lax.axis_index("frame") == 0)
    def none_earlier():
        for buffer in (lo, pairs, stacked):
            buffer[:HALO] = jnp.zeros((HALO,) + buffer.shape[1:], buffer.dtype)

    def put(frame, rows_of):
        for r, cells in enumerate(rows_of):
            fill(lo, pairs, stacked, frame, r + HALO, every, *cells[:2])
            fill(lo, pairs, stacked, frame, r + HALO, beside, *cells[2:])

    @if_earlier
    def build():
        for f in range(HALO):
            put(f, [(*whole.read(block, f, r, rest), *whole.read_beside(block, f, r, rest)) for r in range(rows)])

    for f in range(frames):
        cells = [own[f, r] for r in range(rows)]
        tiles = [own_beside(neighbour, f, r, cols) for r in range(rows)]
        put(HALO + f, [(c[:, :LANES], c[:, LANES:], *tile) for c, tile in zip(cells, tiles)])
    start, count = safe_rows(strips, rows)
    lefts = jnp.concatenate([columns(all_taps(t), lo, pairs, stacked, start, count) for t in range(frames)], axis=0)
    products = convolve(all_taps(0), [plane, middle, last], lefts)
    gain = gains[...]
    for t in range(frames):
        for r in range(count):
            h = hidden_row(join(products, (t * count + r) * width, width), gain, cols).astype(jnp.bfloat16)
            fill(h_lo, h_pairs, h_stacked, t, start + r, slice(0, width), h[:, :LANES], h[:, LANES:])
    for copy in copies:
        copy.wait()
    (start, count), _ = safe_sums(strips, rows)
    if count:
        partial_sums(frames, (h_lo, h_pairs, h_stacked), w2, start, count, cols, partial)


def edge_kernel(strips, rows, cols, *refs):
    *refs, near_lo, near_pairs, near_stacked = refs
    *refs, h_lo, h_pairs, h_stacked, partial = refs
    *edges, block, edge_sums, _, _, _, _, plane, middle, gains, w2_first, w2_middle = refs
    frames, channels = edge_sums.shape[1], edge_sums.shape[-1]
    width, rest = cols + TILE, channels - LANES
    strip = lax.axis_index("strip")
    whole, strip_block = Packed(HALO, rows, cols), Packed(frames, HALO, cols)
    near = (near_lo, near_pairs, near_stacked)
    near_pairs[:, 2 * HALO] = jnp.zeros(near_pairs.shape[:1] + near_pairs.shape[2:], near_pairs.dtype)

    @pl.when(lax.axis_index("frame") == 0)
    def none_earlier():
        clear(near)

    gain = gains[...]
    for group, (edge, top) in enumerate(zip(edges, at_top(strips))):

        def own_row(f, r):
            low = pl.multiple_of((f * rows + r) * cols, TILE)
            high = pl.multiple_of(whole.high + (f * (rows // 2) + r // 2) * cols, TILE)
            pair = block[pl.ds(high, cols), :]
            return block[pl.ds(low, cols), :], pair, *beside_from(block, whole.beside, (f * rows + r) * HALO, rest)

        def halo_row(f, j):
            sent = frames - HALO + f
            return *strip_block.read(edge, sent, j, rest), *strip_block.read_beside(edge, sent, j, rest)

        def own_half(f, r, j):
            low, pair, *tile = own_row(f, r)
            return low, pair[:, (j % 2) * rest : (j % 2 + 1) * rest], *tile

        @if_earlier
        def build():
            every, beside = slice(0, cols), slice(cols, width)
            found = []
            for f in range(HALO):
                for j in range(HALO):
                    mine = own_half(f, (1 - top) * (rows - HALO) + j, j)
                    found += [(f, HALO * top + j, mine), (f, HALO * (1 - top) + j, halo_row(f, j))]
            for f, row, cells in found:
                fill(*near, f, row, every, *cells[:2])
                fill(*near, f, row, beside, *cells[2:])

        sums = [[edge_sums[group, t, r] for r in range(HALO)] for t in range(frames)]
        found = []
        for t in range(frames):
            taps = earlier_taps(t)
            products = convolve(taps, [plane, middle], columns(taps, *near, 0, HALO)) if taps else None
            for r in range(HALO):
                y = sums[t][r]
                if taps:
                    y = y + join(products, r * width, width)
                h = hidden_row(y, gain, cols)
                if strips != 2 and r == 1 - top:
                    h = h * jnp.where(strip == (0 if top else strips - 1), 0.0, 1.0)
                found.append((t, (1 - top) * rows + r, h.astype(jnp.bfloat16)))
        for t, row, h in found:
            fill(h_lo, h_pairs, h_stacked, t, row, slice(0, width), h[:, :LANES], h[:, LANES:])

    _, (start, count) = safe_sums(strips, rows)
    partial_sums(frames, (h_lo, h_pairs, h_stacked), [w2_first, w2_middle], start, count, cols, partial)


def second_kernel(frames, rows, cols, h_lo, h_pairs, h_stacked, *refs):
    *w2, out = refs
    width = cols + TILE
    for t in range(frames):
        taps = [(f, f - t + 2) for f in range(max(0, t - 2), t + 1)]
        products = convolve(taps, w2, columns(taps, h_lo, h_pairs, h_stacked, 0, rows))
        for r in range(rows):
            out[t, r] = join(products, r * width, width)[:cols]


def finish_kernel(partial, own, gains, out_far, out, left):
    frames, rows, cols, channels = out.shape
    rest = channels - LANES
    gain = gains[...]

    sums = []
    for t in range(frames):
        y = own[t]
        if t < HALO:
            halves = [partial[t, rows + r // 2, :, (r % 2) * rest : (r % 2 + 1) * rest] for r in range(rows)]
            sent = [jnp.concatenate([partial[t, r], halves[r]], axis=-1) for r in range(rows)]
            y = y + jnp.stack(sent).astype(jnp.float32)
        sums.append(y.reshape(rows * cols, channels))
    results = [activate(y, gain).astype(jnp.bfloat16) for y in sums]
    copies = [pltpu.make_async_copy(out.at[t], out_far.at[t], left.at[t]) for t in range(frames)]
    for t in range(frames):
        out[t] = results[t].reshape(rows, cols, channels)
        copies[t].start()
    for copy in copies:
        copy.wait()


def call(kernel, name, ins, outs, scratch=(), semaphores=0, flops=0, far=(), far_out=False, alias=None):
    near, away = pl.BlockSpec(memory_space=pltpu.VMEM), pl.BlockSpec(memory_space=pltpu.HBM)
    in_specs, ins = [near] * len(ins), list(ins)
    for place in far:
        ins[place] = pltpu.with_memory_space_constraint(ins[place], pltpu.HBM)
        in_specs[place] = away
    one = not isinstance(outs, list)
    return pl.pallas_call(
        kernel,
        out_shape=outs,
        in_specs=in_specs,
        out_specs=(away if far_out else near) if one else [near] * len(outs),
        scratch_shapes=[pltpu.VMEM(shape, jnp.bfloat16) for shape in scratch]
        + [pltpu.SemaphoreType.DMA((semaphores,))] * (semaphores > 0),
        input_output_aliases=alias or {},
        compiler_params=pltpu.CompilerParams(vmem_limit_bytes=24 * 1024 * 1024),
        cost_estimate=pl.CostEstimate(flops=flops, bytes_accessed=4 * 1024 * 1024, transcendentals=0),
        name=name,
    )(*ins)


def block_scratch(frames, rows, width):
    return [(frames, rows, width, LANES), (frames, rows + 1, width, LANES), (frames - 1, rows, width, LANES)]


def shards(frames_in, weight_first, scale_first, weight_second, scale_second):
    frames, rows, cols, channels = frames_in.shape
    strips = lax.axis_size("strip")
    width = cols + TILE
    flops = frames * rows * cols * 27 * channels * channels
    bf16 = functools.partial(jax.ShapeDtypeStruct, dtype=jnp.bfloat16)
    f32 = functools.partial(jax.ShapeDtypeStruct, dtype=jnp.float32)

    plane_shape = bf16(weight_first.shape[1:])
    neighbour = swap(frames_in, "slab")
    own_in, middle, last = call(
        stage_kernel,
        "stage",
        [frames_in, weight_first],
        [bf16(frames_in.shape), plane_shape, plane_shape],
        semaphores=3,
        far=[0, 1],
    )
    edge_shape = bf16(Packed(frames, HALO, cols).shape)
    block, *edges = call(
        functools.partial(pack_kernel, strips),
        "pack",
        [own_in, neighbour],
        [bf16(Packed(HALO, rows, cols).shape)] + [edge_shape] * (1 if strips == 2 else 2),
    )
    ups = [(i, i + 1) for i in range(strips - 1)]
    downs = [(i + 1, i) for i in range(strips - 1)]
    ways = [[(0, 1), (1, 0)]] if strips == 2 else [ups, downs]
    before = forward(block)
    own_edges = [lax.ppermute(edge, "strip", way) for edge, way in zip(edges, ways)]
    before_edges = [forward(edge, way) for edge, way in zip(edges, ways)]
    edge_sums, plane = call(
        functools.partial(edge_own_kernel, strips),
        "edge_rows_own",
        [own_in, neighbour, *own_edges, middle, last, weight_first],
        [f32((len(ways), frames, HALO, width, channels)), plane_shape],
        block_scratch(frames + min(frames, 3) - 1, 2 * HALO, width),
        semaphores=1,
        flops=flops // 4,
        far=[-1],
    )
    gain_first = scale_first[None]
    h_shapes = [bf16(shape) for shape in block_scratch(frames, rows + 2, width)]
    partial_shape = bf16((HALO, rows + rows // 2, cols, LANES))
    *safe, w2_first, w2_middle, w2_last = call(
        functools.partial(safe_kernel, strips),
        "safe_rows",
        [own_in, neighbour, before, plane, middle, last, gain_first, weight_second],
        h_shapes + [partial_shape] + [plane_shape] * 3,
        block_scratch(HALO + frames, rows + 2 * HALO, width),
        semaphores=3,
        flops=flops,
        far=[-1],
    )
    h_lo, h_pairs, h_stacked, partial = call(
        functools.partial(edge_kernel, strips, rows, cols),
        "edge_rows",
        [*before_edges, before, edge_sums, *safe, plane, middle, gain_first, w2_first, w2_middle],
        h_shapes + [partial_shape],
        block_scratch(HALO, 2 * HALO, width),
        flops=flops,
        alias={len(before_edges) + 2 + k: k for k in range(4)},
    )
    sent = forward(partial)
    own = call(
        functools.partial(second_kernel, frames, rows, cols),
        "second_layer",
        [h_lo, h_pairs, h_stacked, w2_first, w2_middle, w2_last],
        f32((frames, rows, cols, channels)),
        flops=flops,
    )
    out = bf16(frames_in.shape)
    return call(
        finish_kernel,
        "finish",
        [sent, own, scale_second[None]],
        out,
        [out.shape],
        semaphores=frames,
        far_out=True,
    )


def solution(mesh):
    return jax.shard_map(
        shards,
        mesh=mesh,
        in_specs=(P(("groups", "frame"), "strip", "slab", None), P(), P(), P(), P()),
        out_specs=P(("groups", "frame"), "strip", "slab", None),
        check_vma=False,
    )
```

```python
import functools

import jax
import jax.numpy as jnp
from jax import lax
from jax.experimental import pallas as pl
from jax.experimental.pallas import tpu as pltpu
from jax.sharding import PartitionSpec as P

LANES = 128
TILE = 16
EPS = 1e-06


HALO = 2


def swap(x, axis):
    return lax.ppermute(x, axis, [(0, 1), (1, 0)])


def forward(x, way=None):
    steps, count = lax.axis_size("frame"), lax.axis_size("strip")
    way = [(i, i) for i in range(count)] if way is None else way
    pairs = [(f * count + i, (f + 1) * count + j) for f in range(steps - 1) for i, j in way]
    return lax.ppermute(x, ("frame", "strip"), pairs)


def if_earlier(build):
    pl.when(lax.axis_index("frame") > 0)(build)


class Packed:
    def __init__(self, frames, rows, cols):
        self.frames, self.rows, self.cols = frames, rows, cols
        self.high = frames * rows * cols
        self.beside = self.high + frames * (rows // 2) * cols
        self.tiles = -(-frames * rows * HALO // TILE)
        self.shared = frames * rows * HALO <= TILE // 2
        self.shape = (self.beside + (1 if self.shared else 2) * self.tiles * TILE, LANES)

    def low_at(self, f, r):
        return slice((f * self.rows + r) * self.cols, (f * self.rows + r + 1) * self.cols)

    def high_at(self, f, r):
        start = self.high + (f * (self.rows // 2) + r // 2) * self.cols
        return slice(start, start + self.cols)

    def spot(self, f, r):
        cell = (f * self.rows + r) * HALO
        return cell // TILE, cell % TILE

    def beside_at(self, tile, high):
        start = self.beside + (2 * tile + high) * TILE
        return slice(start, start + TILE)

    def write(self, out, cells, tile_of):
        slab = lax.axis_index("slab")
        at = lax.broadcasted_iota(jnp.int32, (TILE, 1), 0)
        sums = [None] * self.tiles
        for f in range(self.frames):
            for r in range(self.rows):
                row = cells(f, r)
                out[self.low_at(f, r), :] = row[:, :LANES]
                rest = row.shape[-1] - LANES
                half = slice((r % 2) * rest, (r % 2 + 1) * rest)
                out[self.high_at(f, r), half] = row[:, LANES:]
                tile, place = self.spot(f, r)
                moved = pltpu.roll(tile_of(f, r).astype(jnp.float32), lax.rem(place + HALO * slab, TILE), 0)
                moved = jnp.where((at >= place) & (at < place + HALO), moved, 0.0)
                sums[tile] = moved if sums[tile] is None else sums[tile] + moved
        if self.shared:
            low, high = sums[0][:, :LANES], sums[0][:, LANES:]
            high = jnp.concatenate([high, jnp.zeros((TILE, LANES - rest), jnp.float32)], axis=-1)
            both = jnp.where(at < TILE // 2, low, pltpu.roll(high, TILE // 2, 0))
            out[self.beside_at(0, 0), :] = both.astype(jnp.bfloat16)
            return
        for tile, cells_beside in enumerate(sums):
            cells_beside = cells_beside.astype(jnp.bfloat16)
            out[self.beside_at(tile, 0), :] = cells_beside[:, :LANES]
            out[self.beside_at(tile, 1), :rest] = cells_beside[:, LANES:]

    def read(self, ref, f, r, rest):
        half = slice((r % 2) * rest, (r % 2 + 1) * rest)
        return ref[self.low_at(f, r), :], ref[self.high_at(f, r), half]

    def read_beside(self, ref, f, r, rest):
        return beside_from(ref, self.beside, (f * self.rows + r) * HALO, rest, self.shared)


def beside_from(ref, start, cell, rest, shared=False):
    slab = lax.axis_index("slab")
    parts = []
    for high, lanes in ((0, LANES), (1, rest)):
        at = start if shared else start + (2 * (cell // TILE) + high) * TILE
        below = TILE // 2 if shared and high else 0
        cells = ref[pl.ds(pl.multiple_of(at, TILE), TILE), :].astype(jnp.float32)
        cells = pltpu.roll(cells, lax.rem(2 * TILE - cell % TILE - below - HALO * slab, TILE), 0)
        parts.append(only_beside(cells).astype(jnp.bfloat16)[:, :lanes])
    return parts


def only_beside(tile):
    slab = lax.axis_index("slab")
    at = lax.broadcasted_iota(jnp.int32, tile.shape, 0)
    begin = slab * (TILE - HALO)
    return jnp.where((at >= begin) & (at < begin + HALO), tile, 0.0)


def fill(lo, pairs, stacked, frame, row, cols, low, high):
    rest = high.shape[-1]
    lo[frame, row, cols, :] = low
    pairs[frame, row + 1, cols, :rest] = high
    pairs[frame, row, cols, rest:] = high
    if frame < stacked.shape[0]:
        stacked[frame, row, cols, :rest] = high
    if frame > 0:
        stacked[frame - 1, row, cols, rest:] = high


def columns(taps, lo, pairs, stacked, row, rows):
    def flat(block):
        return block.reshape(-1, LANES)

    pieces = [flat(lo[f, pl.ds(row + b, rows)]) for f, _ in taps for b in range(3)]
    pieces += [flat(pairs[f, pl.ds(row + 1, rows)]) for f, _ in taps]
    for k in range(0, len(taps), 2):
        f = taps[k][0]
        if k + 1 < len(taps):
            pieces.append(flat(stacked[f, pl.ds(row + 2, rows)]))
        else:
            pieces.append(flat(pairs[f, pl.ds(row + 3, rows)]))
    return jnp.concatenate(pieces, axis=-1)


def planes(taps, weight, c):
    pieces = [weight[a][b, c, :LANES, :] for _, a in taps for b in range(3)]
    for _, a in taps:
        pieces += [weight[a][0, c, LANES:, :], weight[a][1, c, LANES:, :]]
    for _, a in taps:
        pieces.append(weight[a][2, c, LANES:, :])
    if len(taps) % 2:
        pieces.append(jnp.zeros_like(weight[a][0, c, LANES:, :]))
    return jnp.concatenate(pieces, axis=0)


def convolve(taps, weight, lefts):
    return [
        jnp.dot(lefts, planes(taps, weight, c), preferred_element_type=jnp.float32)
        for c in range(3)
    ]


def join(products, start, width):
    before, middle, after = [p[start : start + width] for p in products]
    return pltpu.roll(before, 1, 0) + middle + pltpu.roll(after, width - 1, 0)


def activate(y, gains):
    mean_square = jnp.sum(y * y, axis=-1, keepdims=True) * (1.0 / y.shape[-1])
    v = y * lax.rsqrt(mean_square + EPS) * gains
    return v / (1.0 + jnp.exp(-v))


def clear(buffers):
    for buffer in buffers:
        buffer[...] = jnp.zeros_like(buffer)


def clear_rows(buffers, above, below):
    lo, pairs, stacked = buffers
    for buffer, rows in ((lo, (above, below)), (pairs, (above, above + 1, below, below + 1)), (stacked, (above, below))):
        for row in rows:
            buffer[:, row] = jnp.zeros(buffer.shape[:1] + buffer.shape[2:], buffer.dtype)


def facing(strips, rows):
    if strips == 2:
        return [jnp.where(lax.axis_index("strip") == 0, rows - HALO, 0)]
    return [rows - HALO, 0]


def at_top(strips):
    return [lax.axis_index("strip")] if strips == 2 else [1, 0]


def safe_rows(strips, rows):
    return (1 + lax.axis_index("strip"), rows - 1) if strips == 2 else (2, rows - 2)


def beside_of(neighbour, f, r, cols):
    start = pl.multiple_of(lax.axis_index("slab") * (cols - TILE), TILE)
    return neighbour[f, r, pl.ds(start, TILE), :]


def stage_kernel(own_far, weight_far, own, middle, last, arrived):
    copies = [
        pltpu.make_async_copy(own_far, own, arrived.at[0]),
        pltpu.make_async_copy(weight_far.at[2], last, arrived.at[1]),
        pltpu.make_async_copy(weight_far.at[1], middle, arrived.at[2]),
    ]
    for copy in copies:
        copy.start()
    for copy in copies:
        copy.wait()


def pack_kernel(strips, own, neighbour, block, *edges):
    frames, rows, cols, _ = own.shape
    whole = Packed(HALO, rows, cols)
    skip = frames - HALO
    whole.write(block, lambda f, r: own[f + skip, r], lambda f, r: beside_of(neighbour, f + skip, r, cols))
    for start, edge in zip(facing(strips, rows), edges):
        Packed(frames, HALO, cols).write(
            edge, lambda f, r: own[f, start + r], lambda f, r: beside_of(neighbour, f, start + r, cols)
        )


def own_beside(neighbour, f, r, cols):
    tile = only_beside(beside_of(neighbour, f, r, cols).astype(jnp.float32)).astype(jnp.bfloat16)
    return tile[:, :LANES], tile[:, LANES:]


def window(buffers, skip, frames, top, rows, cols, own, halo):
    every, beside = slice(0, cols), slice(cols, cols + TILE)
    for f in range(frames):
        found = []
        for j in range(HALO):
            found.append((HALO * top + j, own(f, (1 - top) * (rows - HALO) + j)))
            found.append((HALO * (1 - top) + j, halo(f, j)))
        for row, cells in found:
            fill(*buffers, skip + f, row, every, *cells[:2])
            fill(*buffers, skip + f, row, beside, *cells[2:])


def edge_own_kernel(strips, *refs):
    *refs, near_lo, near_pairs, near_stacked, arrived = refs
    own, neighbour, *edges, middle, last, weight_far, edge_sums, plane = refs
    frames, rows, cols, channels = own.shape
    width, rest = cols + TILE, channels - LANES
    copy = pltpu.make_async_copy(weight_far.at[0], plane, arrived.at[0])
    copy.start()
    if frames > 2:
        copy.wait()
    strip_block = Packed(frames, HALO, cols)
    near = (near_lo, near_pairs, near_stacked)
    span = min(frames, 3)
    zeros = span - 1
    clear((near_pairs,))
    for buffer in (near_lo, near_stacked):
        buffer[:zeros] = jnp.zeros((zeros,) + buffer.shape[1:], buffer.dtype)
    for group, (edge, top) in enumerate(zip(edges, at_top(strips))):

        def own_row(f, r):
            cells = own[f, r]
            return cells[:, :LANES], cells[:, LANES:], *own_beside(neighbour, f, r, cols)

        def halo_row(f, j):
            return *strip_block.read(edge, f, j, rest), *strip_block.read_beside(edge, f, j, rest)

        window(near, zeros, frames, top, rows, cols, own_row, halo_row)
        lefts = [columns([(t + k, 3 - span + k) for k in range(span)], *near, 0, HALO) for t in range(frames)]
        taps = [(k, 3 - span + k) for k in range(span)]
        products = convolve(taps, [plane, middle, last], jnp.concatenate(lefts, axis=0))
        for t in range(frames):
            for r in range(HALO):
                edge_sums[group, t, r] = join(products, (t * HALO + r) * width, width)
    if frames <= 2:
        copy.wait()


def own_taps(t):
    return [(f, f - t + 2) for f in range(max(0, t - 2), t + 1)]


def earlier_taps(t):
    return [(f, f - t) for f in range(t, HALO)]


def hidden_row(y, gain, cols):
    width, slab = y.shape[0], lax.axis_index("slab")
    position = lax.broadcasted_iota(jnp.int32, (width, 1), 0)
    right = cols + (slab == 0).astype(jnp.int32)
    left = width - (slab == 1).astype(jnp.int32)
    return jnp.where((position < right) | (position >= left), activate(y, gain), 0.0)


def all_taps(t):
    return [(t, 0), (t + 1, 1), (t + 2, 2)]


def partial_sums(frames, hidden, w2, rows, cols, partial):
    width, last = cols + TILE, frames - 1
    for t, taps in enumerate(([(last - 1, 0), (last, 1)], [(last, 0)])):
        products = convolve(taps, w2, columns(taps, *hidden, 0, rows))
        for r in range(rows):
            y = join(products, r * width, width)[:cols].astype(jnp.bfloat16)
            rest = y.shape[-1] - LANES
            partial[t, r] = y[:, :LANES]
            half = slice((r % 2) * rest, (r % 2 + 1) * rest)
            partial[t, rows + r // 2, :, half] = y[:, LANES:]


def safe_kernel(strips, *refs):
    *refs, lo, pairs, stacked, arrived = refs
    own, neighbour, block, plane, middle, last, gains, w2_far, h_lo, h_pairs, h_stacked, *w2 = refs
    copies = [pltpu.make_async_copy(w2_far.at[a], w2[a], arrived.at[a]) for a in range(3)]
    for copy in copies:
        copy.start()
    frames, rows, cols, channels = own.shape
    width, rest = cols + TILE, channels - LANES
    every, beside = slice(0, cols), slice(cols, width)
    clear_rows((lo, pairs, stacked), HALO - 1, HALO + rows)
    clear_rows((h_lo, h_pairs, h_stacked), 0, rows + 1)
    whole = Packed(HALO, rows, cols)

    @pl.when(lax.axis_index("frame") == 0)
    def none_earlier():
        for buffer in (lo, pairs, stacked):
            buffer[:HALO] = jnp.zeros((HALO,) + buffer.shape[1:], buffer.dtype)

    def put(frame, rows_of):
        for r, cells in enumerate(rows_of):
            fill(lo, pairs, stacked, frame, r + HALO, every, *cells[:2])
            fill(lo, pairs, stacked, frame, r + HALO, beside, *cells[2:])

    @if_earlier
    def build():
        for f in range(HALO):
            put(f, [(*whole.read(block, f, r, rest), *whole.read_beside(block, f, r, rest)) for r in range(rows)])

    for f in range(frames):
        cells = [own[f, r] for r in range(rows)]
        tiles = [own_beside(neighbour, f, r, cols) for r in range(rows)]
        put(HALO + f, [(c[:, :LANES], c[:, LANES:], *tile) for c, tile in zip(cells, tiles)])
    start, count = safe_rows(strips, rows)
    lefts = jnp.concatenate([columns(all_taps(t), lo, pairs, stacked, start, count) for t in range(frames)], axis=0)
    products = convolve(all_taps(0), [plane, middle, last], lefts)
    gain = gains[...]
    for t in range(frames):
        for r in range(count):
            h = hidden_row(join(products, (t * count + r) * width, width), gain, cols).astype(jnp.bfloat16)
            fill(h_lo, h_pairs, h_stacked, t, start + r, slice(0, width), h[:, :LANES], h[:, LANES:])
    for copy in copies:
        copy.wait()


def edge_kernel(strips, rows, cols, *refs):
    *refs, near_lo, near_pairs, near_stacked = refs
    *refs, h_lo, h_pairs, h_stacked, partial = refs
    *edges, block, edge_sums, safe_lo, safe_pairs, safe_stacked, plane, middle, gains, w2_first, w2_middle = refs
    frames, channels = edge_sums.shape[1], edge_sums.shape[-1]
    width, rest = cols + TILE, channels - LANES
    strip = lax.axis_index("strip")
    whole, strip_block = Packed(HALO, rows, cols), Packed(frames, HALO, cols)
    near = (near_lo, near_pairs, near_stacked)
    near_pairs[:, 2 * HALO] = jnp.zeros(near_pairs.shape[:1] + near_pairs.shape[2:], near_pairs.dtype)

    @pl.when(lax.axis_index("frame") == 0)
    def none_earlier():
        clear(near)

    gain = gains[...]
    for group, (edge, top) in enumerate(zip(edges, at_top(strips))):

        def own_row(f, r):
            low = pl.multiple_of((f * rows + r) * cols, TILE)
            high = pl.multiple_of(whole.high + (f * (rows // 2) + r // 2) * cols, TILE)
            pair = block[pl.ds(high, cols), :]
            return block[pl.ds(low, cols), :], pair, *beside_from(block, whole.beside, (f * rows + r) * HALO, rest)

        def halo_row(f, j):
            sent = frames - HALO + f
            return *strip_block.read(edge, sent, j, rest), *strip_block.read_beside(edge, sent, j, rest)

        def own_half(f, r, j):
            low, pair, *tile = own_row(f, r)
            return low, pair[:, (j % 2) * rest : (j % 2 + 1) * rest], *tile

        @if_earlier
        def build():
            every, beside = slice(0, cols), slice(cols, width)
            found = []
            for f in range(HALO):
                for j in range(HALO):
                    mine = own_half(f, (1 - top) * (rows - HALO) + j, j)
                    found += [(f, HALO * top + j, mine), (f, HALO * (1 - top) + j, halo_row(f, j))]
            for f, row, cells in found:
                fill(*near, f, row, every, *cells[:2])
                fill(*near, f, row, beside, *cells[2:])

        sums = [[edge_sums[group, t, r] for r in range(HALO)] for t in range(frames)]
        found = []
        for t in range(frames):
            taps = earlier_taps(t)
            products = convolve(taps, [plane, middle], columns(taps, *near, 0, HALO)) if taps else None
            for r in range(HALO):
                y = sums[t][r]
                if taps:
                    y = y + join(products, r * width, width)
                h = hidden_row(y, gain, cols)
                if strips != 2 and r == 1 - top:
                    h = h * jnp.where(strip == (0 if top else strips - 1), 0.0, 1.0)
                found.append((t, (1 - top) * rows + r, h.astype(jnp.bfloat16)))
        for t, row, h in found:
            fill(h_lo, h_pairs, h_stacked, t, row, slice(0, width), h[:, :LANES], h[:, LANES:])

    partial_sums(frames, (h_lo, h_pairs, h_stacked), [w2_first, w2_middle], rows, cols, partial)


def second_kernel(frames, rows, cols, h_lo, h_pairs, h_stacked, *refs):
    *w2, out = refs
    width = cols + TILE
    for t in range(frames):
        taps = [(f, f - t + 2) for f in range(max(0, t - 2), t + 1)]
        products = convolve(taps, w2, columns(taps, h_lo, h_pairs, h_stacked, 0, rows))
        for r in range(rows):
            out[t, r] = join(products, r * width, width)[:cols]


def finish_kernel(partial, own, gains, out_far, out, left):
    frames, rows, cols, channels = out.shape
    rest = channels - LANES
    gain = gains[...]

    sums = []
    for t in range(frames):
        y = own[t]
        if t < HALO:
            halves = [partial[t, rows + r // 2, :, (r % 2) * rest : (r % 2 + 1) * rest] for r in range(rows)]
            sent = [jnp.concatenate([partial[t, r], halves[r]], axis=-1) for r in range(rows)]
            y = y + jnp.stack(sent).astype(jnp.float32)
        sums.append(y.reshape(rows * cols, channels))
    results = [activate(y, gain).astype(jnp.bfloat16) for y in sums]
    copies = [pltpu.make_async_copy(out.at[t], out_far.at[t], left.at[t]) for t in range(frames)]
    for t in range(frames):
        out[t] = results[t].reshape(rows, cols, channels)
        copies[t].start()
    for copy in copies:
        copy.wait()


def call(kernel, name, ins, outs, scratch=(), semaphores=0, flops=0, far=(), far_out=False, alias=None):
    near, away = pl.BlockSpec(memory_space=pltpu.VMEM), pl.BlockSpec(memory_space=pltpu.HBM)
    in_specs, ins = [near] * len(ins), list(ins)
    for place in far:
        ins[place] = pltpu.with_memory_space_constraint(ins[place], pltpu.HBM)
        in_specs[place] = away
    one = not isinstance(outs, list)
    return pl.pallas_call(
        kernel,
        out_shape=outs,
        in_specs=in_specs,
        out_specs=(away if far_out else near) if one else [near] * len(outs),
        scratch_shapes=[pltpu.VMEM(shape, jnp.bfloat16) for shape in scratch]
        + [pltpu.SemaphoreType.DMA((semaphores,))] * (semaphores > 0),
        input_output_aliases=alias or {},
        compiler_params=pltpu.CompilerParams(vmem_limit_bytes=24 * 1024 * 1024),
        cost_estimate=pl.CostEstimate(flops=flops, bytes_accessed=4 * 1024 * 1024, transcendentals=0),
        name=name,
    )(*ins)


def block_scratch(frames, rows, width):
    return [(frames, rows, width, LANES), (frames, rows + 1, width, LANES), (frames - 1, rows, width, LANES)]


def shards(frames_in, weight_first, scale_first, weight_second, scale_second):
    frames, rows, cols, channels = frames_in.shape
    strips = lax.axis_size("strip")
    width = cols + TILE
    flops = frames * rows * cols * 27 * channels * channels
    bf16 = functools.partial(jax.ShapeDtypeStruct, dtype=jnp.bfloat16)
    f32 = functools.partial(jax.ShapeDtypeStruct, dtype=jnp.float32)

    plane_shape = bf16(weight_first.shape[1:])
    neighbour = swap(frames_in, "slab")
    own_in, middle, last = call(
        stage_kernel,
        "stage",
        [frames_in, weight_first],
        [bf16(frames_in.shape), plane_shape, plane_shape],
        semaphores=3,
        far=[0, 1],
    )
    edge_shape = bf16(Packed(frames, HALO, cols).shape)
    block, *edges = call(
        functools.partial(pack_kernel, strips),
        "pack",
        [own_in, neighbour],
        [bf16(Packed(HALO, rows, cols).shape)] + [edge_shape] * (1 if strips == 2 else 2),
    )
    ups = [(i, i + 1) for i in range(strips - 1)]
    downs = [(i + 1, i) for i in range(strips - 1)]
    ways = [[(0, 1), (1, 0)]] if strips == 2 else [ups, downs]
    before = forward(block)
    own_edges = [lax.ppermute(edge, "strip", way) for edge, way in zip(edges, ways)]
    before_edges = [forward(edge, way) for edge, way in zip(edges, ways)]
    edge_sums, plane = call(
        functools.partial(edge_own_kernel, strips),
        "edge_rows_own",
        [own_in, neighbour, *own_edges, middle, last, weight_first],
        [f32((len(ways), frames, HALO, width, channels)), plane_shape],
        block_scratch(frames + min(frames, 3) - 1, 2 * HALO, width),
        semaphores=1,
        flops=flops // 4,
        far=[-1],
    )
    gain_first = scale_first[None]
    h_shapes = [bf16(shape) for shape in block_scratch(frames, rows + 2, width)]
    partial_shape = bf16((HALO, rows + rows // 2, cols, LANES))
    *safe, w2_first, w2_middle, w2_last = call(
        functools.partial(safe_kernel, strips),
        "safe_rows",
        [own_in, neighbour, before, plane, middle, last, gain_first, weight_second],
        h_shapes + [plane_shape] * 3,
        block_scratch(HALO + frames, rows + 2 * HALO, width),
        semaphores=3,
        flops=flops,
        far=[-1],
    )
    h_lo, h_pairs, h_stacked, partial = call(
        functools.partial(edge_kernel, strips, rows, cols),
        "edge_rows",
        [*before_edges, before, edge_sums, *safe, plane, middle, gain_first, w2_first, w2_middle],
        h_shapes + [partial_shape],
        block_scratch(HALO, 2 * HALO, width),
        flops=flops,
        alias={len(before_edges) + 2 + k: k for k in range(3)},
    )
    sent = forward(partial)
    own = call(
        functools.partial(second_kernel, frames, rows, cols),
        "second_layer",
        [h_lo, h_pairs, h_stacked, w2_first, w2_middle, w2_last],
        f32((frames, rows, cols, channels)),
        flops=flops,
    )
    out = bf16(frames_in.shape)
    return call(
        finish_kernel,
        "finish",
        [sent, own, scale_second[None]],
        out,
        [out.shape],
        semaphores=frames,
        far_out=True,
    )


def solution(mesh):
    return jax.shard_map(
        shards,
        mesh=mesh,
        in_specs=(P(("groups", "frame"), "strip", "slab", None), P(), P(), P(), P()),
        out_specs=P(("groups", "frame"), "strip", "slab", None),
        check_vma=False,
    )
```

```python
import functools

import jax
import jax.numpy as jnp
from jax import lax
from jax.experimental import pallas as pl
from jax.experimental.pallas import tpu as pltpu
from jax.sharding import PartitionSpec as P

LANES = 128
TILE = 16
EPS = 1e-06


HALO = 2


def swap(x, axis):
    return lax.ppermute(x, axis, [(0, 1), (1, 0)])


def forward(x, way=None):
    steps, count = lax.axis_size("frame"), lax.axis_size("strip")
    way = [(i, i) for i in range(count)] if way is None else way
    pairs = [(f * count + i, (f + 1) * count + j) for f in range(steps - 1) for i, j in way]
    return lax.ppermute(x, ("frame", "strip"), pairs)


def if_earlier(build):
    pl.when(lax.axis_index("frame") > 0)(build)


class Packed:
    def __init__(self, frames, rows, cols):
        self.frames, self.rows, self.cols = frames, rows, cols
        self.high = frames * rows * cols
        self.beside = self.high + frames * (rows // 2) * cols
        self.tiles = -(-frames * rows * HALO // TILE)
        self.shared = frames * rows * HALO <= TILE // 2
        self.shape = (self.beside + (1 if self.shared else 2) * self.tiles * TILE, LANES)

    def low_at(self, f, r):
        return slice((f * self.rows + r) * self.cols, (f * self.rows + r + 1) * self.cols)

    def high_at(self, f, r):
        start = self.high + (f * (self.rows // 2) + r // 2) * self.cols
        return slice(start, start + self.cols)

    def spot(self, f, r):
        cell = (f * self.rows + r) * HALO
        return cell // TILE, cell % TILE

    def beside_at(self, tile, high):
        start = self.beside + (2 * tile + high) * TILE
        return slice(start, start + TILE)

    def write(self, out, cells, tile_of):
        slab = lax.axis_index("slab")
        at = lax.broadcasted_iota(jnp.int32, (TILE, 1), 0)
        sums = [None] * self.tiles
        for f in range(self.frames):
            for r in range(self.rows):
                row = cells(f, r)
                out[self.low_at(f, r), :] = row[:, :LANES]
                rest = row.shape[-1] - LANES
                half = slice((r % 2) * rest, (r % 2 + 1) * rest)
                out[self.high_at(f, r), half] = row[:, LANES:]
                tile, place = self.spot(f, r)
                moved = pltpu.roll(tile_of(f, r).astype(jnp.float32), lax.rem(place + HALO * slab, TILE), 0)
                moved = jnp.where((at >= place) & (at < place + HALO), moved, 0.0)
                sums[tile] = moved if sums[tile] is None else sums[tile] + moved
        if self.shared:
            low, high = sums[0][:, :LANES], sums[0][:, LANES:]
            high = jnp.concatenate([high, jnp.zeros((TILE, LANES - rest), jnp.float32)], axis=-1)
            both = jnp.where(at < TILE // 2, low, pltpu.roll(high, TILE // 2, 0))
            out[self.beside_at(0, 0), :] = both.astype(jnp.bfloat16)
            return
        for tile, cells_beside in enumerate(sums):
            cells_beside = cells_beside.astype(jnp.bfloat16)
            out[self.beside_at(tile, 0), :] = cells_beside[:, :LANES]
            out[self.beside_at(tile, 1), :rest] = cells_beside[:, LANES:]

    def read(self, ref, f, r, rest):
        half = slice((r % 2) * rest, (r % 2 + 1) * rest)
        return ref[self.low_at(f, r), :], ref[self.high_at(f, r), half]

    def read_beside(self, ref, f, r, rest):
        return beside_from(ref, self.beside, (f * self.rows + r) * HALO, rest, self.shared)


def beside_from(ref, start, cell, rest, shared=False):
    slab = lax.axis_index("slab")
    parts = []
    for high, lanes in ((0, LANES), (1, rest)):
        at = start if shared else start + (2 * (cell // TILE) + high) * TILE
        below = TILE // 2 if shared and high else 0
        cells = ref[pl.ds(pl.multiple_of(at, TILE), TILE), :].astype(jnp.float32)
        cells = pltpu.roll(cells, lax.rem(2 * TILE - cell % TILE - below - HALO * slab, TILE), 0)
        parts.append(only_beside(cells).astype(jnp.bfloat16)[:, :lanes])
    return parts


def only_beside(tile):
    slab = lax.axis_index("slab")
    at = lax.broadcasted_iota(jnp.int32, tile.shape, 0)
    begin = slab * (TILE - HALO)
    return jnp.where((at >= begin) & (at < begin + HALO), tile, 0.0)


def fill(lo, pairs, stacked, frame, row, cols, low, high):
    rest = high.shape[-1]
    lo[frame, row, cols, :] = low
    pairs[frame, row + 1, cols, :rest] = high
    pairs[frame, row, cols, rest:] = high
    if frame < stacked.shape[0]:
        stacked[frame, row, cols, :rest] = high
    if frame > 0:
        stacked[frame - 1, row, cols, rest:] = high


def columns(taps, lo, pairs, stacked, row, rows):
    def flat(block):
        return block.reshape(-1, LANES)

    pieces = [flat(lo[f, pl.ds(row + b, rows)]) for f, _ in taps for b in range(3)]
    pieces += [flat(pairs[f, pl.ds(row + 1, rows)]) for f, _ in taps]
    for k in range(0, len(taps), 2):
        f = taps[k][0]
        if k + 1 < len(taps):
            pieces.append(flat(stacked[f, pl.ds(row + 2, rows)]))
        else:
            pieces.append(flat(pairs[f, pl.ds(row + 3, rows)]))
    return jnp.concatenate(pieces, axis=-1)


def planes(taps, weight, c):
    pieces = [weight[a][b, c, :LANES, :] for _, a in taps for b in range(3)]
    for _, a in taps:
        pieces += [weight[a][0, c, LANES:, :], weight[a][1, c, LANES:, :]]
    for _, a in taps:
        pieces.append(weight[a][2, c, LANES:, :])
    if len(taps) % 2:
        pieces.append(jnp.zeros_like(weight[a][0, c, LANES:, :]))
    return jnp.concatenate(pieces, axis=0)


def convolve(taps, weight, lefts):
    return [
        jnp.dot(lefts, planes(taps, weight, c), preferred_element_type=jnp.float32)
        for c in range(3)
    ]


def join(products, start, width):
    before, middle, after = [p[start : start + width] for p in products]
    return pltpu.roll(before, 1, 0) + middle + pltpu.roll(after, width - 1, 0)


def activate(y, gains):
    mean_square = jnp.sum(y * y, axis=-1, keepdims=True) * (1.0 / y.shape[-1])
    v = y * lax.rsqrt(mean_square + EPS) * gains
    half = 0.5 * v
    return half + half * jnp.tanh(half)


def clear(buffers):
    for buffer in buffers:
        buffer[...] = jnp.zeros_like(buffer)


def clear_rows(buffers, above, below):
    lo, pairs, stacked = buffers
    for buffer, rows in ((lo, (above, below)), (pairs, (above, above + 1, below, below + 1)), (stacked, (above, below))):
        for row in rows:
            buffer[:, row] = jnp.zeros(buffer.shape[:1] + buffer.shape[2:], buffer.dtype)


def facing(strips, rows):
    if strips == 2:
        return [jnp.where(lax.axis_index("strip") == 0, rows - HALO, 0)]
    return [rows - HALO, 0]


def at_top(strips):
    return [lax.axis_index("strip")] if strips == 2 else [1, 0]


def safe_rows(strips, rows):
    return (1 + lax.axis_index("strip"), rows - 1) if strips == 2 else (2, rows - 2)


def beside_of(neighbour, f, r, cols):
    start = pl.multiple_of(lax.axis_index("slab") * (cols - TILE), TILE)
    return neighbour[f, r, pl.ds(start, TILE), :]


def stage_kernel(own_far, weight_far, own, middle, last, arrived):
    copies = [
        pltpu.make_async_copy(own_far, own, arrived.at[0]),
        pltpu.make_async_copy(weight_far.at[2], last, arrived.at[1]),
        pltpu.make_async_copy(weight_far.at[1], middle, arrived.at[2]),
    ]
    for copy in copies:
        copy.start()
    for copy in copies:
        copy.wait()


def pack_kernel(strips, own, neighbour, block, *edges):
    frames, rows, cols, _ = own.shape
    whole = Packed(HALO, rows, cols)
    skip = frames - HALO
    whole.write(block, lambda f, r: own[f + skip, r], lambda f, r: beside_of(neighbour, f + skip, r, cols))
    for start, edge in zip(facing(strips, rows), edges):
        Packed(frames, HALO, cols).write(
            edge, lambda f, r: own[f, start + r], lambda f, r: beside_of(neighbour, f, start + r, cols)
        )


def own_beside(neighbour, f, r, cols):
    tile = only_beside(beside_of(neighbour, f, r, cols).astype(jnp.float32)).astype(jnp.bfloat16)
    return tile[:, :LANES], tile[:, LANES:]


def window(buffers, skip, frames, top, rows, cols, own, halo):
    every, beside = slice(0, cols), slice(cols, cols + TILE)
    for f in range(frames):
        found = []
        for j in range(HALO):
            found.append((HALO * top + j, own(f, (1 - top) * (rows - HALO) + j)))
            found.append((HALO * (1 - top) + j, halo(f, j)))
        for row, cells in found:
            fill(*buffers, skip + f, row, every, *cells[:2])
            fill(*buffers, skip + f, row, beside, *cells[2:])


def edge_own_kernel(strips, *refs):
    *refs, near_lo, near_pairs, near_stacked, arrived = refs
    own, neighbour, *edges, middle, last, weight_far, edge_sums, plane = refs
    frames, rows, cols, channels = own.shape
    width, rest = cols + TILE, channels - LANES
    copy = pltpu.make_async_copy(weight_far.at[0], plane, arrived.at[0])
    copy.start()
    if frames > 2:
        copy.wait()
    strip_block = Packed(frames, HALO, cols)
    near = (near_lo, near_pairs, near_stacked)
    span = min(frames, 3)
    zeros = span - 1
    clear((near_pairs,))
    for buffer in (near_lo, near_stacked):
        buffer[:zeros] = jnp.zeros((zeros,) + buffer.shape[1:], buffer.dtype)
    for group, (edge, top) in enumerate(zip(edges, at_top(strips))):

        def own_row(f, r):
            cells = own[f, r]
            return cells[:, :LANES], cells[:, LANES:], *own_beside(neighbour, f, r, cols)

        def halo_row(f, j):
            return *strip_block.read(edge, f, j, rest), *strip_block.read_beside(edge, f, j, rest)

        window(near, zeros, frames, top, rows, cols, own_row, halo_row)
        lefts = [columns([(t + k, 3 - span + k) for k in range(span)], *near, 0, HALO) for t in range(frames)]
        taps = [(k, 3 - span + k) for k in range(span)]
        products = convolve(taps, [plane, middle, last], jnp.concatenate(lefts, axis=0))
        for t in range(frames):
            for r in range(HALO):
                edge_sums[group, t, r] = join(products, (t * HALO + r) * width, width)
    if frames <= 2:
        copy.wait()


def own_taps(t):
    return [(f, f - t + 2) for f in range(max(0, t - 2), t + 1)]


def earlier_taps(t):
    return [(f, f - t) for f in range(t, HALO)]


def hidden_row(y, gain, cols):
    width, slab = y.shape[0], lax.axis_index("slab")
    position = lax.broadcasted_iota(jnp.int32, (width, 1), 0)
    right = cols + (slab == 0).astype(jnp.int32)
    left = width - (slab == 1).astype(jnp.int32)
    return jnp.where((position < right) | (position >= left), activate(y, gain), 0.0)


def all_taps(t):
    return [(t, 0), (t + 1, 1), (t + 2, 2)]


def partial_sums(frames, hidden, w2, rows, cols, partial):
    width, last = cols + TILE, frames - 1
    for t, taps in enumerate(([(last - 1, 0), (last, 1)], [(last, 0)])):
        products = convolve(taps, w2, columns(taps, *hidden, 0, rows))
        for r in range(rows):
            y = join(products, r * width, width)[:cols].astype(jnp.bfloat16)
            rest = y.shape[-1] - LANES
            partial[t, r] = y[:, :LANES]
            half = slice((r % 2) * rest, (r % 2 + 1) * rest)
            partial[t, rows + r // 2, :, half] = y[:, LANES:]


def safe_kernel(strips, *refs):
    *refs, lo, pairs, stacked, arrived = refs
    own, neighbour, block, plane, middle, last, gains, w2_far, h_lo, h_pairs, h_stacked, *w2 = refs
    copies = [pltpu.make_async_copy(w2_far.at[a], w2[a], arrived.at[a]) for a in range(3)]
    for copy in copies:
        copy.start()
    frames, rows, cols, channels = own.shape
    width, rest = cols + TILE, channels - LANES
    every, beside = slice(0, cols), slice(cols, width)
    clear_rows((lo, pairs, stacked), HALO - 1, HALO + rows)
    clear_rows((h_lo, h_pairs, h_stacked), 0, rows + 1)
    whole = Packed(HALO, rows, cols)

    @pl.when(lax.axis_index("frame") == 0)
    def none_earlier():
        for buffer in (lo, pairs, stacked):
            buffer[:HALO] = jnp.zeros((HALO,) + buffer.shape[1:], buffer.dtype)

    def put(frame, rows_of):
        for r, cells in enumerate(rows_of):
            fill(lo, pairs, stacked, frame, r + HALO, every, *cells[:2])
            fill(lo, pairs, stacked, frame, r + HALO, beside, *cells[2:])

    @if_earlier
    def build():
        for f in range(HALO):
            put(f, [(*whole.read(block, f, r, rest), *whole.read_beside(block, f, r, rest)) for r in range(rows)])

    for f in range(frames):
        cells = [own[f, r] for r in range(rows)]
        tiles = [own_beside(neighbour, f, r, cols) for r in range(rows)]
        put(HALO + f, [(c[:, :LANES], c[:, LANES:], *tile) for c, tile in zip(cells, tiles)])
    start, count = safe_rows(strips, rows)
    lefts = jnp.concatenate([columns(all_taps(t), lo, pairs, stacked, start, count) for t in range(frames)], axis=0)
    products = convolve(all_taps(0), [plane, middle, last], lefts)
    gain = gains[...]
    for t in range(frames):
        for r in range(count):
            h = hidden_row(join(products, (t * count + r) * width, width), gain, cols).astype(jnp.bfloat16)
            fill(h_lo, h_pairs, h_stacked, t, start + r, slice(0, width), h[:, :LANES], h[:, LANES:])
    for copy in copies:
        copy.wait()


def edge_kernel(strips, rows, cols, *refs):
    *refs, near_lo, near_pairs, near_stacked = refs
    *refs, h_lo, h_pairs, h_stacked, partial = refs
    *edges, block, edge_sums, safe_lo, safe_pairs, safe_stacked, plane, middle, gains, w2_first, w2_middle = refs
    frames, channels = edge_sums.shape[1], edge_sums.shape[-1]
    width, rest = cols + TILE, channels - LANES
    strip = lax.axis_index("strip")
    whole, strip_block = Packed(HALO, rows, cols), Packed(frames, HALO, cols)
    near = (near_lo, near_pairs, near_stacked)
    near_pairs[:, 2 * HALO] = jnp.zeros(near_pairs.shape[:1] + near_pairs.shape[2:], near_pairs.dtype)

    @pl.when(lax.axis_index("frame") == 0)
    def none_earlier():
        clear(near)

    gain = gains[...]
    for group, (edge, top) in enumerate(zip(edges, at_top(strips))):

        def own_row(f, r):
            low = pl.multiple_of((f * rows + r) * cols, TILE)
            high = pl.multiple_of(whole.high + (f * (rows // 2) + r // 2) * cols, TILE)
            pair = block[pl.ds(high, cols), :]
            return block[pl.ds(low, cols), :], pair, *beside_from(block, whole.beside, (f * rows + r) * HALO, rest)

        def halo_row(f, j):
            sent = frames - HALO + f
            return *strip_block.read(edge, sent, j, rest), *strip_block.read_beside(edge, sent, j, rest)

        def own_half(f, r, j):
            low, pair, *tile = own_row(f, r)
            return low, pair[:, (j % 2) * rest : (j % 2 + 1) * rest], *tile

        @if_earlier
        def build():
            every, beside = slice(0, cols), slice(cols, width)
            found = []
            for f in range(HALO):
                for j in range(HALO):
                    mine = own_half(f, (1 - top) * (rows - HALO) + j, j)
                    found += [(f, HALO * top + j, mine), (f, HALO * (1 - top) + j, halo_row(f, j))]
            for f, row, cells in found:
                fill(*near, f, row, every, *cells[:2])
                fill(*near, f, row, beside, *cells[2:])

        sums = [[edge_sums[group, t, r] for r in range(HALO)] for t in range(frames)]
        found = []
        for t in range(frames):
            taps = earlier_taps(t)
            products = convolve(taps, [plane, middle], columns(taps, *near, 0, HALO)) if taps else None
            for r in range(HALO):
                y = sums[t][r]
                if taps:
                    y = y + join(products, r * width, width)
                h = hidden_row(y, gain, cols)
                if strips != 2 and r == 1 - top:
                    h = h * jnp.where(strip == (0 if top else strips - 1), 0.0, 1.0)
                found.append((t, (1 - top) * rows + r, h.astype(jnp.bfloat16)))
        for t, row, h in found:
            fill(h_lo, h_pairs, h_stacked, t, row, slice(0, width), h[:, :LANES], h[:, LANES:])

    partial_sums(frames, (h_lo, h_pairs, h_stacked), [w2_first, w2_middle], rows, cols, partial)


def second_kernel(frames, rows, cols, h_lo, h_pairs, h_stacked, *refs):
    *w2, out = refs
    width = cols + TILE
    for t in range(frames):
        taps = [(f, f - t + 2) for f in range(max(0, t - 2), t + 1)]
        products = convolve(taps, w2, columns(taps, h_lo, h_pairs, h_stacked, 0, rows))
        for r in range(rows):
            out[t, r] = join(products, r * width, width)[:cols]


def finish_kernel(partial, own, gains, out_far, out, left):
    frames, rows, cols, channels = out.shape
    rest = channels - LANES
    gain = gains[...]

    sums = []
    for t in range(frames):
        y = own[t]
        if t < HALO:
            halves = [partial[t, rows + r // 2, :, (r % 2) * rest : (r % 2 + 1) * rest] for r in range(rows)]
            sent = [jnp.concatenate([partial[t, r], halves[r]], axis=-1) for r in range(rows)]
            y = y + jnp.stack(sent).astype(jnp.float32)
        sums.append(y.reshape(rows * cols, channels))
    results = [activate(y, gain).astype(jnp.bfloat16) for y in sums]
    copies = [pltpu.make_async_copy(out.at[t], out_far.at[t], left.at[t]) for t in range(frames)]
    for t in range(frames):
        out[t] = results[t].reshape(rows, cols, channels)
        copies[t].start()
    for copy in copies:
        copy.wait()


def call(kernel, name, ins, outs, scratch=(), semaphores=0, flops=0, far=(), far_out=False, alias=None):
    near, away = pl.BlockSpec(memory_space=pltpu.VMEM), pl.BlockSpec(memory_space=pltpu.HBM)
    in_specs, ins = [near] * len(ins), list(ins)
    for place in far:
        ins[place] = pltpu.with_memory_space_constraint(ins[place], pltpu.HBM)
        in_specs[place] = away
    one = not isinstance(outs, list)
    return pl.pallas_call(
        kernel,
        out_shape=outs,
        in_specs=in_specs,
        out_specs=(away if far_out else near) if one else [near] * len(outs),
        scratch_shapes=[pltpu.VMEM(shape, jnp.bfloat16) for shape in scratch]
        + [pltpu.SemaphoreType.DMA((semaphores,))] * (semaphores > 0),
        input_output_aliases=alias or {},
        compiler_params=pltpu.CompilerParams(vmem_limit_bytes=24 * 1024 * 1024),
        cost_estimate=pl.CostEstimate(flops=flops, bytes_accessed=4 * 1024 * 1024, transcendentals=0),
        name=name,
    )(*ins)


def block_scratch(frames, rows, width):
    return [(frames, rows, width, LANES), (frames, rows + 1, width, LANES), (frames - 1, rows, width, LANES)]


def shards(frames_in, weight_first, scale_first, weight_second, scale_second):
    frames, rows, cols, channels = frames_in.shape
    strips = lax.axis_size("strip")
    width = cols + TILE
    flops = frames * rows * cols * 27 * channels * channels
    bf16 = functools.partial(jax.ShapeDtypeStruct, dtype=jnp.bfloat16)
    f32 = functools.partial(jax.ShapeDtypeStruct, dtype=jnp.float32)

    plane_shape = bf16(weight_first.shape[1:])
    neighbour = swap(frames_in, "slab")
    own_in, middle, last = call(
        stage_kernel,
        "stage",
        [frames_in, weight_first],
        [bf16(frames_in.shape), plane_shape, plane_shape],
        semaphores=3,
        far=[0, 1],
    )
    edge_shape = bf16(Packed(frames, HALO, cols).shape)
    block, *edges = call(
        functools.partial(pack_kernel, strips),
        "pack",
        [own_in, neighbour],
        [bf16(Packed(HALO, rows, cols).shape)] + [edge_shape] * (1 if strips == 2 else 2),
    )
    ups = [(i, i + 1) for i in range(strips - 1)]
    downs = [(i + 1, i) for i in range(strips - 1)]
    ways = [[(0, 1), (1, 0)]] if strips == 2 else [ups, downs]
    before = forward(block)
    own_edges = [lax.ppermute(edge, "strip", way) for edge, way in zip(edges, ways)]
    before_edges = [forward(edge, way) for edge, way in zip(edges, ways)]
    edge_sums, plane = call(
        functools.partial(edge_own_kernel, strips),
        "edge_rows_own",
        [own_in, neighbour, *own_edges, middle, last, weight_first],
        [f32((len(ways), frames, HALO, width, channels)), plane_shape],
        block_scratch(frames + min(frames, 3) - 1, 2 * HALO, width),
        semaphores=1,
        flops=flops // 4,
        far=[-1],
    )
    gain_first = scale_first[None]
    h_shapes = [bf16(shape) for shape in block_scratch(frames, rows + 2, width)]
    partial_shape = bf16((HALO, rows + rows // 2, cols, LANES))
    *safe, w2_first, w2_middle, w2_last = call(
        functools.partial(safe_kernel, strips),
        "safe_rows",
        [own_in, neighbour, before, plane, middle, last, gain_first, weight_second],
        h_shapes + [plane_shape] * 3,
        block_scratch(HALO + frames, rows + 2 * HALO, width),
        semaphores=3,
        flops=flops,
        far=[-1],
    )
    h_lo, h_pairs, h_stacked, partial = call(
        functools.partial(edge_kernel, strips, rows, cols),
        "edge_rows",
        [*before_edges, before, edge_sums, *safe, plane, middle, gain_first, w2_first, w2_middle],
        h_shapes + [partial_shape],
        block_scratch(HALO, 2 * HALO, width),
        flops=flops,
        alias={len(before_edges) + 2 + k: k for k in range(3)},
    )
    sent = forward(partial)
    own = call(
        functools.partial(second_kernel, frames, rows, cols),
        "second_layer",
        [h_lo, h_pairs, h_stacked, w2_first, w2_middle, w2_last],
        f32((frames, rows, cols, channels)),
        flops=flops,
    )
    out = bf16(frames_in.shape)
    return call(
        finish_kernel,
        "finish",
        [sent, own, scale_second[None]],
        out,
        [out.shape],
        semaphores=frames,
        far_out=True,
    )


def solution(mesh):
    return jax.shard_map(
        shards,
        mesh=mesh,
        in_specs=(P(("groups", "frame"), "strip", "slab", None), P(), P(), P(), P()),
        out_specs=P(("groups", "frame"), "strip", "slab", None),
        check_vma=False,
    )
```

```python
import functools

import jax
import jax.numpy as jnp
from jax import lax
from jax.experimental import pallas as pl
from jax.experimental.pallas import tpu as pltpu
from jax.sharding import PartitionSpec as P

LANES = 128
TILE = 16
EPS = 1e-06


HALO = 2


def swap(x, axis):
    return lax.ppermute(x, axis, [(0, 1), (1, 0)])


def forward(x, way=None):
    steps, count = lax.axis_size("frame"), lax.axis_size("strip")
    way = [(i, i) for i in range(count)] if way is None else way
    pairs = [(f * count + i, (f + 1) * count + j) for f in range(steps - 1) for i, j in way]
    return lax.ppermute(x, ("frame", "strip"), pairs)


def if_earlier(build):
    pl.when(lax.axis_index("frame") > 0)(build)


class Packed:
    def __init__(self, frames, rows, cols):
        self.frames, self.rows, self.cols = frames, rows, cols
        self.high = frames * rows * cols
        self.beside = self.high + frames * (rows // 2) * cols
        self.tiles = -(-frames * rows * HALO // TILE)
        self.shared = frames * rows * HALO <= TILE // 2
        self.shape = (self.beside + (1 if self.shared else 2) * self.tiles * TILE, LANES)

    def low_at(self, f, r):
        return slice((f * self.rows + r) * self.cols, (f * self.rows + r + 1) * self.cols)

    def high_at(self, f, r):
        start = self.high + (f * (self.rows // 2) + r // 2) * self.cols
        return slice(start, start + self.cols)

    def spot(self, f, r):
        cell = (f * self.rows + r) * HALO
        return cell // TILE, cell % TILE

    def beside_at(self, tile, high):
        start = self.beside + (2 * tile + high) * TILE
        return slice(start, start + TILE)

    def write(self, out, cells, tile_of):
        slab = lax.axis_index("slab")
        at = lax.broadcasted_iota(jnp.int32, (TILE, 1), 0)
        sums = [None] * self.tiles
        for f in range(self.frames):
            for r in range(self.rows):
                row = cells(f, r)
                out[self.low_at(f, r), :] = row[:, :LANES]
                rest = row.shape[-1] - LANES
                half = slice((r % 2) * rest, (r % 2 + 1) * rest)
                out[self.high_at(f, r), half] = row[:, LANES:]
                tile, place = self.spot(f, r)
                moved = pltpu.roll(tile_of(f, r).astype(jnp.float32), lax.rem(place + HALO * slab, TILE), 0)
                moved = jnp.where((at >= place) & (at < place + HALO), moved, 0.0)
                sums[tile] = moved if sums[tile] is None else sums[tile] + moved
        if self.shared:
            low, high = sums[0][:, :LANES], sums[0][:, LANES:]
            high = jnp.concatenate([high, jnp.zeros((TILE, LANES - rest), jnp.float32)], axis=-1)
            both = jnp.where(at < TILE // 2, low, pltpu.roll(high, TILE // 2, 0))
            out[self.beside_at(0, 0), :] = both.astype(jnp.bfloat16)
            return
        for tile, cells_beside in enumerate(sums):
            cells_beside = cells_beside.astype(jnp.bfloat16)
            out[self.beside_at(tile, 0), :] = cells_beside[:, :LANES]
            out[self.beside_at(tile, 1), :rest] = cells_beside[:, LANES:]

    def read(self, ref, f, r, rest):
        half = slice((r % 2) * rest, (r % 2 + 1) * rest)
        return ref[self.low_at(f, r), :], ref[self.high_at(f, r), half]

    def read_beside(self, ref, f, r, rest):
        return beside_from(ref, self.beside, (f * self.rows + r) * HALO, rest, self.shared)


def beside_from(ref, start, cell, rest, shared=False):
    slab = lax.axis_index("slab")
    parts = []
    for high, lanes in ((0, LANES), (1, rest)):
        at = start if shared else start + (2 * (cell // TILE) + high) * TILE
        below = TILE // 2 if shared and high else 0
        cells = ref[pl.ds(pl.multiple_of(at, TILE), TILE), :].astype(jnp.float32)
        cells = pltpu.roll(cells, lax.rem(2 * TILE - cell % TILE - below - HALO * slab, TILE), 0)
        parts.append(only_beside(cells).astype(jnp.bfloat16)[:, :lanes])
    return parts


def only_beside(tile):
    slab = lax.axis_index("slab")
    at = lax.broadcasted_iota(jnp.int32, tile.shape, 0)
    begin = slab * (TILE - HALO)
    return jnp.where((at >= begin) & (at < begin + HALO), tile, 0.0)


def fill(lo, pairs, stacked, frame, row, cols, low, high):
    rest = high.shape[-1]
    lo[frame, row, cols, :] = low
    pairs[frame, row + 1, cols, :rest] = high
    pairs[frame, row, cols, rest:] = high
    if frame < stacked.shape[0]:
        stacked[frame, row, cols, :rest] = high
    if frame > 0:
        stacked[frame - 1, row, cols, rest:] = high


def columns(taps, lo, pairs, stacked, row, rows):
    def flat(block):
        return block.reshape(-1, LANES)

    pieces = [flat(lo[f, pl.ds(row + b, rows)]) for f, _ in taps for b in range(3)]
    pieces += [flat(pairs[f, pl.ds(row + 1, rows)]) for f, _ in taps]
    for k in range(0, len(taps), 2):
        f = taps[k][0]
        if k + 1 < len(taps):
            pieces.append(flat(stacked[f, pl.ds(row + 2, rows)]))
        else:
            pieces.append(flat(pairs[f, pl.ds(row + 3, rows)]))
    return jnp.concatenate(pieces, axis=-1)


def planes(taps, weight, c):
    pieces = [weight[a][b, c, :LANES, :] for _, a in taps for b in range(3)]
    for _, a in taps:
        pieces += [weight[a][0, c, LANES:, :], weight[a][1, c, LANES:, :]]
    for _, a in taps:
        pieces.append(weight[a][2, c, LANES:, :])
    if len(taps) % 2:
        pieces.append(jnp.zeros_like(weight[a][0, c, LANES:, :]))
    return jnp.concatenate(pieces, axis=0)


def convolve(taps, weight, lefts):
    return [
        jnp.dot(lefts, planes(taps, weight, c), preferred_element_type=jnp.float32)
        for c in range(3)
    ]


def join(products, start, width):
    before, middle, after = [p[start : start + width] for p in products]
    return pltpu.roll(before, 1, 0) + middle + pltpu.roll(after, width - 1, 0)


def activate(y, gains):
    mean_square = jnp.sum(y * y, axis=-1, keepdims=True) * (1.0 / y.shape[-1])
    v = y * lax.rsqrt(mean_square + EPS) * gains
    return v / (1.0 + jnp.exp(-v))


def clear(buffers):
    for buffer in buffers:
        buffer[...] = jnp.zeros_like(buffer)


def clear_rows(buffers, above, below):
    lo, pairs, stacked = buffers
    for buffer, rows in ((lo, (above, below)), (pairs, (above, above + 1, below, below + 1)), (stacked, (above, below))):
        for row in rows:
            buffer[:, row] = jnp.zeros(buffer.shape[:1] + buffer.shape[2:], buffer.dtype)


def facing(strips, rows):
    if strips == 2:
        return [jnp.where(lax.axis_index("strip") == 0, rows - HALO, 0)]
    return [rows - HALO, 0]


def at_top(strips):
    return [lax.axis_index("strip")] if strips == 2 else [1, 0]


def safe_rows(strips, rows):
    return (1 + lax.axis_index("strip"), rows - 1) if strips == 2 else (2, rows - 2)


def beside_of(neighbour, f, r, cols):
    start = pl.multiple_of(lax.axis_index("slab") * (cols - TILE), TILE)
    return neighbour[f, r, pl.ds(start, TILE), :]


def stage_kernel(own_far, weight_far, own, middle, last, arrived):
    copies = [
        pltpu.make_async_copy(own_far, own, arrived.at[0]),
        pltpu.make_async_copy(weight_far.at[2], last, arrived.at[1]),
        pltpu.make_async_copy(weight_far.at[1], middle, arrived.at[2]),
    ]
    for copy in copies:
        copy.start()
    for copy in copies:
        copy.wait()


def pack_kernel(strips, own, neighbour, block, *edges):
    frames, rows, cols, _ = own.shape
    whole = Packed(HALO, rows, cols)
    skip = frames - HALO
    whole.write(block, lambda f, r: own[f + skip, r], lambda f, r: beside_of(neighbour, f + skip, r, cols))
    for start, edge in zip(facing(strips, rows), edges):
        Packed(frames, HALO, cols).write(
            edge, lambda f, r: own[f, start + r], lambda f, r: beside_of(neighbour, f, start + r, cols)
        )


def own_beside(neighbour, f, r, cols):
    tile = only_beside(beside_of(neighbour, f, r, cols).astype(jnp.float32)).astype(jnp.bfloat16)
    return tile[:, :LANES], tile[:, LANES:]


def window(buffers, skip, frames, top, rows, cols, own, halo):
    every, beside = slice(0, cols), slice(cols, cols + TILE)
    for f in range(frames):
        found = []
        for j in range(HALO):
            found.append((HALO * top + j, own(f, (1 - top) * (rows - HALO) + j)))
            found.append((HALO * (1 - top) + j, halo(f, j)))
        for row, cells in found:
            fill(*buffers, skip + f, row, every, *cells[:2])
            fill(*buffers, skip + f, row, beside, *cells[2:])


def edge_own_kernel(strips, *refs):
    *refs, near_lo, near_pairs, near_stacked, arrived = refs
    own, neighbour, *edges, middle, last, weight_far, edge_sums, plane = refs
    frames, rows, cols, channels = own.shape
    width, rest = cols + TILE, channels - LANES
    copy = pltpu.make_async_copy(weight_far.at[0], plane, arrived.at[0])
    copy.start()
    if frames > 2:
        copy.wait()
    strip_block = Packed(frames, HALO, cols)
    near = (near_lo, near_pairs, near_stacked)
    span = min(frames, 3)
    zeros = span - 1
    clear((near_pairs,))
    for buffer in (near_lo, near_stacked):
        buffer[:zeros] = jnp.zeros((zeros,) + buffer.shape[1:], buffer.dtype)
    for group, (edge, top) in enumerate(zip(edges, at_top(strips))):

        def own_row(f, r):
            cells = own[f, r]
            return cells[:, :LANES], cells[:, LANES:], *own_beside(neighbour, f, r, cols)

        def halo_row(f, j):
            return *strip_block.read(edge, f, j, rest), *strip_block.read_beside(edge, f, j, rest)

        window(near, zeros, frames, top, rows, cols, own_row, halo_row)
        lefts = [columns([(t + k, 3 - span + k) for k in range(span)], *near, 0, HALO) for t in range(frames)]
        taps = [(k, 3 - span + k) for k in range(span)]
        products = convolve(taps, [plane, middle, last], jnp.concatenate(lefts, axis=0))
        for t in range(frames):
            for r in range(HALO):
                edge_sums[group, t, r] = join(products, (t * HALO + r) * width, width)
    if frames <= 2:
        copy.wait()


def own_taps(t):
    return [(f, f - t + 2) for f in range(max(0, t - 2), t + 1)]


def earlier_taps(t):
    return [(f, f - t) for f in range(t, HALO)]


def hidden_row(y, gain, cols):
    width, slab = y.shape[0], lax.axis_index("slab")
    position = lax.broadcasted_iota(jnp.int32, (width, 1), 0)
    right = cols + (slab == 0).astype(jnp.int32)
    left = width - (slab == 1).astype(jnp.int32)
    return jnp.where((position < right) | (position >= left), activate(y, gain), 0.0)


def all_taps(t):
    return [(t, 0), (t + 1, 1), (t + 2, 2)]


def partial_sums(frames, hidden, w2, rows, cols, partial):
    width, last = cols + TILE, frames - 1
    for t, taps in enumerate(([(last - 1, 0), (last, 1)], [(last, 0)])):
        products = convolve(taps, w2, columns(taps, *hidden, 0, rows))
        for r in range(rows):
            y = join(products, r * width, width)[:cols].astype(jnp.bfloat16)
            rest = y.shape[-1] - LANES
            partial[t, r] = y[:, :LANES]
            half = slice((r % 2) * rest, (r % 2 + 1) * rest)
            partial[t, rows + r // 2, :, half] = y[:, LANES:]


def safe_kernel(strips, *refs):
    *refs, lo, pairs, stacked, arrived = refs
    own, neighbour, block, plane, middle, last, gains, w2_far, h_lo, h_pairs, h_stacked, *w2 = refs
    copies = [pltpu.make_async_copy(w2_far.at[a], w2[a], arrived.at[a]) for a in range(3)]
    for copy in copies:
        copy.start()
    frames, rows, cols, channels = own.shape
    width, rest = cols + TILE, channels - LANES
    every, beside = slice(0, cols), slice(cols, width)
    clear_rows((lo, pairs, stacked), HALO - 1, HALO + rows)
    clear_rows((h_lo, h_pairs, h_stacked), 0, rows + 1)
    whole = Packed(HALO, rows, cols)

    @pl.when(lax.axis_index("frame") == 0)
    def none_earlier():
        for buffer in (lo, pairs, stacked):
            buffer[:HALO] = jnp.zeros((HALO,) + buffer.shape[1:], buffer.dtype)

    def put(frame, rows_of):
        for r, cells in enumerate(rows_of):
            fill(lo, pairs, stacked, frame, r + HALO, every, *cells[:2])
            fill(lo, pairs, stacked, frame, r + HALO, beside, *cells[2:])

    @if_earlier
    def build():
        for f in range(HALO):
            put(f, [(*whole.read(block, f, r, rest), *whole.read_beside(block, f, r, rest)) for r in range(rows)])

    for f in range(frames):
        cells = [own[f, r] for r in range(rows)]
        tiles = [own_beside(neighbour, f, r, cols) for r in range(rows)]
        put(HALO + f, [(c[:, :LANES], c[:, LANES:], *tile) for c, tile in zip(cells, tiles)])
    start, count = safe_rows(strips, rows)
    lefts = jnp.concatenate([columns(all_taps(t), lo, pairs, stacked, start, count) for t in range(frames)], axis=0)
    products = convolve(all_taps(0), [plane, middle, last], lefts)
    gain = gains[...]
    for t in range(frames):
        for r in range(count):
            h = hidden_row(join(products, (t * count + r) * width, width), gain, cols).astype(jnp.bfloat16)
            fill(h_lo, h_pairs, h_stacked, t, start + r, slice(0, width), h[:, :LANES], h[:, LANES:])
    for copy in copies:
        copy.wait()


def edge_kernel(strips, rows, cols, *refs):
    *refs, near_lo, near_pairs, near_stacked = refs
    *refs, h_lo, h_pairs, h_stacked, partial = refs
    *edges, block, edge_sums, safe_lo, safe_pairs, safe_stacked, plane, middle, gains, w2_first, w2_middle = refs
    frames, channels = edge_sums.shape[1], edge_sums.shape[-1]
    width, rest = cols + TILE, channels - LANES
    strip = lax.axis_index("strip")
    whole, strip_block = Packed(HALO, rows, cols), Packed(frames, HALO, cols)
    near = (near_lo, near_pairs, near_stacked)
    near_pairs[:, 2 * HALO] = jnp.zeros(near_pairs.shape[:1] + near_pairs.shape[2:], near_pairs.dtype)

    @pl.when(lax.axis_index("frame") == 0)
    def none_earlier():
        clear(near)

    gain = gains[...]
    for group, (edge, top) in enumerate(zip(edges, at_top(strips))):

        def own_row(f, r):
            low = pl.multiple_of((f * rows + r) * cols, TILE)
            high = pl.multiple_of(whole.high + (f * (rows // 2) + r // 2) * cols, TILE)
            pair = block[pl.ds(high, cols), :]
            return block[pl.ds(low, cols), :], pair, *beside_from(block, whole.beside, (f * rows + r) * HALO, rest)

        def halo_row(f, j):
            sent = frames - HALO + f
            return *strip_block.read(edge, sent, j, rest), *strip_block.read_beside(edge, sent, j, rest)

        def own_half(f, r, j):
            low, pair, *tile = own_row(f, r)
            return low, pair[:, (j % 2) * rest : (j % 2 + 1) * rest], *tile

        @if_earlier
        def build():
            every, beside = slice(0, cols), slice(cols, width)
            found = []
            for f in range(HALO):
                for j in range(HALO):
                    mine = own_half(f, (1 - top) * (rows - HALO) + j, j)
                    found += [(f, HALO * top + j, mine), (f, HALO * (1 - top) + j, halo_row(f, j))]
            for f, row, cells in found:
                fill(*near, f, row, every, *cells[:2])
                fill(*near, f, row, beside, *cells[2:])

        sums = [[edge_sums[group, t, r] for r in range(HALO)] for t in range(frames)]
        found = []
        for t in range(frames):
            taps = earlier_taps(t)
            products = convolve(taps, [plane, middle], columns(taps, *near, 0, HALO)) if taps else None
            for r in range(HALO):
                y = sums[t][r]
                if taps:
                    y = y + join(products, r * width, width)
                h = hidden_row(y, gain, cols)
                if strips != 2 and r == 1 - top:
                    h = h * jnp.where(strip == (0 if top else strips - 1), 0.0, 1.0)
                found.append((t, (1 - top) * rows + r, h.astype(jnp.bfloat16)))
        for t, row, h in found:
            fill(h_lo, h_pairs, h_stacked, t, row, slice(0, width), h[:, :LANES], h[:, LANES:])

    partial_sums(frames, (h_lo, h_pairs, h_stacked), [w2_first, w2_middle], rows, cols, partial)


def second_kernel(frames, rows, cols, h_lo, h_pairs, h_stacked, *refs):
    *w2, out = refs
    width = cols + TILE
    for t in range(frames):
        taps = [(f, f - t + 2) for f in range(max(0, t - 2), t + 1)]
        products = convolve(taps, w2, columns(taps, h_lo, h_pairs, h_stacked, 0, rows))
        for r in range(rows):
            out[t, r] = join(products, r * width, width)[:cols]


def finish_kernel(partial, own, gains, out_far, out, left):
    frames, rows, cols, channels = out.shape
    rest = channels - LANES
    gain = gains[...]

    sums = []
    for t in range(frames):
        y = own[t]
        if t < HALO:
            halves = [partial[t, rows + r // 2, :, (r % 2) * rest : (r % 2 + 1) * rest] for r in range(rows)]
            sent = [jnp.concatenate([partial[t, r], halves[r]], axis=-1) for r in range(rows)]
            y = y + jnp.stack(sent).astype(jnp.float32)
        sums.append(y.reshape(rows * cols, channels))
    copies = [pltpu.make_async_copy(out.at[t], out_far.at[t], left.at[t]) for t in range(frames)]
    for t in range(frames):
        result = activate(sums[t], gain).astype(jnp.bfloat16)
        out[t] = result.reshape(rows, cols, channels)
        copies[t].start()
    for copy in copies:
        copy.wait()


def call(kernel, name, ins, outs, scratch=(), semaphores=0, flops=0, far=(), far_out=False, alias=None):
    near, away = pl.BlockSpec(memory_space=pltpu.VMEM), pl.BlockSpec(memory_space=pltpu.HBM)
    in_specs, ins = [near] * len(ins), list(ins)
    for place in far:
        ins[place] = pltpu.with_memory_space_constraint(ins[place], pltpu.HBM)
        in_specs[place] = away
    one = not isinstance(outs, list)
    return pl.pallas_call(
        kernel,
        out_shape=outs,
        in_specs=in_specs,
        out_specs=(away if far_out else near) if one else [near] * len(outs),
        scratch_shapes=[pltpu.VMEM(shape, jnp.bfloat16) for shape in scratch]
        + [pltpu.SemaphoreType.DMA((semaphores,))] * (semaphores > 0),
        input_output_aliases=alias or {},
        compiler_params=pltpu.CompilerParams(vmem_limit_bytes=24 * 1024 * 1024),
        cost_estimate=pl.CostEstimate(flops=flops, bytes_accessed=4 * 1024 * 1024, transcendentals=0),
        name=name,
    )(*ins)


def block_scratch(frames, rows, width):
    return [(frames, rows, width, LANES), (frames, rows + 1, width, LANES), (frames - 1, rows, width, LANES)]


def shards(frames_in, weight_first, scale_first, weight_second, scale_second):
    frames, rows, cols, channels = frames_in.shape
    strips = lax.axis_size("strip")
    width = cols + TILE
    flops = frames * rows * cols * 27 * channels * channels
    bf16 = functools.partial(jax.ShapeDtypeStruct, dtype=jnp.bfloat16)
    f32 = functools.partial(jax.ShapeDtypeStruct, dtype=jnp.float32)

    plane_shape = bf16(weight_first.shape[1:])
    neighbour = swap(frames_in, "slab")
    own_in, middle, last = call(
        stage_kernel,
        "stage",
        [frames_in, weight_first],
        [bf16(frames_in.shape), plane_shape, plane_shape],
        semaphores=3,
        far=[0, 1],
    )
    edge_shape = bf16(Packed(frames, HALO, cols).shape)
    block, *edges = call(
        functools.partial(pack_kernel, strips),
        "pack",
        [own_in, neighbour],
        [bf16(Packed(HALO, rows, cols).shape)] + [edge_shape] * (1 if strips == 2 else 2),
    )
    ups = [(i, i + 1) for i in range(strips - 1)]
    downs = [(i + 1, i) for i in range(strips - 1)]
    ways = [[(0, 1), (1, 0)]] if strips == 2 else [ups, downs]
    before = forward(block)
    own_edges = [lax.ppermute(edge, "strip", way) for edge, way in zip(edges, ways)]
    before_edges = [forward(edge, way) for edge, way in zip(edges, ways)]
    edge_sums, plane = call(
        functools.partial(edge_own_kernel, strips),
        "edge_rows_own",
        [own_in, neighbour, *own_edges, middle, last, weight_first],
        [f32((len(ways), frames, HALO, width, channels)), plane_shape],
        block_scratch(frames + min(frames, 3) - 1, 2 * HALO, width),
        semaphores=1,
        flops=flops // 4,
        far=[-1],
    )
    gain_first = scale_first[None]
    h_shapes = [bf16(shape) for shape in block_scratch(frames, rows + 2, width)]
    partial_shape = bf16((HALO, rows + rows // 2, cols, LANES))
    *safe, w2_first, w2_middle, w2_last = call(
        functools.partial(safe_kernel, strips),
        "safe_rows",
        [own_in, neighbour, before, plane, middle, last, gain_first, weight_second],
        h_shapes + [plane_shape] * 3,
        block_scratch(HALO + frames, rows + 2 * HALO, width),
        semaphores=3,
        flops=flops,
        far=[-1],
    )
    h_lo, h_pairs, h_stacked, partial = call(
        functools.partial(edge_kernel, strips, rows, cols),
        "edge_rows",
        [*before_edges, before, edge_sums, *safe, plane, middle, gain_first, w2_first, w2_middle],
        h_shapes + [partial_shape],
        block_scratch(HALO, 2 * HALO, width),
        flops=flops,
        alias={len(before_edges) + 2 + k: k for k in range(3)},
    )
    sent = forward(partial)
    own = call(
        functools.partial(second_kernel, frames, rows, cols),
        "second_layer",
        [h_lo, h_pairs, h_stacked, w2_first, w2_middle, w2_last],
        f32((frames, rows, cols, channels)),
        flops=flops,
    )
    out = bf16(frames_in.shape)
    return call(
        finish_kernel,
        "finish",
        [sent, own, scale_second[None]],
        out,
        [out.shape],
        semaphores=frames,
        far_out=True,
    )


def solution(mesh):
    return jax.shard_map(
        shards,
        mesh=mesh,
        in_specs=(P(("groups", "frame"), "strip", "slab", None), P(), P(), P(), P()),
        out_specs=P(("groups", "frame"), "strip", "slab", None),
        check_vma=False,
    )
```
